256 devices in a mesh: seq: 64 (over y, x_hi, z), head: 4 (over x_lo, core).
Axes of the slice: x: 4 (x_hi: 2, x_lo: 2; x = x_hi * 2 + x_lo), y: 4, z: 8, core: 2. Of those that a mesh axis runs over, the one named last changes fastest.
Arguments:
- queries: bfloat16 [65536, 2048], P('seq', 'head'), may hold values from -11 to 11
- keys_values: bfloat16 [65536, 2, 2048], P('seq', None, 'head'), may hold values from -6 to 6
- rand_blocks: int32 [1024, 2], P('seq'), may hold values from 0 to 1023, as said below
- w_out: bfloat16 [2048, 4096], P('head'), may hold values from -1 to 1
Outputs:
- mixed: bfloat16 [65536, 4096], P(('seq', 'head'))
The draws below stay inside these ranges and needn't reach their ends.
Inputs may be any that keep to these rules, and one draw needn't show every extreme that they name: `rand_blocks`: of the 32 entries in the rows of one index of seq, at most 1 name blocks o * 16 to o * 16 + 15 of any one index o; in every draw the blocks of some index o are named exactly 1 times from the rows of every index.
All inputs are finite; a program needn't handle non-finite values.
Results may differ from the reference program's by a relative error of at most 0.013.
Values may be sent and summed in bfloat16 or wider, within the bound.
No kernel may reach another device: no remote copies, remote signals or barrier semaphores. Data moves between devices by JAX's collectives and lax.ppermute only.
A program may use at most 128 MiB of HBM per device.

```python
import jax
import jax.numpy as jnp
from jax import lax

D = 4096
HEADS = 16
HEAD_DIM = 128
BLOCK = 64
RAND = 2
BPD = 16
NB = 1024
TOKENS = 65536
GROUPS = 4
FEAT = 2048
FEAT_GROUP = 512
N_SEQ = 64


def attention_inputs(key):
    base = jax.random.fold_in(key, 17)
    part_q, part_k, part_v = jax.random.split(base, 3)
    feat = HEADS * HEAD_DIM
    queries = jnp.clip(jax.random.normal(part_q, (TOKENS, feat), jnp.float32), -6.0, 6.0)
    keys = jnp.clip(jax.random.normal(part_k, (TOKENS, feat), jnp.float32), -6.0, 6.0)
    values = jnp.clip(jax.random.normal(part_v, (TOKENS, feat), jnp.float32), -6.0, 6.0)
    return (queries, jnp.stack([keys, values], axis=1))


def draw_queries(key, part):
    queries, paired = attention_inputs(key)
    return queries.astype(jnp.bfloat16)


def draw_keys_values(key, part):
    queries, paired = attention_inputs(key)
    return paired.astype(jnp.bfloat16)


def draw_rand_blocks(key, part):
    entries = RAND * BPD
    devices = N_SEQ
    star = jax.random.randint(jax.random.fold_in(key, 1), (), 0, devices)
    device_keys = jax.random.split(jax.random.fold_in(key, 2), devices)

    def one_device(sub):
        key_a, key_b, key_c = jax.random.split(sub, 3)
        others = (star + 1 + jax.random.permutation(key_a, devices - 1)) % devices
        order = jnp.concatenate([star[None], others])
        owners = order[jnp.arange(entries) % devices]
        owners = owners[jax.random.permutation(key_b, entries)]
        offsets = jax.random.randint(key_c, (entries,), 0, BPD)
        return (owners * BPD + offsets).astype(jnp.int32)
    blocks = jax.vmap(one_device)(device_keys)
    return blocks.reshape(NB, RAND)


def block_levels(own_key, extent, shards, smallest, top_value):
    loudness = 1.0
    for position, shards_of in shards:
        heights = jax.random.uniform(jax.random.fold_in(jax.random.fold_in(own_key, 6), position), (shards_of,), jnp.float32, smallest / len(shards), top_value / len(shards))
        loudness = loudness * jnp.repeat(jnp.exp(heights), extent[position] // shards_of).reshape((-1,) + (1,) * (len(extent) - 1 - position))
    return loudness


def normal_values(rng, extent, scale, bound, cuts=(), kind=jnp.bfloat16):
    result = jax.random.normal(rng, extent, jnp.float32) * scale
    if len(cuts) > 0:
        result = block_levels(rng, extent, cuts, -0.22, 0.18) * result
    return jnp.clip(result, min=-bound, max=bound).astype(kind)


def setup_inputs(seed: int = 0) -> dict:
    arg_keys = jax.random.split(jax.random.key(seed), 5)
    return {
        "queries": draw_queries(jax.random.fold_in(arg_keys[4], 71), 0),
        "keys_values": draw_keys_values(jax.random.fold_in(arg_keys[4], 71), 0),
        "rand_blocks": draw_rand_blocks(jax.random.fold_in(arg_keys[4], 71), 0),
        "w_out": normal_values(arg_keys[3], (FEAT, D), (FEAT // 64) ** -0.5, 1.0, ((0, 4),)),
    }


def reference(queries, keys_values, rand_blocks, w_out):
    scale = HEAD_DIM ** -0.5
    query_groups = queries.reshape(N_SEQ, BPD, BLOCK, HEADS, HEAD_DIM)
    block_kv = keys_values.reshape(NB, BLOCK, 2, HEADS, HEAD_DIM)
    rand_groups = rand_blocks.reshape(N_SEQ, BPD, RAND)
    block_ids = jnp.arange(NB, dtype=jnp.int32).reshape(N_SEQ, BPD)

    def one_group(item):
        query_part, rand_part, ids = item
        zeros_ids = jnp.zeros_like(ids)
        last_ids = zeros_ids + (NB - 1)
        taken = [ids - 1, ids, ids + 1, zeros_ids, last_ids]
        valid = [ids >= 1, ids >= 0, ids <= NB - 2, ids >= 2, ids <= NB - 3]
        for column in range(RAND):
            chosen = rand_part[:, column]
            clash = chosen == taken[0]
            for other in taken[1:]:
                clash = jnp.logical_or(clash, chosen == other)
            valid.append(jnp.logical_not(clash))
            taken.append(chosen)
        index = jnp.clip(jnp.stack(taken, axis=1), 0, NB - 1).astype(jnp.int32)
        mask = jnp.repeat(jnp.stack(valid, axis=1), BLOCK, axis=1)[:, None, None, :]
        picked = block_kv[index]
        count = index.shape[1] * BLOCK
        keys = picked[:, :, :, 0].reshape(BPD, count, HEADS, HEAD_DIM).astype(jnp.float32)
        values = picked[:, :, :, 1].reshape(BPD, count, HEADS, HEAD_DIM).astype(jnp.float32)
        scores = jnp.einsum("jqhd,jkhd->jhqk", query_part.astype(jnp.float32), keys) * scale
        scores = jnp.where(mask, scores, -1e30)
        peak = jnp.max(scores, axis=-1, keepdims=True)
        raw = jnp.where(mask, jnp.exp(scores - peak), 0.0)
        total = jnp.sum(raw, axis=-1)
        weights = raw.astype(jnp.bfloat16).astype(jnp.float32)
        mixture = jnp.einsum("jhqk,jkhd->jqhd", weights, values)
        attended = (mixture / jnp.transpose(total, (0, 2, 1))[..., None]).astype(jnp.bfloat16)
        attended = attended.reshape(BPD * BLOCK, FEAT)
        partials = []
        for group in range(GROUPS):
            lower = group * FEAT_GROUP
            term = jnp.dot(attended[:, lower:lower + FEAT_GROUP], w_out[lower:lower + FEAT_GROUP], preferred_element_type=jnp.float32)
            partials.append(term.astype(jnp.bfloat16))
        stacked = lax.optimization_barrier(jnp.stack(partials))
        return jnp.sum(stacked.astype(jnp.float32), axis=0).astype(jnp.bfloat16)

    mixed = lax.map(one_group, (query_groups, rand_groups, block_ids))
    return mixed.reshape(TOKENS, D)
```

```python
from functools import reduce

import jax
import jax.numpy as jnp
from jax import lax
from jax.experimental import pallas as pl
from jax.experimental.pallas import tpu as pltpu
from jax.sharding import Mesh, PartitionSpec as P

HEAD_DIM = 128
BLOCK = 64
NEG = -1e30
SEQ = ("y", "xh", "z")
LANE = ("y", "xh")
HEAD = ("xl", "core")
XRING = ("xh", "xl")
NY, NXH, NZ, NXL, NC = 4, 2, 8, 2, 2
LANES = NY * NXH
SCALE = HEAD_DIM ** (-0.5)
F32 = jnp.float32
BF16 = jnp.bfloat16
VMEM_LIMIT = 48 * 1024 * 1024


def dot_nt(a, b):
    return lax.dot_general(a, b, (((1,), (1,)), ((), ())), preferred_element_type=F32)


def local_kernel(all_blocks, id_ref, q_ref, kv_ref, ends_ref, o_ref, st_ref):
    feat = q_ref.shape[1]
    heads = feat // HEAD_DIM
    blocks = q_ref.shape[0] // BLOCK
    col = lax.broadcasted_iota(jnp.int32, (BLOCK, 3 * BLOCK), 1)
    shift = jnp.where(col < BLOCK, -1, jnp.where(col < 2 * BLOCK, 0, 1))
    end_col = lax.broadcasted_iota(jnp.int32, (BLOCK, 2 * BLOCK), 1)

    def step(j, carry):
        block = id_ref[0] + j
        near = block + shift
        near_ok = jnp.logical_and(near >= 0, near < all_blocks)
        ends_ok = jnp.where(end_col < BLOCK, block, all_blocks - 1 - block) >= 2
        rows = pl.ds(pl.multiple_of(j * BLOCK, BLOCK), BLOCK)
        wrows = pl.ds(pl.multiple_of(j * BLOCK, BLOCK), 3 * BLOCK)
        for h in range(heads):
            kcol = pl.ds(h * HEAD_DIM, HEAD_DIM)
            vcol = pl.ds(feat + h * HEAD_DIM, HEAD_DIM)
            q = q_ref[rows, kcol]
            sw = jnp.where(near_ok, dot_nt(q, kv_ref[wrows, kcol]) * SCALE, NEG)
            se = jnp.where(ends_ok, dot_nt(q, ends_ref[:, kcol]) * SCALE, NEG)
            peak = jnp.maximum(
                jnp.max(sw, axis=1, keepdims=True), jnp.max(se, axis=1, keepdims=True)
            )
            pw = jnp.exp(sw - peak)
            pe = jnp.exp(se - peak)
            total = jnp.sum(pw, axis=1, keepdims=True) + jnp.sum(pe, axis=1, keepdims=True)
            out = jnp.dot(pw.astype(BF16), kv_ref[wrows, vcol], preferred_element_type=F32)
            out += jnp.dot(pe.astype(BF16), ends_ref[:, vcol], preferred_element_type=F32)
            o_ref[rows, kcol] = out
            st_ref[rows, pl.ds(h, 1)] = peak
            st_ref[rows, pl.ds(heads + h, 1)] = total
        return carry

    lax.fori_loop(0, blocks, step, 0)


def add_slots(where_ref, base, slots_ref, q_ref, o_ref, st_ref):
    feat = q_ref.shape[1]
    heads = feat // HEAD_DIM

    def step(s, carry):
        j = where_ref[base + s]

        @pl.when(j >= 0)
        def _():
            rows = pl.ds(pl.multiple_of(j * BLOCK, BLOCK), BLOCK)
            for h in range(heads):
                kcol = pl.ds(h * HEAD_DIM, HEAD_DIM)
                vcol = pl.ds(feat + h * HEAD_DIM, HEAD_DIM)
                sc = dot_nt(q_ref[rows, kcol], slots_ref[s, :, kcol]) * SCALE
                old = st_ref[rows, pl.ds(h, 1)]
                peak = jnp.maximum(old, jnp.max(sc, axis=1, keepdims=True))
                fade = jnp.exp(old - peak)
                p = jnp.exp(sc - peak)
                total = st_ref[rows, pl.ds(heads + h, 1)] * fade + jnp.sum(p, axis=1, keepdims=True)
                out = jnp.dot(p.astype(BF16), slots_ref[s, :, vcol], preferred_element_type=F32)
                o_ref[rows, kcol] = o_ref[rows, kcol] * fade + out
                st_ref[rows, pl.ds(h, 1)] = peak
                st_ref[rows, pl.ds(heads + h, 1)] = total

        return carry

    lax.fori_loop(0, slots_ref.shape[0], step, 0)


def more_kernel(count, where_ref, q_ref, oin_ref, stin_ref, *refs):
    slots, (o_ref, st_ref) = refs[:count], refs[count:]
    o_ref[...] = oin_ref[...]
    st_ref[...] = stin_ref[...]
    base = 0
    for ref in slots:
        add_slots(where_ref, base, ref, q_ref, o_ref, st_ref)
        base += ref.shape[0]


def final_kernel(count, where_ref, q_ref, oin_ref, stin_ref, *refs):
    slots, (att_ref, o_ref, st_ref) = refs[:count], refs[count:]
    o_ref[...] = oin_ref[...]
    st_ref[...] = stin_ref[...]
    base = 0
    for ref in slots:
        add_slots(where_ref, base, ref, q_ref, o_ref, st_ref)
        base += ref.shape[0]
    heads = q_ref.shape[1] // HEAD_DIM

    def step(j, carry):
        rows = pl.ds(pl.multiple_of(j * BLOCK, BLOCK), BLOCK)
        for h in range(heads):
            kcol = pl.ds(h * HEAD_DIM, HEAD_DIM)
            att_ref[rows, kcol] = (
                o_ref[rows, kcol] / st_ref[rows, pl.ds(heads + h, 1)]
            ).astype(BF16)
        return carry

    lax.fori_loop(0, q_ref.shape[0] // BLOCK, step, 0)


VM = pl.BlockSpec(memory_space=pltpu.VMEM)
SM = pl.BlockSpec(memory_space=pltpu.SMEM)


def local_part(first_id, all_blocks, q, kv_pad, ends):
    tok, feat = q.shape
    return pl.pallas_call(
        lambda *refs: local_kernel(all_blocks, *refs),
        out_shape=(
            jax.ShapeDtypeStruct((tok, feat), F32),
            jax.ShapeDtypeStruct((tok, 128), F32),
        ),
        in_specs=[SM, VM, VM, VM],
        out_specs=(VM, VM),
        compiler_params=pltpu.CompilerParams(vmem_limit_bytes=VMEM_LIMIT),
        cost_estimate=pl.CostEstimate(
            flops=4 * tok * feat * 5 * BLOCK, bytes_accessed=8 * 2**20, transcendentals=0
        ),
        name="local_part",
    )(first_id, q, kv_pad, ends)


def more_part(where, q, o, st, slots):
    tok, feat = q.shape
    return pl.pallas_call(
        lambda *refs: more_kernel(len(slots), *refs),
        out_shape=(
            jax.ShapeDtypeStruct((tok, feat), F32),
            jax.ShapeDtypeStruct((tok, 128), F32),
        ),
        in_specs=[SM] + [VM] * (3 + len(slots)),
        out_specs=(VM, VM),
        compiler_params=pltpu.CompilerParams(vmem_limit_bytes=VMEM_LIMIT),
        cost_estimate=pl.CostEstimate(
            flops=2 * tok * feat * BLOCK, bytes_accessed=8 * 2**20, transcendentals=0
        ),
        name="more_part",
    )(where, q, o, st, *slots)


def final_part(where, q, o, st, slots):
    tok, feat = q.shape
    return pl.pallas_call(
        lambda *refs: final_kernel(len(slots), *refs),
        out_shape=jax.ShapeDtypeStruct((tok, feat), BF16),
        in_specs=[SM] + [VM] * (3 + len(slots)),
        out_specs=VM,
        scratch_shapes=[pltpu.VMEM((tok, feat), F32), pltpu.VMEM((tok, 128), F32)],
        compiler_params=pltpu.CompilerParams(vmem_limit_bytes=VMEM_LIMIT),
        name="final_part",
    )(where, q, o, st, *slots)


def project_kernel(me_ref, a_ref, own_ref, core_ref, lo_ref, hi_ref, clo_ref, chi_ref, out_ref):
    me = me_ref[0]
    half = lo_ref.shape[0]

    def mul(a, w_ref):
        return jnp.dot(a, w_ref[...], preferred_element_type=F32)

    acc = mul(a_ref[me], own_ref)
    acc += mul(a_ref[me ^ 1], core_ref)
    acc += mul(a_ref[me ^ 2, :, :half], lo_ref)
    acc += mul(a_ref[me ^ 2, :, half:], hi_ref)
    acc += mul(a_ref[me ^ 3, :, :half], clo_ref)
    acc += mul(a_ref[me ^ 3, :, half:], chi_ref)
    out_ref[...] = acc.astype(BF16)


def project(me, a, weights, tile=512):
    _, rows, feat = a.shape
    cols = weights[0].shape[1]
    return pl.pallas_call(
        project_kernel,
        out_shape=jax.ShapeDtypeStruct((rows, cols), BF16),
        grid_spec=pltpu.PrefetchScalarGridSpec(
            num_scalar_prefetch=1,
            grid=(cols // tile,),
            in_specs=[pl.BlockSpec(a.shape, lambda n, me: (0, 0, 0))]
            + [pl.BlockSpec((w.shape[0], tile), lambda n, me: (0, n)) for w in weights],
            out_specs=pl.BlockSpec((rows, tile), lambda n, me: (0, n)),
        ),
        compiler_params=pltpu.CompilerParams(vmem_limit_bytes=VMEM_LIMIT),
        name="project",
    )(me, a, *weights)


def z_shift(x, by):
    return lax.ppermute(x, "z", [(i, (i + by) % NZ) for i in range(NZ)])


def lane_exchange(x):
    return lax.all_to_all(x, LANE, split_axis=0, concat_axis=0, tiled=True)


def wanted_blocks(rand_blocks, block_ids, all_blocks, blocks_dev):
    taken = [
        block_ids - 1,
        block_ids,
        block_ids + 1,
        jnp.zeros_like(block_ids),
        jnp.zeros_like(block_ids) + (all_blocks - 1),
    ]
    fresh = []
    for column in range(rand_blocks.shape[1]):
        chosen = rand_blocks[:, column]
        clash = reduce(jnp.logical_or, [chosen == other for other in taken])
        fresh.append(jnp.logical_not(clash))
        taken.append(chosen)
    fresh = jnp.stack(fresh, axis=1).reshape(-1)
    flat = rand_blocks.reshape(-1)
    entries = flat.shape[0]
    query = jnp.arange(entries, dtype=jnp.int32) // rand_blocks.shape[1]
    owners = jnp.arange(all_blocks // blocks_dev, dtype=jnp.int32)
    named = (flat // blocks_dev)[:, None] == owners[None, :]
    offset = jnp.sum(jnp.where(named, (flat % blocks_dev)[:, None], 0), axis=0)
    used = jnp.logical_and(named, fresh[:, None])
    where = jnp.sum(jnp.where(used, query[:, None] + 1, 0), axis=0) - 1
    return offset.astype(jnp.int32), where.astype(jnp.int32)


def body(queries, keys_values, rand_blocks, w_out):
    tok, feat = queries.shape
    blocks_dev = tok // BLOCK
    all_blocks = blocks_dev * LANES * NZ
    z = lax.axis_index("z")
    seq = lax.axis_index(SEQ)
    me = lax.axis_index(HEAD)
    first_id = seq * blocks_dev

    kv = keys_values.reshape(blocks_dev, BLOCK, 2 * feat)

    block_ids = first_id + jnp.arange(blocks_dev, dtype=jnp.int32)
    offset, where = wanted_blocks(rand_blocks, block_ids, all_blocks, blocks_dev)
    asked = jnp.broadcast_to(offset.reshape(LANES, 1, NZ), (LANES, NZ, NZ)).reshape(-1, NZ)
    asked = lax.all_to_all(asked, SEQ, split_axis=0, concat_axis=0, tiled=True)
    asked = asked.reshape(LANES, NZ, NZ)

    def asks(plane, owner):
        part = lax.dynamic_index_in_dim(asked, plane % NZ, axis=1, keepdims=False)
        return lax.dynamic_index_in_dim(part, owner % NZ, axis=1, keepdims=False)

    def for_query(owner):
        return lax.dynamic_index_in_dim(
            where.reshape(LANES, NZ), owner % NZ, axis=1, keepdims=False
        )

    up1, down1 = z_shift(kv, 1), z_shift(kv, -1)
    edge = jnp.where(z == 0, kv[0], kv[blocks_dev - 1])
    turns = [(NZ * i + NZ - 1, NZ * i + NZ) for i in range(LANES - 1)]
    crossed = lax.ppermute(edge, SEQ, turns + [(b, a) for a, b in turns])
    up2, down2 = z_shift(up1, 1), z_shift(down1, -1)
    half = LANES // 2
    up4 = z_shift(up2[asks(z + 2, z - 2)[:half]], 1)
    down4 = z_shift(down2[asks(z - 2, z + 2)[half:]], -1)
    up3 = z_shift(up2[asks(z + 1, z - 2)], 1)
    down3 = z_shift(down2[asks(z - 1, z + 2)], -1)
    far = jnp.concatenate([z_shift(up4, 1), z_shift(down4, -1)], axis=0)

    r0 = lane_exchange(kv[asks(z, z)])
    r1u = lane_exchange(up1[asks(z, z - 1)])
    r1d = lane_exchange(down1[asks(z, z + 1)])
    r2u = lane_exchange(up2[asks(z, z - 2)])
    r2d = lane_exchange(down2[asks(z, z + 2)])
    r3u = lane_exchange(up3)
    r3d = lane_exchange(down3)
    r4 = lane_exchange(far)

    plane_ends = lane_exchange(jnp.broadcast_to(edge[None], (LANES,) + edge.shape))
    held = jnp.where(z == 0, plane_ends[0], plane_ends[LANES - 1])
    got = lax.ppermute(held, "z", [(0, 4), (7, 3)])
    held = jnp.where(jnp.logical_or(z == 4, z == 3), got, held)
    got = lax.ppermute(held, "z", [(0, 2), (4, 6), (7, 5), (3, 1)])
    fresh = reduce(jnp.logical_or, [z == 2, z == 6, z == 5, z == 1])
    held = jnp.where(fresh, got, held)
    got = lax.ppermute(held, "z", [(i, i ^ 1) for i in range(NZ)])
    even = z % 2 == 0
    ends = jnp.concatenate([jnp.where(even, held, got), jnp.where(even, got, held)], axis=0)

    rows = w_out.shape[0] // 2
    ring = NXH * NXL
    lo = lax.ppermute(w_out[:rows], XRING, [(i, (i + 1) % ring) for i in range(ring)])
    hi = lax.ppermute(w_out[rows:], XRING, [(i, (i - 1) % ring) for i in range(ring)])
    swap = [(0, 1), (1, 0)]
    weights = [w_out, lax.ppermute(w_out, "core", swap), lo, hi]
    weights += [lax.ppermute(lo, "core", swap), lax.ppermute(hi, "core", swap)]

    before = jnp.where(z == 0, crossed, up1[blocks_dev - 1])
    after = jnp.where(z == NZ - 1, crossed, down1[0])
    kv_pad = jnp.concatenate([before, kv.reshape(tok, 2 * feat), after], axis=0)
    o, st = local_part(first_id.reshape(1), all_blocks, queries, kv_pad, ends)
    at = [for_query(z), for_query(z - 1), for_query(z + 1)]
    o, st = more_part(jnp.concatenate(at), queries, o, st, [r0, r1u, r1d])
    at = [for_query(z - 2), for_query(z + 2)]
    o, st = more_part(jnp.concatenate(at), queries, o, st, [r2u, r2d])
    at = [for_query(z - 3), for_query(z + 3)]
    o, st = more_part(jnp.concatenate(at), queries, o, st, [r3u, r3d])
    attended = final_part(for_query(z + 4), queries, o, st, [r4])

    heads = NXL * NC
    a = lax.all_to_all(
        attended.reshape(heads, tok // heads, feat), HEAD, split_axis=0, concat_axis=0, tiled=True
    )
    return project(me.reshape(1), a, weights)


def solution(mesh):
    fine = Mesh(mesh.devices.reshape(NY, NXH, NZ, NXL, NC), ("y", "xh", "z", "xl", "core"))
    in_specs = (P(SEQ, HEAD), P(SEQ, None, HEAD), P(SEQ, None), P(HEAD, None))
    out_specs = P(SEQ + HEAD, None)
    return jax.shard_map(body, mesh=fine, in_specs=in_specs, out_specs=out_specs, check_vma=False)
```

```python
from functools import reduce

import jax
import jax.numpy as jnp
from jax import lax
from jax.experimental import pallas as pl
from jax.experimental.pallas import tpu as pltpu
from jax.sharding import Mesh, PartitionSpec as P

HEAD_DIM = 128
BLOCK = 64
NEG = -1e30
SEQ = ("y", "xh", "z")
LANE = ("y", "xh")
HEAD = ("xl", "core")
XRING = ("xh", "xl")
NY, NXH, NZ, NXL, NC = 4, 2, 8, 2, 2
LANES = NY * NXH
SCALE = HEAD_DIM ** (-0.5)
F32 = jnp.float32
BF16 = jnp.bfloat16
VMEM_LIMIT = 24 * 1024 * 1024
VM = pl.BlockSpec(memory_space=pltpu.VMEM)
SM = pl.BlockSpec(memory_space=pltpu.SMEM)
HB = pl.BlockSpec(memory_space=pltpu.HBM)


def dot_nt(a, b):
    return lax.dot_general(a, b, (((1,), (1,)), ((), ())), preferred_element_type=F32)


def dot_nn(a, b):
    return jnp.dot(a, b, preferred_element_type=F32)


def row_max(a):
    return jnp.max(a, axis=1, keepdims=True)


def row_sum(a):
    return jnp.sum(a, axis=1, keepdims=True)


def local_kernel(all_blocks, deltas, z_ref, where_ref, id_ref, *refs):
    q_ref, kv_ref, ends_ref, slots_ref, o_ref, st_ref = refs
    feat = q_ref.shape[1]
    heads = range(feat // HEAD_DIM)
    blocks = q_ref.shape[0] // BLOCK
    col = lax.broadcasted_iota(jnp.int32, (BLOCK, 3 * BLOCK), 1)
    shift = jnp.where(col < BLOCK, -1, jnp.where(col < 2 * BLOCK, 0, 1))
    end_col = lax.broadcasted_iota(jnp.int32, (BLOCK, 2 * BLOCK), 1)
    kcol = [pl.ds(h * HEAD_DIM, HEAD_DIM) for h in heads]
    vcol = [pl.ds(feat + h * HEAD_DIM, HEAD_DIM) for h in heads]

    def step(j, carry):
        block = id_ref[0] + j
        near = block + shift
        near_ok = jnp.logical_and(near >= 0, near < all_blocks)
        ends_ok = jnp.where(end_col < BLOCK, block, all_blocks - 1 - block) >= 2
        rows = pl.ds(pl.multiple_of(j * BLOCK, BLOCK), BLOCK)
        wrows = pl.ds(pl.multiple_of(j * BLOCK, BLOCK), 3 * BLOCK)
        q = [q_ref[rows, kcol[h]] for h in heads]
        sw = [dot_nt(q[h], kv_ref[wrows, kcol[h]]) for h in heads]
        se = [dot_nt(q[h], ends_ref[:, kcol[h]]) for h in heads]
        sw = [jnp.where(near_ok, x * SCALE, NEG) for x in sw]
        se = [jnp.where(ends_ok, x * SCALE, NEG) for x in se]
        peak = [jnp.maximum(row_max(sw[h]), row_max(se[h])) for h in heads]
        pw = [jnp.exp(sw[h] - peak[h]) for h in heads]
        pe = [jnp.exp(se[h] - peak[h]) for h in heads]
        total = [row_sum(pw[h]) + row_sum(pe[h]) for h in heads]
        out = [
            dot_nn(pw[h].astype(BF16), kv_ref[wrows, vcol[h]])
            + dot_nn(pe[h].astype(BF16), ends_ref[:, vcol[h]])
            for h in heads
        ]
        for h in heads:
            o_ref[rows, kcol[h]] = out[h]
            st_ref[rows, pl.ds(h, 1)] = peak[h]
            st_ref[rows, pl.ds(len(heads) + h, 1)] = total[h]
        return carry

    lax.fori_loop(0, blocks, step, 0)
    add_slots(deltas, z_ref, where_ref, slots_ref, q_ref, o_ref, st_ref)


def add_slots(deltas, z_ref, where_ref, slots_ref, q_ref, o_ref, st_ref):
    feat = q_ref.shape[1]
    heads = range(feat // HEAD_DIM)
    kcol = [pl.ds(h * HEAD_DIM, HEAD_DIM) for h in heads]
    vcol = [pl.ds(feat + h * HEAD_DIM, HEAD_DIM) for h in heads]

    def step(lane, carry):
        for s, delta in enumerate(deltas):
            j = where_ref[lane * NZ + lax.rem(z_ref[0] + (delta + NZ), NZ)]

            @pl.when(j >= 0)
            def _():
                rows = pl.ds(pl.multiple_of(j * BLOCK, BLOCK), BLOCK)
                sc = [
                    dot_nt(q_ref[rows, kcol[h]], slots_ref[lane, s, :, kcol[h]]) * SCALE
                    for h in heads
                ]
                old = [st_ref[rows, pl.ds(h, 1)] for h in heads]
                tot = [st_ref[rows, pl.ds(len(heads) + h, 1)] for h in heads]
                acc = [o_ref[rows, kcol[h]] for h in heads]
                peak = [jnp.maximum(old[h], row_max(sc[h])) for h in heads]
                fade = [jnp.exp(old[h] - peak[h]) for h in heads]
                p = [jnp.exp(sc[h] - peak[h]) for h in heads]
                tot = [tot[h] * fade[h] + row_sum(p[h]) for h in heads]
                out = [dot_nn(p[h].astype(BF16), slots_ref[lane, s, :, vcol[h]]) for h in heads]
                for h in heads:
                    o_ref[rows, kcol[h]] = acc[h] * fade[h] + out[h]
                    st_ref[rows, pl.ds(h, 1)] = peak[h]
                    st_ref[rows, pl.ds(len(heads) + h, 1)] = tot[h]

        return carry

    lax.fori_loop(0, LANES, step, 0)


def more_kernel(deltas, z_ref, where_ref, q_ref, oin_ref, stin_ref, *refs):
    slots, (o_ref, st_ref) = refs[: len(deltas)], refs[len(deltas) :]
    o_ref[...] = oin_ref[...]
    st_ref[...] = stin_ref[...]
    for which, ref in zip(deltas, slots):
        add_slots(which, z_ref, where_ref, ref, q_ref, o_ref, st_ref)


def final_kernel(deltas, z_ref, where_ref, q_ref, oin_ref, stin_ref, *refs):
    slots, (att_ref, o_ref, st_ref) = refs[: len(deltas)], refs[len(deltas) :]
    more_kernel(deltas, z_ref, where_ref, q_ref, oin_ref, stin_ref, *slots, o_ref, st_ref)
    heads = range(q_ref.shape[1] // HEAD_DIM)

    def step(j, carry):
        rows = pl.ds(pl.multiple_of(j * BLOCK, BLOCK), BLOCK)
        for h in heads:
            kcol = pl.ds(h * HEAD_DIM, HEAD_DIM)
            total = st_ref[rows, pl.ds(len(heads) + h, 1)]
            att_ref[rows, kcol] = (o_ref[rows, kcol] / total).astype(BF16)
        return carry

    lax.fori_loop(0, q_ref.shape[0] // BLOCK, step, 0)


def cost(us):
    return pl.CostEstimate(flops=int(us * 1e9), bytes_accessed=4 * 2**20, transcendentals=0)


def local_part(z, where, first_id, all_blocks, q, kv_pad, ends, deltas, slots):
    tok, feat = q.shape
    return pl.pallas_call(
        lambda *refs: local_kernel(all_blocks, deltas, *refs),
        out_shape=(
            jax.ShapeDtypeStruct((tok, feat), F32),
            jax.ShapeDtypeStruct((tok, 128), F32),
        ),
        in_specs=[SM, SM, SM, VM, VM, VM, VM],
        out_specs=(VM, VM),
        compiler_params=pltpu.CompilerParams(vmem_limit_bytes=VMEM_LIMIT),
        cost_estimate=cost(25),
        name="local_part",
    )(z, where, first_id, q, kv_pad, ends, slots)


def more_part(z, where, q, o, st, deltas, slots):
    tok, feat = q.shape
    return pl.pallas_call(
        lambda *refs: more_kernel(deltas, *refs),
        out_shape=(
            jax.ShapeDtypeStruct((tok, feat), F32),
            jax.ShapeDtypeStruct((tok, 128), F32),
        ),
        in_specs=[SM, SM] + [VM] * (3 + len(slots)),
        out_specs=(VM, VM),
        compiler_params=pltpu.CompilerParams(vmem_limit_bytes=VMEM_LIMIT),
        cost_estimate=cost(12),
        name="more_part",
    )(z, where, q, o, st, *slots)


def final_part(z, where, q, o, st, deltas, slots):
    tok, feat = q.shape
    return pl.pallas_call(
        lambda *refs: final_kernel(deltas, *refs),
        out_shape=jax.ShapeDtypeStruct((tok, feat), BF16),
        in_specs=[SM, SM] + [VM] * (3 + len(slots)),
        out_specs=VM,
        scratch_shapes=[pltpu.VMEM((tok, feat), F32), pltpu.VMEM((tok, 128), F32)],
        compiler_params=pltpu.CompilerParams(vmem_limit_bytes=VMEM_LIMIT),
        cost_estimate=cost(6),
        name="final_part",
    )(z, where, q, o, st, *slots)


def pick(z, asked, sources, plan, shapes):
    def kernel(z_ref, asked_ref, *refs):
        src, out = refs[: len(sources)], refs[len(sources) : -1]
        sems = refs[-1]
        copies = []
        for n, (o, position, s, lane, plane, owner) in enumerate(plan):
            row = lane * NZ + lax.rem(z_ref[0] + (plane + NZ), NZ)
            block = asked_ref[row, lax.rem(z_ref[0] + (owner + NZ), NZ)]
            copies.append(
                pltpu.make_async_copy(src[s].at[block], out[o].at[position], sems.at[n])
            )
            copies[-1].start()
        for copy in copies:
            copy.wait()

    block_shape = sources[0].shape[1:]
    return pl.pallas_call(
        kernel,
        out_shape=tuple(pltpu.HBM(shape + block_shape, BF16) for shape in shapes),
        in_specs=[SM, SM] + [HB] * len(sources),
        out_specs=tuple(HB for _ in shapes),
        scratch_shapes=[pltpu.SemaphoreType.DMA((len(plan),))],
        compiler_params=pltpu.CompilerParams(vmem_limit_bytes=2 * 1024 * 1024),
        cost_estimate=cost(3),
        name="pick",
    )(z, asked, *sources)


def project_kernel(me_ref, a_ref, own_ref, core_ref, lo_ref, hi_ref, clo_ref, chi_ref, out_ref):
    me = me_ref[0]
    half = lo_ref.shape[0]

    def mul(a, w_ref):
        return jnp.dot(a, w_ref[...], preferred_element_type=F32)

    acc = mul(a_ref[me], own_ref)
    acc += mul(a_ref[me ^ 1], core_ref)
    acc += mul(a_ref[me ^ 2, :, :half], lo_ref)
    acc += mul(a_ref[me ^ 2, :, half:], hi_ref)
    acc += mul(a_ref[me ^ 3, :, :half], clo_ref)
    acc += mul(a_ref[me ^ 3, :, half:], chi_ref)
    out_ref[...] = acc.astype(BF16)


def project(me, a, weights, tile=512):
    _, rows, feat = a.shape
    cols = weights[0].shape[1]
    return pl.pallas_call(
        project_kernel,
        out_shape=jax.ShapeDtypeStruct((rows, cols), BF16),
        grid_spec=pltpu.PrefetchScalarGridSpec(
            num_scalar_prefetch=1,
            grid=(cols // tile,),
            in_specs=[pl.BlockSpec(a.shape, lambda n, me: (0, 0, 0))]
            + [pl.BlockSpec((w.shape[0], tile), lambda n, me: (0, n)) for w in weights],
            out_specs=pl.BlockSpec((rows, tile), lambda n, me: (0, n)),
        ),
        compiler_params=pltpu.CompilerParams(vmem_limit_bytes=VMEM_LIMIT),
        name="project",
    )(me, a, *weights)


def z_shift(x, by):
    return lax.ppermute(x, "z", [(i, (i + by) % NZ) for i in range(NZ)])


def lane_exchange(x):
    return lax.all_to_all(x, LANE, split_axis=0, concat_axis=0, tiled=True)


def wanted_blocks(rand_blocks, block_ids, all_blocks, blocks_dev):
    taken = [
        block_ids - 1,
        block_ids,
        block_ids + 1,
        jnp.zeros_like(block_ids),
        jnp.zeros_like(block_ids) + (all_blocks - 1),
    ]
    fresh = []
    for column in range(rand_blocks.shape[1]):
        chosen = rand_blocks[:, column]
        clash = reduce(jnp.logical_or, [chosen == other for other in taken])
        fresh.append(jnp.logical_not(clash))
        taken.append(chosen)
    fresh = jnp.stack(fresh, axis=1).reshape(-1)
    flat = rand_blocks.reshape(-1)
    entries = flat.shape[0]
    query = jnp.arange(entries, dtype=jnp.int32) // rand_blocks.shape[1]
    owners = jnp.arange(all_blocks // blocks_dev, dtype=jnp.int32)
    named = (flat // blocks_dev)[:, None] == owners[None, :]
    offset = jnp.sum(jnp.where(named, (flat % blocks_dev)[:, None], 0), axis=0)
    used = jnp.logical_and(named, fresh[:, None])
    where = jnp.sum(jnp.where(used, query[:, None] + 1, 0), axis=0) - 1
    return offset.astype(jnp.int32), where.astype(jnp.int32)


def tie(*arrays):
    return lax.optimization_barrier(arrays)


def body(queries, keys_values, rand_blocks, w_out):
    tok, feat = queries.shape
    blocks_dev = tok // BLOCK
    all_blocks = blocks_dev * LANES * NZ
    lanes = range(LANES)
    half = LANES // 2
    z = lax.axis_index("z")
    zs = z.reshape(1)
    first_id = lax.axis_index(SEQ) * blocks_dev

    kv = keys_values.reshape(blocks_dev, BLOCK, 2 * feat)

    block_ids = first_id + jnp.arange(blocks_dev, dtype=jnp.int32)
    offset, where = wanted_blocks(rand_blocks, block_ids, all_blocks, blocks_dev)
    asked = jnp.broadcast_to(offset.reshape(LANES, 1, NZ), (LANES, NZ, NZ)).reshape(-1, NZ)
    edge = jnp.where(z == 0, kv[0], kv[blocks_dev - 1])
    rows = w_out.shape[0] // 2
    low, high = w_out[:rows], w_out[rows:]
    asked = lax.all_to_all(asked, SEQ, split_axis=0, concat_axis=0, tiled=True)
    up1, down1 = z_shift(kv, 1), z_shift(kv, -1)
    ring = NXH * NXL
    low = lax.ppermute(low, XRING, [(i, (i + 1) % ring) for i in range(ring)])
    high = lax.ppermute(high, XRING, [(i, (i - 1) % ring) for i in range(ring)])
    turns = [(NZ * i + NZ - 1, NZ * i + NZ) for i in range(LANES - 1)]
    crossed = lax.ppermute(edge, SEQ, turns + [(b, a) for a, b in turns])
    plane_ends = lane_exchange(jnp.broadcast_to(edge[None], (LANES,) + edge.shape))
    up1, down1, asked, low, high, crossed, plane_ends = tie(
        up1, down1, asked, low, high, crossed, plane_ends
    )

    up2, down2 = z_shift(up1, 1), z_shift(down1, -1)
    plan = [(0, (lane, 0), 0, lane, 0, 0) for lane in lanes]
    plan += [(0, (lane, 1), 1, lane, 0, -1) for lane in lanes]
    plan += [(0, (lane, 2), 2, lane, 0, 1) for lane in lanes]
    (c1,) = pick(zs, asked, [kv, up1, down1], plan, [(LANES, 3)])
    r1 = lane_exchange(c1)
    swap = [(0, 1), (1, 0)]
    weights = [w_out, lax.ppermute(w_out, "core", swap), low, high]
    weights += [lax.ppermute(low, "core", swap), lax.ppermute(high, "core", swap)]
    held = jnp.where(z == 0, plane_ends[0], plane_ends[LANES - 1])
    got = lax.ppermute(held, "z", [(0, 4), (7, 3)])
    held = jnp.where(jnp.logical_or(z == 4, z == 3), got, held)
    got = lax.ppermute(held, "z", [(0, 2), (4, 6), (7, 5), (3, 1)])
    fresh = reduce(jnp.logical_or, [z == 2, z == 6, z == 5, z == 1])
    held = jnp.where(fresh, got, held)
    got = lax.ppermute(held, "z", [(i, i ^ 1) for i in range(NZ)])
    even = z % 2 == 0
    ends = jnp.concatenate([jnp.where(even, held, got), jnp.where(even, got, held)], axis=0)
    before = jnp.where(z == 0, crossed, up1[blocks_dev - 1])
    after = jnp.where(z == NZ - 1, crossed, down1[0])
    kv_pad = jnp.concatenate([before, kv.reshape(tok, 2 * feat), after], axis=0)
    up2, down2, r1, ends, kv_pad = tie(up2, down2, r1, ends, kv_pad)

    plan = [(0, lane, 0, lane, 1, -2) for lane in lanes]
    plan += [(1, lane, 1, lane, -1, 2) for lane in lanes]
    plan += [(2, lane, 0, lane, 2, -2) for lane in lanes[:half]]
    plan += [(3, lane - half, 1, lane, -2, 2) for lane in lanes[half:]]
    plan += [(4, (lane, 0), 0, lane, 0, -2) for lane in lanes]
    plan += [(4, (lane, 1), 1, lane, 0, 2) for lane in lanes]
    c3u, c3d, fu, fd, c2 = pick(
        zs, asked, [up2, down2], plan, [(LANES,), (LANES,), (half,), (half,), (LANES, 2)]
    )
    fu, fd = z_shift(fu, 1), z_shift(fd, -1)
    c3u = lane_exchange(c3u)
    c3d, c3u, fu, fd = tie(c3d, c3u, fu, fd)
    r3u = z_shift(c3u, 1)
    fu, fd = z_shift(fu, 1), z_shift(fd, -1)
    c3d = lane_exchange(c3d)
    c2, c3d, fu, fd = tie(c2, c3d, fu, fd)
    r3d = z_shift(c3d, -1)
    r2 = lane_exchange(c2)
    far = jnp.concatenate([fu, fd], axis=0)
    far, r2 = tie(far, r2)
    r4 = lane_exchange(far)

    def slots(x):
        return x.reshape(LANES, 1, BLOCK, 2 * feat)

    o, st = local_part(
        zs, where, first_id.reshape(1), all_blocks, queries, kv_pad, ends, (0, -1, 1), r1
    )
    o, st = more_part(
        zs, where, queries, o, st, [(-3,), (3,), (-2, 2)], [slots(r3u), slots(r3d), r2]
    )
    attended = final_part(zs, where, queries, o, st, [(4,)], [slots(r4)])

    heads = NXL * NC
    a = lax.all_to_all(
        attended.reshape(heads, tok // heads, feat), HEAD, split_axis=0, concat_axis=0, tiled=True
    )
    return project(lax.axis_index(HEAD).reshape(1), a, weights)


def solution(mesh):
    fine = Mesh(mesh.devices.reshape(NY, NXH, NZ, NXL, NC), ("y", "xh", "z", "xl", "core"))
    in_specs = (P(SEQ, HEAD), P(SEQ, None, HEAD), P(SEQ, None), P(HEAD, None))
    out_specs = P(SEQ + HEAD, None)
    return jax.shard_map(body, mesh=fine, in_specs=in_specs, out_specs=out_specs, check_vma=False)
```

```python
from functools import reduce

import jax
import jax.numpy as jnp
from jax import lax
from jax.experimental import pallas as pl
from jax.experimental.pallas import tpu as pltpu
from jax.sharding import Mesh, PartitionSpec as P

HEAD_DIM = 128
BLOCK = 64
NEG = -1e30
SEQ = ("y", "xh", "z")
LANE = ("y", "xh")
HEAD = ("xl", "core")
XRING = ("xh", "xl")
NY, NXH, NZ, NXL, NC = 4, 2, 8, 2, 2
LANES = NY * NXH
SCALE = HEAD_DIM ** (-0.5)
F32 = jnp.float32
BF16 = jnp.bfloat16
VMEM_LIMIT = 24 * 1024 * 1024
VM = pl.BlockSpec(memory_space=pltpu.VMEM)
SM = pl.BlockSpec(memory_space=pltpu.SMEM)
HB = pl.BlockSpec(memory_space=pltpu.HBM)


def dot_nt(a, b):
    return lax.dot_general(a, b, (((1,), (1,)), ((), ())), preferred_element_type=F32)


def dot_nn(a, b):
    return jnp.dot(a, b, preferred_element_type=F32)


def row_max(a):
    return jnp.max(a, axis=1, keepdims=True)


def row_sum(a):
    return jnp.sum(a, axis=1, keepdims=True)


def local_kernel(all_blocks, deltas, z_ref, where_ref, id_ref, *refs):
    q_ref, kv_ref, ends_ref, slots_ref, o_ref, st_ref = refs
    feat = q_ref.shape[1]
    heads = range(feat // HEAD_DIM)
    blocks = q_ref.shape[0] // BLOCK
    col = lax.broadcasted_iota(jnp.int32, (BLOCK, 3 * BLOCK), 1)
    shift = jnp.where(col < BLOCK, -1, jnp.where(col < 2 * BLOCK, 0, 1))
    end_col = lax.broadcasted_iota(jnp.int32, (BLOCK, 2 * BLOCK), 1)
    kcol = [pl.ds(h * HEAD_DIM, HEAD_DIM) for h in heads]
    vcol = [pl.ds(feat + h * HEAD_DIM, HEAD_DIM) for h in heads]

    def step(j, carry):
        block = id_ref[0] + j
        near = block + shift
        near_ok = jnp.logical_and(near >= 0, near < all_blocks)
        ends_ok = jnp.where(end_col < BLOCK, block, all_blocks - 1 - block) >= 2
        rows = pl.ds(pl.multiple_of(j * BLOCK, BLOCK), BLOCK)
        wrows = pl.ds(pl.multiple_of(j * BLOCK, BLOCK), 3 * BLOCK)
        q = [q_ref[rows, kcol[h]] for h in heads]
        sw = [dot_nt(q[h], kv_ref[wrows, kcol[h]]) for h in heads]
        se = [dot_nt(q[h], ends_ref[:, kcol[h]]) for h in heads]
        sw = [jnp.where(near_ok, x * SCALE, NEG) for x in sw]
        se = [jnp.where(ends_ok, x * SCALE, NEG) for x in se]
        peak = [jnp.maximum(row_max(sw[h]), row_max(se[h])) for h in heads]
        pw = [jnp.exp(sw[h] - peak[h]) for h in heads]
        pe = [jnp.exp(se[h] - peak[h]) for h in heads]
        total = [row_sum(pw[h]) + row_sum(pe[h]) for h in heads]
        out = [
            dot_nn(pw[h].astype(BF16), kv_ref[wrows, vcol[h]])
            + dot_nn(pe[h].astype(BF16), ends_ref[:, vcol[h]])
            for h in heads
        ]
        for h in heads:
            o_ref[rows, kcol[h]] = out[h]
            st_ref[rows, pl.ds(h, 1)] = peak[h]
            st_ref[rows, pl.ds(len(heads) + h, 1)] = total[h]
        return carry

    lax.fori_loop(0, blocks, step, 0)
    add_slots(deltas, z_ref, where_ref, slots_ref, q_ref, o_ref, st_ref)


def add_slots(deltas, z_ref, where_ref, slots_ref, q_ref, o_ref, st_ref):
    feat = q_ref.shape[1]
    heads = range(feat // HEAD_DIM)
    kcol = [pl.ds(h * HEAD_DIM, HEAD_DIM) for h in heads]
    vcol = [pl.ds(feat + h * HEAD_DIM, HEAD_DIM) for h in heads]

    def step(lane, carry):
        for s, delta in enumerate(deltas):
            j = where_ref[lane * NZ + lax.rem(z_ref[0] + (delta + NZ), NZ)]

            @pl.when(j >= 0)
            def _():
                rows = pl.ds(pl.multiple_of(j * BLOCK, BLOCK), BLOCK)
                sc = [
                    dot_nt(q_ref[rows, kcol[h]], slots_ref[lane, s, :, kcol[h]]) * SCALE
                    for h in heads
                ]
                old = [st_ref[rows, pl.ds(h, 1)] for h in heads]
                tot = [st_ref[rows, pl.ds(len(heads) + h, 1)] for h in heads]
                acc = [o_ref[rows, kcol[h]] for h in heads]
                peak = [jnp.maximum(old[h], row_max(sc[h])) for h in heads]
                fade = [jnp.exp(old[h] - peak[h]) for h in heads]
                p = [jnp.exp(sc[h] - peak[h]) for h in heads]
                tot = [tot[h] * fade[h] + row_sum(p[h]) for h in heads]
                out = [dot_nn(p[h].astype(BF16), slots_ref[lane, s, :, vcol[h]]) for h in heads]
                for h in heads:
                    o_ref[rows, kcol[h]] = acc[h] * fade[h] + out[h]
                    st_ref[rows, pl.ds(h, 1)] = peak[h]
                    st_ref[rows, pl.ds(len(heads) + h, 1)] = tot[h]

        return carry

    lax.fori_loop(0, LANES, step, 0)


def more_kernel(deltas, z_ref, where_ref, q_ref, oin_ref, stin_ref, *refs):
    slots, (o_ref, st_ref) = refs[: len(deltas)], refs[len(deltas) :]
    o_ref[...] = oin_ref[...]
    st_ref[...] = stin_ref[...]
    for which, ref in zip(deltas, slots):
        add_slots(which, z_ref, where_ref, ref, q_ref, o_ref, st_ref)


def final_kernel(deltas, z_ref, where_ref, q_ref, oin_ref, stin_ref, *refs):
    slots, (att_ref, o_ref, st_ref) = refs[: len(deltas)], refs[len(deltas) :]
    more_kernel(deltas, z_ref, where_ref, q_ref, oin_ref, stin_ref, *slots, o_ref, st_ref)
    heads = range(q_ref.shape[1] // HEAD_DIM)

    def step(j, carry):
        rows = pl.ds(pl.multiple_of(j * BLOCK, BLOCK), BLOCK)
        for h in heads:
            kcol = pl.ds(h * HEAD_DIM, HEAD_DIM)
            total = st_ref[rows, pl.ds(len(heads) + h, 1)]
            att_ref[rows, kcol] = (o_ref[rows, kcol] / total).astype(BF16)
        return carry

    lax.fori_loop(0, q_ref.shape[0] // BLOCK, step, 0)


def cost(us):
    return pl.CostEstimate(flops=int(us * 1e9), bytes_accessed=4 * 2**20, transcendentals=0)


def local_part(z, where, first_id, all_blocks, q, kv_pad, ends, deltas, slots):
    tok, feat = q.shape
    return pl.pallas_call(
        lambda *refs: local_kernel(all_blocks, deltas, *refs),
        out_shape=(
            jax.ShapeDtypeStruct((tok, feat), F32),
            jax.ShapeDtypeStruct((tok, 128), F32),
        ),
        in_specs=[SM, SM, SM, VM, VM, VM, VM],
        out_specs=(VM, VM),
        compiler_params=pltpu.CompilerParams(vmem_limit_bytes=VMEM_LIMIT),
        cost_estimate=cost(25),
        name="local_part",
    )(z, where, first_id, q, kv_pad, ends, slots)


def more_part(z, where, q, o, st, deltas, slots):
    tok, feat = q.shape
    return pl.pallas_call(
        lambda *refs: more_kernel(deltas, *refs),
        out_shape=(
            jax.ShapeDtypeStruct((tok, feat), F32),
            jax.ShapeDtypeStruct((tok, 128), F32),
        ),
        in_specs=[SM, SM] + [VM] * (3 + len(slots)),
        out_specs=(VM, VM),
        compiler_params=pltpu.CompilerParams(vmem_limit_bytes=VMEM_LIMIT),
        cost_estimate=cost(12),
        name="more_part",
    )(z, where, q, o, st, *slots)


def final_part(z, where, q, o, st, deltas, slots):
    tok, feat = q.shape
    return pl.pallas_call(
        lambda *refs: final_kernel(deltas, *refs),
        out_shape=jax.ShapeDtypeStruct((tok, feat), BF16),
        in_specs=[SM, SM] + [VM] * (3 + len(slots)),
        out_specs=VM,
        scratch_shapes=[pltpu.VMEM((tok, feat), F32), pltpu.VMEM((tok, 128), F32)],
        compiler_params=pltpu.CompilerParams(vmem_limit_bytes=VMEM_LIMIT),
        cost_estimate=cost(6),
        name="final_part",
    )(z, where, q, o, st, *slots)


def pick(z, asked, sources, plan, shapes):
    def kernel(z_ref, asked_ref, *refs):
        src, out = refs[: len(sources)], refs[len(sources) : -3]
        held, in_sems, out_sems = refs[-3:]
        loads, stores = [], []
        for n, (o, position, s, lane, plane, owner) in enumerate(plan):
            row = lane * NZ + lax.rem(z_ref[0] + (plane + NZ), NZ)
            block = asked_ref[row, lax.rem(z_ref[0] + (owner + NZ), NZ)]
            loads.append(pltpu.make_async_copy(src[s].at[block], held.at[n], in_sems.at[n]))
            stores.append(pltpu.make_async_copy(held.at[n], out[o].at[position], out_sems.at[n]))
            loads[-1].start()
        for load, store in zip(loads, stores):
            load.wait()
            store.start()
        for store in stores:
            store.wait()

    block_shape = sources[0].shape[1:]
    return pl.pallas_call(
        kernel,
        out_shape=tuple(pltpu.HBM(shape + block_shape, BF16) for shape in shapes),
        in_specs=[SM, SM] + [HB] * len(sources),
        out_specs=tuple(HB for _ in shapes),
        scratch_shapes=[
            pltpu.VMEM((len(plan),) + block_shape, BF16),
            pltpu.SemaphoreType.DMA((len(plan),)),
            pltpu.SemaphoreType.DMA((len(plan),)),
        ],
        compiler_params=pltpu.CompilerParams(vmem_limit_bytes=8 * 1024 * 1024),
        cost_estimate=cost(3),
        name="pick",
    )(z, asked, *sources)


def project_kernel(tile, me_ref, a_ref, *refs):
    weights, (out_ref, w_ref, acat_ref, sems) = refs[:-4], refs[-4:]
    rows, feat = a_ref.shape[1:]
    cols = out_ref.shape[1]
    copies = []
    for n in range(cols // tile):
        top = 0
        span = pl.ds(n * tile, tile)
        for k, weight in enumerate(weights):
            part = pl.ds(top, weight.shape[0])
            copies.append(
                pltpu.make_async_copy(
                    weight.at[:, span], w_ref.at[part, span], sems.at[n * len(weights) + k]
                )
            )
            copies[-1].start()
            top += weight.shape[0]
    me = me_ref[0]
    for g in range(a_ref.shape[0]):
        acat_ref[:, pl.ds(g * feat, feat)] = a_ref[me ^ g]
    for n in range(cols // tile):
        for k in range(len(weights)):
            copies[n * len(weights) + k].wait()
        span = pl.ds(n * tile, tile)
        out_ref[:, span] = dot_nn(acat_ref[...], w_ref[:, span]).astype(BF16)


def project(me, a, weights, tile=512):
    groups, rows, feat = a.shape
    cols = weights[0].shape[1]
    return pl.pallas_call(
        lambda *refs: project_kernel(tile, *refs),
        out_shape=jax.ShapeDtypeStruct((rows, cols), BF16),
        in_specs=[SM, VM] + [HB] * len(weights),
        out_specs=VM,
        scratch_shapes=[
            pltpu.VMEM((groups * feat, cols), BF16),
            pltpu.VMEM((rows, groups * feat), BF16),
            pltpu.SemaphoreType.DMA((cols // tile * len(weights),)),
        ],
        compiler_params=pltpu.CompilerParams(vmem_limit_bytes=VMEM_LIMIT),
        name="project",
    )(me, a, *weights)


def z_shift(x, by):
    return lax.ppermute(x, "z", [(i, (i + by) % NZ) for i in range(NZ)])


def lane_exchange(x):
    return lax.all_to_all(x, LANE, split_axis=0, concat_axis=0, tiled=True)


def wanted_blocks(rand_blocks, block_ids, all_blocks, blocks_dev):
    taken = [
        block_ids - 1,
        block_ids,
        block_ids + 1,
        jnp.zeros_like(block_ids),
        jnp.zeros_like(block_ids) + (all_blocks - 1),
    ]
    fresh = []
    for column in range(rand_blocks.shape[1]):
        chosen = rand_blocks[:, column]
        clash = reduce(jnp.logical_or, [chosen == other for other in taken])
        fresh.append(jnp.logical_not(clash))
        taken.append(chosen)
    fresh = jnp.stack(fresh, axis=1).reshape(-1)
    flat = rand_blocks.reshape(-1)
    entries = flat.shape[0]
    query = jnp.arange(entries, dtype=jnp.int32) // rand_blocks.shape[1]
    owners = jnp.arange(all_blocks // blocks_dev, dtype=jnp.int32)
    named = (flat // blocks_dev)[:, None] == owners[None, :]
    offset = jnp.sum(jnp.where(named, (flat % blocks_dev)[:, None], 0), axis=0)
    used = jnp.logical_and(named, fresh[:, None])
    where = jnp.sum(jnp.where(used, query[:, None] + 1, 0), axis=0) - 1
    return offset.astype(jnp.int32), where.astype(jnp.int32)


def tie(*arrays):
    return lax.optimization_barrier(arrays)


def body(queries, keys_values, rand_blocks, w_out):
    tok, feat = queries.shape
    blocks_dev = tok // BLOCK
    all_blocks = blocks_dev * LANES * NZ
    lanes = range(LANES)
    half = LANES // 2
    z = lax.axis_index("z")
    zs = z.reshape(1)
    first_id = lax.axis_index(SEQ) * blocks_dev

    kv = keys_values.reshape(blocks_dev, BLOCK, 2 * feat)

    block_ids = first_id + jnp.arange(blocks_dev, dtype=jnp.int32)
    offset, where = wanted_blocks(rand_blocks, block_ids, all_blocks, blocks_dev)
    asked = jnp.broadcast_to(offset.reshape(LANES, 1, NZ), (LANES, NZ, NZ)).reshape(-1, NZ)
    edge = jnp.where(z == 0, kv[0], kv[blocks_dev - 1])
    rows = w_out.shape[0] // 2
    low, high = w_out[:rows], w_out[rows:]
    asked = lax.all_to_all(asked, SEQ, split_axis=0, concat_axis=0, tiled=True)
    up1, down1 = z_shift(kv, 1), z_shift(kv, -1)
    ring = NXH * NXL
    low = lax.ppermute(low, XRING, [(i, (i + 1) % ring) for i in range(ring)])
    high = lax.ppermute(high, XRING, [(i, (i - 1) % ring) for i in range(ring)])
    turns = [(NZ * i + NZ - 1, NZ * i + NZ) for i in range(LANES - 1)]
    crossed = lax.ppermute(edge, SEQ, turns + [(b, a) for a, b in turns])
    up1, down1, asked, low, high, crossed, edge = tie(
        up1, down1, asked, low, high, crossed, edge
    )

    up2, down2 = z_shift(up1, 1), z_shift(down1, -1)
    plan = [(0, (lane, 0), 0, lane, 0, 0) for lane in lanes]
    plan += [(0, (lane, 1), 1, lane, 0, -1) for lane in lanes]
    plan += [(0, (lane, 2), 2, lane, 0, 1) for lane in lanes]
    (c1,) = pick(zs, asked, [kv, up1, down1], plan, [(LANES, 3)])
    r1 = lane_exchange(c1)
    swap = [(0, 1), (1, 0)]
    weights = [w_out, lax.ppermute(w_out, "core", swap), low, high]
    weights += [lax.ppermute(low, "core", swap), lax.ppermute(high, "core", swap)]
    edge, r1 = tie(edge, r1)
    plane_ends = lane_exchange(jnp.broadcast_to(edge[None], (LANES,) + edge.shape))
    before = jnp.where(z == 0, crossed, up1[blocks_dev - 1])
    after = jnp.where(z == NZ - 1, crossed, down1[0])
    kv_pad = jnp.concatenate([before, kv.reshape(tok, 2 * feat), after], axis=0)
    up2, down2, r1, plane_ends, kv_pad = tie(up2, down2, r1, plane_ends, kv_pad)

    held = jnp.where(z == 0, plane_ends[0], plane_ends[LANES - 1])
    got = lax.ppermute(held, "z", [(0, 4), (7, 3)])
    held = jnp.where(jnp.logical_or(z == 4, z == 3), got, held)
    got = lax.ppermute(held, "z", [(0, 2), (4, 6), (7, 5), (3, 1)])
    fresh = reduce(jnp.logical_or, [z == 2, z == 6, z == 5, z == 1])
    held = jnp.where(fresh, got, held)
    got = lax.ppermute(held, "z", [(i, i ^ 1) for i in range(NZ)])
    even = z % 2 == 0
    ends = jnp.concatenate([jnp.where(even, held, got), jnp.where(even, got, held)], axis=0)

    plan = [(0, lane, 0, lane, 1, -2) for lane in lanes]
    plan += [(1, lane, 1, lane, -1, 2) for lane in lanes]
    plan += [(2, lane, 0, lane, 2, -2) for lane in lanes[:half]]
    plan += [(3, lane - half, 1, lane, -2, 2) for lane in lanes[half:]]
    plan += [(4, (lane, 0), 0, lane, 0, -2) for lane in lanes]
    plan += [(4, (lane, 1), 1, lane, 0, 2) for lane in lanes]
    c3u, c3d, fu, fd, c2 = pick(
        zs, asked, [up2, down2], plan, [(LANES,), (LANES,), (half,), (half,), (LANES, 2)]
    )
    fu, fd = z_shift(fu, 1), z_shift(fd, -1)
    c3u = lane_exchange(c3u)
    c3d, c3u, fu, fd = tie(c3d, c3u, fu, fd)
    r3u = z_shift(c3u, 1)
    fu, fd = z_shift(fu, 1), z_shift(fd, -1)
    c3d = lane_exchange(c3d)
    c2, c3d, fu, fd = tie(c2, c3d, fu, fd)
    r3d = z_shift(c3d, -1)
    r2 = lane_exchange(c2)
    far = jnp.concatenate([fu, fd], axis=0)
    far, r2 = tie(far, r2)
    r4 = lane_exchange(far)

    def slots(x):
        return x.reshape(LANES, 1, BLOCK, 2 * feat)

    o, st = local_part(
        zs, where, first_id.reshape(1), all_blocks, queries, kv_pad, ends, (0, -1, 1), r1
    )
    o, st = more_part(
        zs, where, queries, o, st, [(-3,), (3,), (-2, 2)], [slots(r3u), slots(r3d), r2]
    )
    attended = final_part(zs, where, queries, o, st, [(4,)], [slots(r4)])

    heads = NXL * NC
    a = lax.all_to_all(
        attended.reshape(heads, tok // heads, feat), HEAD, split_axis=0, concat_axis=0, tiled=True
    )
    return project(lax.axis_index(HEAD).reshape(1), a, weights)


def solution(mesh):
    fine = Mesh(mesh.devices.reshape(NY, NXH, NZ, NXL, NC), ("y", "xh", "z", "xl", "core"))
    in_specs = (P(SEQ, HEAD), P(SEQ, None, HEAD), P(SEQ, None), P(HEAD, None))
    out_specs = P(SEQ + HEAD, None)
    return jax.shard_map(body, mesh=fine, in_specs=in_specs, out_specs=out_specs, check_vma=False)
```

```python
from functools import reduce

import jax
import jax.numpy as jnp
from jax import lax
from jax.experimental import pallas as pl
from jax.experimental.pallas import tpu as pltpu
from jax.sharding import Mesh, PartitionSpec as P

HEAD_DIM = 128
BLOCK = 64
NEG = -1e30
SEQ = ("y", "xh", "z")
LANE = ("y", "xh")
HEAD = ("xl", "core")
XRING = ("xh", "xl")
NY, NXH, NZ, NXL, NC = 4, 2, 8, 2, 2
LANES = NY * NXH
SCALE = HEAD_DIM ** (-0.5)
F32 = jnp.float32
BF16 = jnp.bfloat16
VMEM_LIMIT = 24 * 1024 * 1024
VM = pl.BlockSpec(memory_space=pltpu.VMEM)
SM = pl.BlockSpec(memory_space=pltpu.SMEM)
HB = pl.BlockSpec(memory_space=pltpu.HBM)


def dot_nt(a, b):
    return lax.dot_general(a, b, (((1,), (1,)), ((), ())), preferred_element_type=F32)


def dot_nn(a, b):
    return jnp.dot(a, b, preferred_element_type=F32)


def row_max(a):
    return jnp.max(a, axis=1, keepdims=True)


def row_sum(a):
    return jnp.sum(a, axis=1, keepdims=True)


def local_kernel(all_blocks, deltas, z_ref, where_ref, id_ref, *refs):
    q_ref, kv_ref, ends_ref = refs[:3]
    slots, (o_ref, st_ref) = refs[3:-2], refs[-2:]
    feat = q_ref.shape[1]
    heads = range(feat // HEAD_DIM)
    blocks = q_ref.shape[0] // BLOCK
    col = lax.broadcasted_iota(jnp.int32, (BLOCK, 3 * BLOCK), 1)
    shift = jnp.where(col < BLOCK, -1, jnp.where(col < 2 * BLOCK, 0, 1))
    end_col = lax.broadcasted_iota(jnp.int32, (BLOCK, 2 * BLOCK), 1)
    kcol = [pl.ds(h * HEAD_DIM, HEAD_DIM) for h in heads]
    vcol = [pl.ds(feat + h * HEAD_DIM, HEAD_DIM) for h in heads]

    def step(j, carry):
        block = id_ref[0] + j
        near = block + shift
        near_ok = jnp.logical_and(near >= 0, near < all_blocks)
        ends_ok = jnp.where(end_col < BLOCK, block, all_blocks - 1 - block) >= 2
        rows = pl.ds(pl.multiple_of(j * BLOCK, BLOCK), BLOCK)
        wrows = pl.ds(pl.multiple_of(j * BLOCK, BLOCK), 3 * BLOCK)
        q = [q_ref[rows, kcol[h]] for h in heads]
        sw = [dot_nt(q[h], kv_ref[wrows, kcol[h]]) for h in heads]
        se = [dot_nt(q[h], ends_ref[:, kcol[h]]) for h in heads]
        sw = [jnp.where(near_ok, x * SCALE, NEG) for x in sw]
        se = [jnp.where(ends_ok, x * SCALE, NEG) for x in se]
        peak = [jnp.maximum(row_max(sw[h]), row_max(se[h])) for h in heads]
        pw = [jnp.exp(sw[h] - peak[h]) for h in heads]
        pe = [jnp.exp(se[h] - peak[h]) for h in heads]
        total = [row_sum(pw[h]) + row_sum(pe[h]) for h in heads]
        out = [
            dot_nn(pw[h].astype(BF16), kv_ref[wrows, vcol[h]])
            + dot_nn(pe[h].astype(BF16), ends_ref[:, vcol[h]])
            for h in heads
        ]
        for h in heads:
            o_ref[rows, kcol[h]] = out[h]
            st_ref[rows, pl.ds(h, 1)] = peak[h]
            st_ref[rows, pl.ds(len(heads) + h, 1)] = total[h]
        return carry

    lax.fori_loop(0, blocks, step, 0)
    for which, ref in zip(deltas, slots):
        add_slots(which, z_ref, where_ref, ref, q_ref, o_ref, st_ref)


def add_slots(deltas, z_ref, where_ref, slots_ref, q_ref, o_ref, st_ref):
    feat = q_ref.shape[1]
    heads = range(feat // HEAD_DIM)
    kcol = [pl.ds(h * HEAD_DIM, HEAD_DIM) for h in heads]
    vcol = [pl.ds(feat + h * HEAD_DIM, HEAD_DIM) for h in heads]

    def step(lane, carry):
        for s, delta in enumerate(deltas):
            j = where_ref[lane * NZ + lax.rem(z_ref[0] + (delta + NZ), NZ)]

            @pl.when(j >= 0)
            def _():
                rows = pl.ds(pl.multiple_of(j * BLOCK, BLOCK), BLOCK)
                sc = [
                    dot_nt(q_ref[rows, kcol[h]], slots_ref[lane, s, :, kcol[h]]) * SCALE
                    for h in heads
                ]
                old = [st_ref[rows, pl.ds(h, 1)] for h in heads]
                tot = [st_ref[rows, pl.ds(len(heads) + h, 1)] for h in heads]
                acc = [o_ref[rows, kcol[h]] for h in heads]
                peak = [jnp.maximum(old[h], row_max(sc[h])) for h in heads]
                fade = [jnp.exp(old[h] - peak[h]) for h in heads]
                p = [jnp.exp(sc[h] - peak[h]) for h in heads]
                tot = [tot[h] * fade[h] + row_sum(p[h]) for h in heads]
                out = [dot_nn(p[h].astype(BF16), slots_ref[lane, s, :, vcol[h]]) for h in heads]
                for h in heads:
                    o_ref[rows, kcol[h]] = acc[h] * fade[h] + out[h]
                    st_ref[rows, pl.ds(h, 1)] = peak[h]
                    st_ref[rows, pl.ds(len(heads) + h, 1)] = tot[h]

        return carry

    lax.fori_loop(0, LANES, step, 0)


def more_kernel(deltas, z_ref, where_ref, q_ref, oin_ref, stin_ref, *refs):
    slots, (o_ref, st_ref) = refs[: len(deltas)], refs[len(deltas) :]
    o_ref[...] = oin_ref[...]
    st_ref[...] = stin_ref[...]
    for which, ref in zip(deltas, slots):
        add_slots(which, z_ref, where_ref, ref, q_ref, o_ref, st_ref)


def final_kernel(deltas, z_ref, where_ref, q_ref, oin_ref, stin_ref, *refs):
    slots, (att_ref, o_ref, st_ref) = refs[: len(deltas)], refs[len(deltas) :]
    more_kernel(deltas, z_ref, where_ref, q_ref, oin_ref, stin_ref, *slots, o_ref, st_ref)
    heads = range(q_ref.shape[1] // HEAD_DIM)

    def step(j, carry):
        rows = pl.ds(pl.multiple_of(j * BLOCK, BLOCK), BLOCK)
        for h in heads:
            kcol = pl.ds(h * HEAD_DIM, HEAD_DIM)
            total = st_ref[rows, pl.ds(len(heads) + h, 1)]
            att_ref[rows, kcol] = (o_ref[rows, kcol] / total).astype(BF16)
        return carry

    lax.fori_loop(0, q_ref.shape[0] // BLOCK, step, 0)


def cost(us):
    return pl.CostEstimate(flops=int(us * 1e9), bytes_accessed=4 * 2**20, transcendentals=0)


def local_part(z, where, first_id, all_blocks, q, kv_pad, ends, deltas, slots):
    tok, feat = q.shape
    return pl.pallas_call(
        lambda *refs: local_kernel(all_blocks, deltas, *refs),
        out_shape=(
            jax.ShapeDtypeStruct((tok, feat), F32),
            jax.ShapeDtypeStruct((tok, 128), F32),
        ),
        in_specs=[SM, SM, SM] + [VM] * (3 + len(slots)),
        out_specs=(VM, VM),
        compiler_params=pltpu.CompilerParams(vmem_limit_bytes=VMEM_LIMIT),
        cost_estimate=cost(25),
        name="local_part",
    )(z, where, first_id, q, kv_pad, ends, *slots)


def more_part(z, where, q, o, st, deltas, slots):
    tok, feat = q.shape
    return pl.pallas_call(
        lambda *refs: more_kernel(deltas, *refs),
        out_shape=(
            jax.ShapeDtypeStruct((tok, feat), F32),
            jax.ShapeDtypeStruct((tok, 128), F32),
        ),
        in_specs=[SM, SM] + [VM] * (3 + len(slots)),
        out_specs=(VM, VM),
        compiler_params=pltpu.CompilerParams(vmem_limit_bytes=VMEM_LIMIT),
        cost_estimate=cost(12),
        name="more_part",
    )(z, where, q, o, st, *slots)


def final_part(z, where, q, o, st, deltas, slots):
    tok, feat = q.shape
    return pl.pallas_call(
        lambda *refs: final_kernel(deltas, *refs),
        out_shape=jax.ShapeDtypeStruct((tok, feat), BF16),
        in_specs=[SM, SM] + [VM] * (3 + len(slots)),
        out_specs=VM,
        scratch_shapes=[pltpu.VMEM((tok, feat), F32), pltpu.VMEM((tok, 128), F32)],
        compiler_params=pltpu.CompilerParams(vmem_limit_bytes=VMEM_LIMIT),
        cost_estimate=cost(6),
        name="final_part",
    )(z, where, q, o, st, *slots)


def pick(z, asked, sources, plan, shapes):
    def kernel(z_ref, asked_ref, *refs):
        src, out = refs[: len(sources)], refs[len(sources) : -3]
        held, in_sems, out_sems = refs[-3:]
        loads, stores = [], []
        for n, (o, position, s, lane, plane, owner) in enumerate(plan):
            if lane is None:
                block = jnp.where(z_ref[0] == 0, 0, sources[s].shape[0] - 1)
            else:
                row = lane
                if asked.shape[0] > LANES:
                    row = lax.rem(z_ref[0] + (plane + NZ), NZ) * LANES + lane
                block = asked_ref[row, lax.rem(z_ref[0] + (owner + NZ), NZ)]
            loads.append(pltpu.make_async_copy(src[s].at[block], held.at[n], in_sems.at[n]))
            stores.append(pltpu.make_async_copy(held.at[n], out[o].at[position], out_sems.at[n]))
            loads[-1].start()
        for load, store in zip(loads, stores):
            load.wait()
            store.start()
        for store in stores:
            store.wait()

    block_shape = sources[0].shape[1:]
    return pl.pallas_call(
        kernel,
        out_shape=tuple(pltpu.HBM(shape + block_shape, BF16) for shape in shapes),
        in_specs=[SM, SM] + [HB] * len(sources),
        out_specs=tuple(HB for _ in shapes),
        scratch_shapes=[
            pltpu.VMEM((len(plan),) + block_shape, BF16),
            pltpu.SemaphoreType.DMA((len(plan),)),
            pltpu.SemaphoreType.DMA((len(plan),)),
        ],
        compiler_params=pltpu.CompilerParams(vmem_limit_bytes=8 * 1024 * 1024),
        cost_estimate=cost(3),
        name="pick",
    )(z, asked, *sources)


def project_kernel(tile, me_ref, a_ref, *refs):
    weights, (out_ref, w_ref, acat_ref, sems) = refs[:-4], refs[-4:]
    rows, feat = a_ref.shape[1:]
    cols = out_ref.shape[1]
    copies = []
    for n in range(cols // tile):
        top = 0
        span = pl.ds(n * tile, tile)
        for k, weight in enumerate(weights):
            part = pl.ds(top, weight.shape[0])
            copies.append(
                pltpu.make_async_copy(
                    weight.at[:, span], w_ref.at[part, span], sems.at[n * len(weights) + k]
                )
            )
            copies[-1].start()
            top += weight.shape[0]
    me = me_ref[0]
    for g in range(a_ref.shape[0]):
        acat_ref[:, pl.ds(g * feat, feat)] = a_ref[me ^ g]
    for n in range(cols // tile):
        for k in range(len(weights)):
            copies[n * len(weights) + k].wait()
        span = pl.ds(n * tile, tile)
        out_ref[:, span] = dot_nn(acat_ref[...], w_ref[:, span]).astype(BF16)


def project(me, a, weights, tile=512):
    groups, rows, feat = a.shape
    cols = weights[0].shape[1]
    return pl.pallas_call(
        lambda *refs: project_kernel(tile, *refs),
        out_shape=jax.ShapeDtypeStruct((rows, cols), BF16),
        in_specs=[SM, VM] + [HB] * len(weights),
        out_specs=VM,
        scratch_shapes=[
            pltpu.VMEM((groups * feat, cols), BF16),
            pltpu.VMEM((rows, groups * feat), BF16),
            pltpu.SemaphoreType.DMA((cols // tile * len(weights),)),
        ],
        compiler_params=pltpu.CompilerParams(vmem_limit_bytes=VMEM_LIMIT),
        name="project",
    )(me, a, *weights)


def z_shift(x, by):
    return lax.ppermute(x, "z", [(i, (i + by) % NZ) for i in range(NZ)])


def lane_exchange(x):
    return lax.all_to_all(x, LANE, split_axis=0, concat_axis=0, tiled=True)


def wanted_blocks(rand_blocks, block_ids, all_blocks, blocks_dev):
    taken = [
        block_ids - 1,
        block_ids,
        block_ids + 1,
        jnp.zeros_like(block_ids),
        jnp.zeros_like(block_ids) + (all_blocks - 1),
    ]
    fresh = []
    for column in range(rand_blocks.shape[1]):
        chosen = rand_blocks[:, column]
        clash = reduce(jnp.logical_or, [chosen == other for other in taken])
        fresh.append(jnp.logical_not(clash))
        taken.append(chosen)
    fresh = jnp.stack(fresh, axis=1).reshape(-1)
    flat = rand_blocks.reshape(-1)
    entries = flat.shape[0]
    query = jnp.arange(entries, dtype=jnp.int32) // rand_blocks.shape[1]
    owners = jnp.arange(all_blocks // blocks_dev, dtype=jnp.int32)
    named = (flat // blocks_dev)[:, None] == owners[None, :]
    offset = jnp.sum(jnp.where(named, (flat % blocks_dev)[:, None], 0), axis=0)
    used = jnp.logical_and(named, fresh[:, None])
    where = jnp.sum(jnp.where(used, query[:, None] + 1, 0), axis=0) - 1
    return offset.astype(jnp.int32), where.astype(jnp.int32)


def tie(*arrays):
    return lax.optimization_barrier(arrays)


def body(queries, keys_values, rand_blocks, w_out):
    tok, feat = queries.shape
    blocks_dev = tok // BLOCK
    all_blocks = blocks_dev * LANES * NZ
    lanes = range(LANES)
    half = LANES // 2
    z = lax.axis_index("z")
    zs = z.reshape(1)
    first_id = lax.axis_index(SEQ) * blocks_dev

    kv = keys_values.reshape(blocks_dev, BLOCK, 2 * feat)

    up1, down1 = z_shift(kv, 1), z_shift(kv, -1)
    block_ids = first_id + jnp.arange(blocks_dev, dtype=jnp.int32)
    offset, where = wanted_blocks(rand_blocks, block_ids, all_blocks, blocks_dev)
    mine = lane_exchange(offset.reshape(LANES, NZ))
    rows = w_out.shape[0] // 2
    own = [w_out[:rows], w_out[rows:]]
    ring = NXH * NXL
    low = lax.ppermute(own[0], XRING, [(i, (i + 1) % ring) for i in range(ring)])
    high = lax.ppermute(own[1], XRING, [(i, (i - 1) % ring) for i in range(ring)])
    edge = jnp.where(z == 0, kv[0], kv[blocks_dev - 1])
    turns = [(NZ * i + NZ - 1, NZ * i + NZ) for i in range(LANES - 1)]
    crossed = lax.ppermute(edge, SEQ, turns + [(b, a) for a, b in turns])
    plan = [(0, (lane, 0), 0, lane, 0, 0) for lane in lanes]
    plan += [(0, (lane, 1), 0, None, 0, 0) for lane in lanes]
    (c0,) = pick(zs, mine, [kv], plan, [(LANES, 2)])
    r0 = lane_exchange(c0)
    table, r0 = tie(mine, r0)
    table = jnp.broadcast_to(table[None], (NZ, LANES, NZ))
    asked = lax.all_to_all(table, "z", split_axis=0, concat_axis=0, tiled=True)
    asked = asked.reshape(NZ * LANES, NZ)
    up1, down1, asked, low, high, crossed, r0 = tie(up1, down1, asked, low, high, crossed, r0)

    plan = [(0, lane, 0, lane, 3, -1) for lane in lanes[:half]]
    plan += [(1, lane - half, 1, lane, -3, 1) for lane in lanes[half:]]
    plan += [(2, lane, 0, lane, 2, -1) for lane in lanes]
    plan += [(3, lane, 1, lane, -2, 1) for lane in lanes]
    fu, fd, c3u, c3d = pick(
        zs, asked, [up1, down1], plan, [(half,), (half,), (LANES,), (LANES,)]
    )
    fu, fd = z_shift(fu, 1), z_shift(fd, -1)
    c3u, c3d = z_shift(c3u, 1), z_shift(c3d, -1)
    plan = [(0, (lane, 0), 0, lane, 1, -1) for lane in lanes]
    plan += [(0, (lane, 1), 1, lane, -1, 1) for lane in lanes]
    plan += [(1, (lane, 0), 0, lane, 0, -1) for lane in lanes]
    plan += [(1, (lane, 1), 1, lane, 0, 1) for lane in lanes]
    c2, c1 = pick(zs, asked, [up1, down1], plan, [(LANES, 2), (LANES, 2)])
    c2 = lane_exchange(c2)
    swap = [(0, 1), (1, 0)]
    weights = own + [lax.ppermute(w_out, "core", swap), low, high]
    weights += [lax.ppermute(low, "core", swap), lax.ppermute(high, "core", swap)]
    before = jnp.where(z == 0, crossed, up1[blocks_dev - 1])
    after = jnp.where(z == NZ - 1, crossed, down1[0])
    kv_pad = jnp.concatenate([before, kv.reshape(tok, 2 * feat), after], axis=0)
    held = jnp.where(z == 0, r0[0, 1], r0[LANES - 1, 1])
    got = lax.ppermute(held, "z", [(0, 4), (7, 3)])
    held = jnp.where(jnp.logical_or(z == 4, z == 3), got, held)
    fu, fd, c3u, c3d, c2, c1, kv_pad, held = tie(fu, fd, c3u, c3d, c2, c1, kv_pad, held)

    fu, fd = z_shift(fu, 1), z_shift(fd, -1)
    r1 = lane_exchange(c1)
    r2u, r2d = z_shift(c2[:, 0], 1), z_shift(c2[:, 1], -1)
    got = lax.ppermute(held, "z", [(0, 2), (4, 6), (7, 5), (3, 1)])
    fresh = reduce(jnp.logical_or, [z == 2, z == 6, z == 5, z == 1])
    held = jnp.where(fresh, got, held)
    c3u, r1, fu, fd = tie(c3u, r1, fu, fd)
    fu, fd = z_shift(fu, 1), z_shift(fd, -1)
    got = lax.ppermute(held, "z", [(i, i ^ 1) for i in range(NZ)])
    even = z % 2 == 0
    ends = jnp.concatenate([jnp.where(even, held, got), jnp.where(even, got, held)], axis=0)
    c3u = lane_exchange(c3u)
    c3d, c3u = tie(c3d, c3u)
    r3u = z_shift(c3u, 1)
    c3d = lane_exchange(c3d)
    far = jnp.concatenate([fu, fd], axis=0)
    far, c3d = tie(far, c3d)
    r3d = z_shift(c3d, -1)
    r4 = lane_exchange(far)

    def slots(x):
        return x.reshape(LANES, 1, BLOCK, 2 * feat)

    o, st = local_part(
        zs, where, first_id.reshape(1), all_blocks, queries, kv_pad, ends, [(0,), (-1, 1)], [r0, r1]
    )
    o, st = more_part(
        zs, where, queries, o, st, [(-2,), (2,), (-3,), (3,)], [slots(x) for x in (r2u, r2d, r3u, r3d)]
    )
    attended = final_part(zs, where, queries, o, st, [(4,)], [slots(r4)])

    heads = NXL * NC
    a = lax.all_to_all(
        attended.reshape(heads, tok // heads, feat), HEAD, split_axis=0, concat_axis=0, tiled=True
    )
    return project(lax.axis_index(HEAD).reshape(1), a, weights)


def solution(mesh):
    fine = Mesh(mesh.devices.reshape(NY, NXH, NZ, NXL, NC), ("y", "xh", "z", "xl", "core"))
    in_specs = (P(SEQ, HEAD), P(SEQ, None, HEAD), P(SEQ, None), P(HEAD, None))
    out_specs = P(SEQ + HEAD, None)
    return jax.shard_map(body, mesh=fine, in_specs=in_specs, out_specs=out_specs, check_vma=False)
```

```python
from functools import reduce

import jax
import jax.numpy as jnp
from jax import lax
from jax.experimental import pallas as pl
from jax.experimental.pallas import tpu as pltpu
from jax.sharding import Mesh, PartitionSpec as P

HEAD_DIM = 128
BLOCK = 64
NEG = -1e30
SEQ = ("y", "xh", "z")
LANE = ("y", "xh")
HEAD = ("xl", "core")
XRING = ("xh", "xl")
NY, NXH, NZ, NXL, NC = 4, 2, 8, 2, 2
LANES = NY * NXH
SCALE = HEAD_DIM ** (-0.5)
F32 = jnp.float32
BF16 = jnp.bfloat16
VMEM_LIMIT = 24 * 1024 * 1024
VM = pl.BlockSpec(memory_space=pltpu.VMEM)
SM = pl.BlockSpec(memory_space=pltpu.SMEM)
HB = pl.BlockSpec(memory_space=pltpu.HBM)


def dot_nt(a, b):
    return lax.dot_general(a, b, (((1,), (1,)), ((), ())), preferred_element_type=F32)


def dot_nn(a, b):
    return jnp.dot(a, b, preferred_element_type=F32)


def row_max(a):
    return jnp.max(a, axis=1, keepdims=True)


def row_sum(a):
    return jnp.sum(a, axis=1, keepdims=True)


def local_kernel(all_blocks, deltas, z_ref, where_ref, id_ref, *refs):
    q_ref, kv_ref, ends_ref, slots_ref, o_ref, st_ref = refs
    feat = q_ref.shape[1]
    heads = range(feat // HEAD_DIM)
    blocks = q_ref.shape[0] // BLOCK
    col = lax.broadcasted_iota(jnp.int32, (BLOCK, 3 * BLOCK), 1)
    shift = jnp.where(col < BLOCK, -1, jnp.where(col < 2 * BLOCK, 0, 1))
    end_col = lax.broadcasted_iota(jnp.int32, (BLOCK, 2 * BLOCK), 1)
    kcol = [pl.ds(h * HEAD_DIM, HEAD_DIM) for h in heads]
    vcol = [pl.ds(feat + h * HEAD_DIM, HEAD_DIM) for h in heads]

    def step(j, carry):
        block = id_ref[0] + j
        near = block + shift
        near_ok = jnp.logical_and(near >= 0, near < all_blocks)
        ends_ok = jnp.where(end_col < BLOCK, block, all_blocks - 1 - block) >= 2
        rows = pl.ds(pl.multiple_of(j * BLOCK, BLOCK), BLOCK)
        wrows = pl.ds(pl.multiple_of(j * BLOCK, BLOCK), 3 * BLOCK)
        q = [q_ref[rows, kcol[h]] for h in heads]
        sw = [dot_nt(q[h], kv_ref[wrows, kcol[h]]) for h in heads]
        se = [dot_nt(q[h], ends_ref[:, kcol[h]]) for h in heads]
        sw = [jnp.where(near_ok, x * SCALE, NEG) for x in sw]
        se = [jnp.where(ends_ok, x * SCALE, NEG) for x in se]
        peak = [jnp.maximum(row_max(sw[h]), row_max(se[h])) for h in heads]
        pw = [jnp.exp(sw[h] - peak[h]) for h in heads]
        pe = [jnp.exp(se[h] - peak[h]) for h in heads]
        total = [row_sum(pw[h]) + row_sum(pe[h]) for h in heads]
        out = [
            dot_nn(pw[h].astype(BF16), kv_ref[wrows, vcol[h]])
            + dot_nn(pe[h].astype(BF16), ends_ref[:, vcol[h]])
            for h in heads
        ]
        for h in heads:
            o_ref[rows, kcol[h]] = out[h]
            st_ref[rows, pl.ds(h, 1)] = peak[h]
            st_ref[rows, pl.ds(len(heads) + h, 1)] = total[h]
        return carry

    lax.fori_loop(0, blocks, step, 0)
    add_slots(deltas, z_ref, where_ref, slots_ref, q_ref, o_ref, st_ref)


def add_slots(deltas, z_ref, where_ref, slots_ref, q_ref, o_ref, st_ref):
    feat = q_ref.shape[1]
    heads = range(feat // HEAD_DIM)
    kcol = [pl.ds(h * HEAD_DIM, HEAD_DIM) for h in heads]
    vcol = [pl.ds(feat + h * HEAD_DIM, HEAD_DIM) for h in heads]

    def step(lane, carry):
        for s, delta in enumerate(deltas):
            j = where_ref[lane * NZ + lax.rem(z_ref[0] + (delta + NZ), NZ)]

            @pl.when(j >= 0)
            def _():
                rows = pl.ds(pl.multiple_of(j * BLOCK, BLOCK), BLOCK)
                sc = [
                    dot_nt(q_ref[rows, kcol[h]], slots_ref[lane, s, :, kcol[h]]) * SCALE
                    for h in heads
                ]
                old = [st_ref[rows, pl.ds(h, 1)] for h in heads]
                tot = [st_ref[rows, pl.ds(len(heads) + h, 1)] for h in heads]
                acc = [o_ref[rows, kcol[h]] for h in heads]
                peak = [jnp.maximum(old[h], row_max(sc[h])) for h in heads]
                fade = [jnp.exp(old[h] - peak[h]) for h in heads]
                p = [jnp.exp(sc[h] - peak[h]) for h in heads]
                tot = [tot[h] * fade[h] + row_sum(p[h]) for h in heads]
                out = [dot_nn(p[h].astype(BF16), slots_ref[lane, s, :, vcol[h]]) for h in heads]
                for h in heads:
                    o_ref[rows, kcol[h]] = acc[h] * fade[h] + out[h]
                    st_ref[rows, pl.ds(h, 1)] = peak[h]
                    st_ref[rows, pl.ds(len(heads) + h, 1)] = tot[h]

        return carry

    lax.fori_loop(0, LANES, step, 0)


def more_kernel(deltas, z_ref, where_ref, q_ref, oin_ref, stin_ref, *refs):
    slots, (o_ref, st_ref) = refs[: len(deltas)], refs[len(deltas) :]
    o_ref[...] = oin_ref[...]
    st_ref[...] = stin_ref[...]
    for which, ref in zip(deltas, slots):
        add_slots(which, z_ref, where_ref, ref, q_ref, o_ref, st_ref)


def final_kernel(deltas, z_ref, where_ref, q_ref, oin_ref, stin_ref, *refs):
    slots, (att_ref, o_ref, st_ref) = refs[: len(deltas)], refs[len(deltas) :]
    more_kernel(deltas, z_ref, where_ref, q_ref, oin_ref, stin_ref, *slots, o_ref, st_ref)
    heads = range(q_ref.shape[1] // HEAD_DIM)

    def step(j, carry):
        rows = pl.ds(pl.multiple_of(j * BLOCK, BLOCK), BLOCK)
        for h in heads:
            kcol = pl.ds(h * HEAD_DIM, HEAD_DIM)
            total = st_ref[rows, pl.ds(len(heads) + h, 1)]
            att_ref[rows, kcol] = (o_ref[rows, kcol] / total).astype(BF16)
        return carry

    lax.fori_loop(0, q_ref.shape[0] // BLOCK, step, 0)


def cost(us):
    return pl.CostEstimate(flops=int(us * 1e9), bytes_accessed=4 * 2**20, transcendentals=0)


def local_part(z, where, first_id, all_blocks, q, kv_pad, ends, deltas, slots):
    tok, feat = q.shape
    return pl.pallas_call(
        lambda *refs: local_kernel(all_blocks, deltas, *refs),
        out_shape=(
            jax.ShapeDtypeStruct((tok, feat), F32),
            jax.ShapeDtypeStruct((tok, 128), F32),
        ),
        in_specs=[SM, SM, SM, VM, VM, VM, VM],
        out_specs=(VM, VM),
        compiler_params=pltpu.CompilerParams(vmem_limit_bytes=VMEM_LIMIT),
        cost_estimate=cost(25),
        name="local_part",
    )(z, where, first_id, q, kv_pad, ends, slots)


def more_part(z, where, q, o, st, deltas, slots):
    tok, feat = q.shape
    return pl.pallas_call(
        lambda *refs: more_kernel(deltas, *refs),
        out_shape=(
            jax.ShapeDtypeStruct((tok, feat), F32),
            jax.ShapeDtypeStruct((tok, 128), F32),
        ),
        in_specs=[SM, SM] + [VM] * (3 + len(slots)),
        out_specs=(VM, VM),
        compiler_params=pltpu.CompilerParams(vmem_limit_bytes=VMEM_LIMIT),
        cost_estimate=cost(12),
        name="more_part",
    )(z, where, q, o, st, *slots)


def final_part(z, where, q, o, st, deltas, slots):
    tok, feat = q.shape
    return pl.pallas_call(
        lambda *refs: final_kernel(deltas, *refs),
        out_shape=jax.ShapeDtypeStruct((tok, feat), BF16),
        in_specs=[SM, SM] + [VM] * (3 + len(slots)),
        out_specs=VM,
        scratch_shapes=[pltpu.VMEM((tok, feat), F32), pltpu.VMEM((tok, 128), F32)],
        compiler_params=pltpu.CompilerParams(vmem_limit_bytes=VMEM_LIMIT),
        cost_estimate=cost(6),
        name="final_part",
    )(z, where, q, o, st, *slots)


def pick(z, asked, sources, plan, shapes):
    def kernel(z_ref, asked_ref, *refs):
        src, out = refs[: len(sources)], refs[len(sources) : -3]
        held, in_sems, out_sems = refs[-3:]
        loads, stores = [], []
        for n, (o, position, s, lane, plane, owner) in enumerate(plan):
            if lane is None:
                block = jnp.where(z_ref[0] == 0, 0, sources[s].shape[0] - 1)
            else:
                row = lane * NZ + lax.rem(z_ref[0] + (plane + NZ), NZ)
                block = asked_ref[row, lax.rem(z_ref[0] + (owner + NZ), NZ)]
            loads.append(pltpu.make_async_copy(src[s].at[block], held.at[n], in_sems.at[n]))
            stores.append(pltpu.make_async_copy(held.at[n], out[o].at[position], out_sems.at[n]))
            loads[-1].start()
        for load, store in zip(loads, stores):
            load.wait()
            store.start()
        for store in stores:
            store.wait()

    block_shape = sources[0].shape[1:]
    return pl.pallas_call(
        kernel,
        out_shape=tuple(pltpu.HBM(shape + block_shape, BF16) for shape in shapes),
        in_specs=[SM, SM] + [HB] * len(sources),
        out_specs=tuple(HB for _ in shapes),
        scratch_shapes=[
            pltpu.VMEM((len(plan),) + block_shape, BF16),
            pltpu.SemaphoreType.DMA((len(plan),)),
            pltpu.SemaphoreType.DMA((len(plan),)),
        ],
        compiler_params=pltpu.CompilerParams(vmem_limit_bytes=8 * 1024 * 1024),
        cost_estimate=cost(3),
        name="pick",
    )(z, asked, *sources)


def project_kernel(tile, me_ref, a_ref, *refs):
    weights, (out_ref, w_ref, acat_ref, sems) = refs[:-4], refs[-4:]
    rows, feat = a_ref.shape[1:]
    cols = out_ref.shape[1]
    copies = []
    for n in range(cols // tile):
        top = 0
        span = pl.ds(n * tile, tile)
        for k, weight in enumerate(weights):
            part = pl.ds(top, weight.shape[0])
            copies.append(
                pltpu.make_async_copy(
                    weight.at[:, span], w_ref.at[part, span], sems.at[n * len(weights) + k]
                )
            )
            copies[-1].start()
            top += weight.shape[0]
    me = me_ref[0]
    for g in range(a_ref.shape[0]):
        acat_ref[:, pl.ds(g * feat, feat)] = a_ref[me ^ g]
    for n in range(cols // tile):
        for k in range(len(weights)):
            copies[n * len(weights) + k].wait()
        span = pl.ds(n * tile, tile)
        out_ref[:, span] = dot_nn(acat_ref[...], w_ref[:, span]).astype(BF16)


def project(me, a, weights, tile=1024):
    groups, rows, feat = a.shape
    cols = weights[0].shape[1]
    return pl.pallas_call(
        lambda *refs: project_kernel(tile, *refs),
        out_shape=jax.ShapeDtypeStruct((rows, cols), BF16),
        in_specs=[SM, VM] + [HB] * len(weights),
        out_specs=VM,
        scratch_shapes=[
            pltpu.VMEM((groups * feat, cols), BF16),
            pltpu.VMEM((rows, groups * feat), BF16),
            pltpu.SemaphoreType.DMA((cols // tile * len(weights),)),
        ],
        compiler_params=pltpu.CompilerParams(vmem_limit_bytes=VMEM_LIMIT),
        name="project",
    )(me, a, *weights)


def z_shift(x, by):
    return lax.ppermute(x, "z", [(i, (i + by) % NZ) for i in range(NZ)])


def lane_exchange(x):
    return lax.all_to_all(x, LANE, split_axis=0, concat_axis=0, tiled=True)


def wanted_blocks(rand_blocks, block_ids, all_blocks, blocks_dev):
    taken = [
        block_ids - 1,
        block_ids,
        block_ids + 1,
        jnp.zeros_like(block_ids),
        jnp.zeros_like(block_ids) + (all_blocks - 1),
    ]
    fresh = []
    for column in range(rand_blocks.shape[1]):
        chosen = rand_blocks[:, column]
        clash = reduce(jnp.logical_or, [chosen == other for other in taken])
        fresh.append(jnp.logical_not(clash))
        taken.append(chosen)
    fresh = jnp.stack(fresh, axis=1).reshape(-1)
    flat = rand_blocks.reshape(-1)
    entries = flat.shape[0]
    query = jnp.arange(entries, dtype=jnp.int32) // rand_blocks.shape[1]
    owners = jnp.arange(all_blocks // blocks_dev, dtype=jnp.int32)
    named = (flat // blocks_dev)[:, None] == owners[None, :]
    offset = jnp.sum(jnp.where(named, (flat % blocks_dev)[:, None], 0), axis=0)
    used = jnp.logical_and(named, fresh[:, None])
    where = jnp.sum(jnp.where(used, query[:, None] + 1, 0), axis=0) - 1
    return offset.astype(jnp.int32), where.astype(jnp.int32)


def tie(*arrays):
    return lax.optimization_barrier(arrays)


def body(queries, keys_values, rand_blocks, w_out):
    tok, feat = queries.shape
    blocks_dev = tok // BLOCK
    all_blocks = blocks_dev * LANES * NZ
    lanes = range(LANES)
    half = LANES // 2
    z = lax.axis_index("z")
    zs = z.reshape(1)
    first_id = lax.axis_index(SEQ) * blocks_dev

    kv = keys_values.reshape(blocks_dev, BLOCK, 2 * feat)

    up1, down1 = z_shift(kv, 1), z_shift(kv, -1)
    block_ids = first_id + jnp.arange(blocks_dev, dtype=jnp.int32)
    offset, where = wanted_blocks(rand_blocks, block_ids, all_blocks, blocks_dev)
    asked = jnp.broadcast_to(offset.reshape(LANES, 1, NZ), (LANES, NZ, NZ)).reshape(-1, NZ)
    asked = lax.all_to_all(asked, SEQ, split_axis=0, concat_axis=0, tiled=True)
    rows = w_out.shape[0] // 2
    own = [w_out[:rows], w_out[rows:]]
    ring = NXH * NXL
    low = lax.ppermute(own[0], XRING, [(i, (i + 1) % ring) for i in range(ring)])
    high = lax.ppermute(own[1], XRING, [(i, (i - 1) % ring) for i in range(ring)])
    edge = jnp.where(z == 0, kv[0], kv[blocks_dev - 1])
    turns = [(NZ * i + NZ - 1, NZ * i + NZ) for i in range(LANES - 1)]
    crossed = lax.ppermute(edge, SEQ, turns + [(b, a) for a, b in turns])
    up1, down1, asked, low, high, crossed, w_core = tie(
        up1, down1, asked, low, high, crossed, w_out
    )

    up2, down2 = z_shift(up1, 1), z_shift(down1, -1)
    plan = [(0, (lane, 0), 0, lane, 0, 0) for lane in lanes]
    plan += [(0, (lane, 1), 1, lane, 0, -1) for lane in lanes]
    plan += [(0, (lane, 2), 2, lane, 0, 1) for lane in lanes]
    plan += [(0, (lane, 3), 0, None, 0, 0) for lane in lanes]
    (c1,) = pick(zs, asked, [kv, up1, down1], plan, [(LANES, 4)])
    r1 = lane_exchange(c1)
    swap = [(0, 1), (1, 0)]
    others = [lax.ppermute(x, "core", swap) for x in (w_core, low, high)]
    before = jnp.where(z == 0, crossed, up1[blocks_dev - 1])
    after = jnp.where(z == NZ - 1, crossed, down1[0])
    kv_pad = jnp.concatenate([before, kv.reshape(tok, 2 * feat), after], axis=0)
    up2, down2, r1, kv_pad, *others = tie(up2, down2, r1, kv_pad, *others)
    weights = own + [others[0], low, high] + others[1:]

    plan = [(0, (lane, 0), 0, lane, 1, -2) for lane in lanes]
    plan += [(0, (lane, 1), 1, lane, -1, 2) for lane in lanes]
    plan += [(1, lane, 0, lane, 2, -2) for lane in lanes[:half]]
    plan += [(2, lane - half, 1, lane, -2, 2) for lane in lanes[half:]]
    plan += [(3, (lane, 0), 0, lane, 0, -2) for lane in lanes]
    plan += [(3, (lane, 1), 1, lane, 0, 2) for lane in lanes]
    c3, fu, fd, c2 = pick(
        zs, asked, [up2, down2], plan, [(LANES, 2), (half,), (half,), (LANES, 2)]
    )
    fu, fd = z_shift(fu, 1), z_shift(fd, -1)
    c3 = lane_exchange(c3)
    held = jnp.where(z == 0, r1[0, 3], r1[LANES - 1, 3])
    got = lax.ppermute(held, "z", [(0, 4), (7, 3)])
    held = jnp.where(jnp.logical_or(z == 4, z == 3), got, held)
    c2, c3, fu, fd = tie(c2, c3, fu, fd)
    r2 = lane_exchange(c2)
    fu, fd = z_shift(fu, 1), z_shift(fd, -1)
    r3u, r3d = z_shift(c3[:, 0], 1), z_shift(c3[:, 1], -1)
    got = lax.ppermute(held, "z", [(0, 2), (4, 6), (7, 5), (3, 1)])
    fresh = reduce(jnp.logical_or, [z == 2, z == 6, z == 5, z == 1])
    held = jnp.where(fresh, got, held)
    got = lax.ppermute(held, "z", [(i, i ^ 1) for i in range(NZ)])
    even = z % 2 == 0
    ends = jnp.concatenate([jnp.where(even, held, got), jnp.where(even, got, held)], axis=0)
    far = jnp.concatenate([fu, fd], axis=0)
    far, r2 = tie(far, r2)
    r4 = lane_exchange(far)

    def slots(x):
        return x.reshape(LANES, 1, BLOCK, 2 * feat)

    o, st = local_part(
        zs, where, first_id.reshape(1), all_blocks, queries, kv_pad, ends, (0, -1, 1), r1
    )
    o, st = more_part(
        zs, where, queries, o, st, [(-3,), (3,), (-2, 2)], [slots(r3u), slots(r3d), r2]
    )
    attended = final_part(zs, where, queries, o, st, [(4,)], [slots(r4)])

    heads = NXL * NC
    a = lax.all_to_all(
        attended.reshape(heads, tok // heads, feat), HEAD, split_axis=0, concat_axis=0, tiled=True
    )
    return project(lax.axis_index(HEAD).reshape(1), a, weights)


def solution(mesh):
    fine = Mesh(mesh.devices.reshape(NY, NXH, NZ, NXL, NC), ("y", "xh", "z", "xl", "core"))
    in_specs = (P(SEQ, HEAD), P(SEQ, None, HEAD), P(SEQ, None), P(HEAD, None))
    out_specs = P(SEQ + HEAD, None)
    return jax.shard_map(body, mesh=fine, in_specs=in_specs, out_specs=out_specs, check_vma=False)
```

```python
from functools import reduce

import jax
import jax.numpy as jnp
from jax import lax
from jax.experimental import pallas as pl
from jax.experimental.pallas import tpu as pltpu
from jax.sharding import Mesh, PartitionSpec as P

HEAD_DIM = 128
BLOCK = 64
NEG = -1e30
SEQ = ("y", "xh", "z")
LANE = ("y", "xh")
HEAD = ("xl", "core")
XRING = ("xh", "xl")
NY, NXH, NZ, NXL, NC = 4, 2, 8, 2, 2
LANES = NY * NXH
SCALE = HEAD_DIM ** (-0.5)
F32 = jnp.float32
BF16 = jnp.bfloat16
VMEM_LIMIT = 24 * 1024 * 1024
VM = pl.BlockSpec(memory_space=pltpu.VMEM)
SM = pl.BlockSpec(memory_space=pltpu.SMEM)
HB = pl.BlockSpec(memory_space=pltpu.HBM)


def dot_nt(a, b):
    return lax.dot_general(a, b, (((1,), (1,)), ((), ())), preferred_element_type=F32)


def dot_nn(a, b):
    return jnp.dot(a, b, preferred_element_type=F32)


def row_max(a):
    return jnp.max(a, axis=1, keepdims=True)


def row_sum(a):
    return jnp.sum(a, axis=1, keepdims=True)


def local_kernel(all_blocks, deltas, z_ref, where_ref, id_ref, *refs):
    q_ref, kv_ref, ends_ref, slots_ref, o_ref, st_ref = refs
    feat = q_ref.shape[1]
    heads = range(feat // HEAD_DIM)
    blocks = q_ref.shape[0] // BLOCK
    col = lax.broadcasted_iota(jnp.int32, (BLOCK, 3 * BLOCK), 1)
    shift = jnp.where(col < BLOCK, -1, jnp.where(col < 2 * BLOCK, 0, 1))
    end_col = lax.broadcasted_iota(jnp.int32, (BLOCK, 2 * BLOCK), 1)
    kcol = [pl.ds(h * HEAD_DIM, HEAD_DIM) for h in heads]
    vcol = [pl.ds(feat + h * HEAD_DIM, HEAD_DIM) for h in heads]

    def step(j, carry):
        block = id_ref[0] + j
        near = block + shift
        near_ok = jnp.logical_and(near >= 0, near < all_blocks)
        ends_ok = jnp.where(end_col < BLOCK, block, all_blocks - 1 - block) >= 2
        rows = pl.ds(pl.multiple_of(j * BLOCK, BLOCK), BLOCK)
        wrows = pl.ds(pl.multiple_of(j * BLOCK, BLOCK), 3 * BLOCK)
        q = [q_ref[rows, kcol[h]] for h in heads]
        sw = [dot_nt(q[h], kv_ref[wrows, kcol[h]]) for h in heads]
        se = [dot_nt(q[h], ends_ref[:, kcol[h]]) for h in heads]
        sw = [jnp.where(near_ok, x * SCALE, NEG) for x in sw]
        se = [jnp.where(ends_ok, x * SCALE, NEG) for x in se]
        peak = [jnp.maximum(row_max(sw[h]), row_max(se[h])) for h in heads]
        pw = [jnp.exp(sw[h] - peak[h]) for h in heads]
        pe = [jnp.exp(se[h] - peak[h]) for h in heads]
        total = [row_sum(pw[h]) + row_sum(pe[h]) for h in heads]
        out = [
            dot_nn(pw[h].astype(BF16), kv_ref[wrows, vcol[h]])
            + dot_nn(pe[h].astype(BF16), ends_ref[:, vcol[h]])
            for h in heads
        ]
        for h in heads:
            o_ref[rows, kcol[h]] = out[h]
            st_ref[rows, pl.ds(h, 1)] = peak[h]
            st_ref[rows, pl.ds(len(heads) + h, 1)] = total[h]
        return carry

    lax.fori_loop(0, blocks, step, 0)
    add_slots(deltas, z_ref, where_ref, slots_ref, q_ref, o_ref, st_ref)


def add_slots(deltas, z_ref, where_ref, slots_ref, q_ref, o_ref, st_ref):
    feat = q_ref.shape[1]
    heads = range(feat // HEAD_DIM)
    kcol = [pl.ds(h * HEAD_DIM, HEAD_DIM) for h in heads]
    vcol = [pl.ds(feat + h * HEAD_DIM, HEAD_DIM) for h in heads]

    def step(lane, carry):
        for s, delta in enumerate(deltas):
            j = where_ref[lane * NZ + lax.rem(z_ref[0] + (delta + NZ), NZ)]

            @pl.when(j >= 0)
            def _():
                rows = pl.ds(pl.multiple_of(j * BLOCK, BLOCK), BLOCK)
                sc = [
                    dot_nt(q_ref[rows, kcol[h]], slots_ref[lane, s, :, kcol[h]]) * SCALE
                    for h in heads
                ]
                old = [st_ref[rows, pl.ds(h, 1)] for h in heads]
                tot = [st_ref[rows, pl.ds(len(heads) + h, 1)] for h in heads]
                acc = [o_ref[rows, kcol[h]] for h in heads]
                peak = [jnp.maximum(old[h], row_max(sc[h])) for h in heads]
                fade = [jnp.exp(old[h] - peak[h]) for h in heads]
                p = [jnp.exp(sc[h] - peak[h]) for h in heads]
                tot = [tot[h] * fade[h] + row_sum(p[h]) for h in heads]
                out = [dot_nn(p[h].astype(BF16), slots_ref[lane, s, :, vcol[h]]) for h in heads]
                for h in heads:
                    o_ref[rows, kcol[h]] = acc[h] * fade[h] + out[h]
                    st_ref[rows, pl.ds(h, 1)] = peak[h]
                    st_ref[rows, pl.ds(len(heads) + h, 1)] = tot[h]

        return carry

    lax.fori_loop(0, LANES, step, 0)


def more_kernel(deltas, z_ref, where_ref, q_ref, oin_ref, stin_ref, *refs):
    slots, (o_ref, st_ref) = refs[: len(deltas)], refs[len(deltas) :]
    o_ref[...] = oin_ref[...]
    st_ref[...] = stin_ref[...]
    for which, ref in zip(deltas, slots):
        add_slots(which, z_ref, where_ref, ref, q_ref, o_ref, st_ref)


def final_kernel(deltas, me_ref, z_ref, where_ref, q_ref, oin_ref, stin_ref, *refs):
    groups = NXL * NC
    slots, outs = refs[: len(deltas)], refs[len(deltas) : len(deltas) + groups]
    o_ref, st_ref = refs[-2:]
    more_kernel(deltas, z_ref, where_ref, q_ref, oin_ref, stin_ref, *slots, o_ref, st_ref)
    heads = range(q_ref.shape[1] // HEAD_DIM)
    share = q_ref.shape[0] // groups

    def step(i, carry):
        to = pl.ds(pl.multiple_of(i * BLOCK, BLOCK), BLOCK)
        for k, out_ref in enumerate(outs):
            start = (me_ref[0] ^ k) * share + i * BLOCK
            rows = pl.ds(pl.multiple_of(start, BLOCK), BLOCK)
            for h in heads:
                kcol = pl.ds(h * HEAD_DIM, HEAD_DIM)
                total = st_ref[rows, pl.ds(len(heads) + h, 1)]
                out_ref[to, kcol] = (o_ref[rows, kcol] / total).astype(BF16)
        return carry

    lax.fori_loop(0, share // BLOCK, step, 0)


def cost(us):
    return pl.CostEstimate(flops=int(us * 1e9), bytes_accessed=4 * 2**20, transcendentals=0)


def local_part(z, where, first_id, all_blocks, q, kv_pad, ends, deltas, slots):
    tok, feat = q.shape
    return pl.pallas_call(
        lambda *refs: local_kernel(all_blocks, deltas, *refs),
        out_shape=(
            jax.ShapeDtypeStruct((tok, feat), F32),
            jax.ShapeDtypeStruct((tok, 128), F32),
        ),
        in_specs=[SM, SM, SM, VM, VM, VM, VM],
        out_specs=(VM, VM),
        compiler_params=pltpu.CompilerParams(vmem_limit_bytes=VMEM_LIMIT),
        cost_estimate=cost(25),
        name="local_part",
    )(z, where, first_id, q, kv_pad, ends, slots)


def more_part(z, where, q, o, st, deltas, slots):
    tok, feat = q.shape
    return pl.pallas_call(
        lambda *refs: more_kernel(deltas, *refs),
        out_shape=(
            jax.ShapeDtypeStruct((tok, feat), F32),
            jax.ShapeDtypeStruct((tok, 128), F32),
        ),
        in_specs=[SM, SM] + [VM] * (3 + len(slots)),
        out_specs=(VM, VM),
        compiler_params=pltpu.CompilerParams(vmem_limit_bytes=VMEM_LIMIT),
        cost_estimate=cost(12),
        name="more_part",
    )(z, where, q, o, st, *slots)


def final_part(me, z, where, q, o, st, deltas, slots):
    tok, feat = q.shape
    groups = NXL * NC
    return pl.pallas_call(
        lambda *refs: final_kernel(deltas, *refs),
        out_shape=tuple(jax.ShapeDtypeStruct((tok // groups, feat), BF16) for _ in range(groups)),
        in_specs=[SM, SM, SM] + [VM] * (3 + len(slots)),
        out_specs=tuple(VM for _ in range(groups)),
        scratch_shapes=[pltpu.VMEM((tok, feat), F32), pltpu.VMEM((tok, 128), F32)],
        compiler_params=pltpu.CompilerParams(vmem_limit_bytes=VMEM_LIMIT),
        cost_estimate=cost(6),
        name="final_part",
    )(me, z, where, q, o, st, *slots)


def pick(z, asked, sources, plan, shapes, us=3):
    def kernel(z_ref, asked_ref, *refs):
        src, out = refs[: len(sources)], refs[len(sources) : -3]
        held, in_sems, out_sems = refs[-3:]
        loads, stores = [], []
        for n, (o, position, s, lane, plane, owner) in enumerate(plan):
            if lane is None:
                block = jnp.where(z_ref[0] == 0, 0, sources[s].shape[0] - 1)
            else:
                row = lane * NZ + lax.rem(z_ref[0] + (plane + NZ), NZ)
                block = asked_ref[row, lax.rem(z_ref[0] + (owner + NZ), NZ)]
            loads.append(pltpu.make_async_copy(src[s].at[block], held.at[n], in_sems.at[n]))
            stores.append(pltpu.make_async_copy(held.at[n], out[o].at[position], out_sems.at[n]))
            loads[-1].start()
        for load, store in zip(loads, stores):
            load.wait()
            store.start()
        for store in stores:
            store.wait()

    block_shape = sources[0].shape[1:]
    return pl.pallas_call(
        kernel,
        out_shape=tuple(pltpu.HBM(shape + block_shape, BF16) for shape in shapes),
        in_specs=[SM, SM] + [HB] * len(sources),
        out_specs=tuple(HB for _ in shapes),
        scratch_shapes=[
            pltpu.VMEM((len(plan),) + block_shape, BF16),
            pltpu.SemaphoreType.DMA((len(plan),)),
            pltpu.SemaphoreType.DMA((len(plan),)),
        ],
        compiler_params=pltpu.CompilerParams(vmem_limit_bytes=8 * 1024 * 1024),
        cost_estimate=cost(us),
        name="pick",
    )(z, asked, *sources)


def project_kernel(tile, count, base, *refs):
    parts, weights = refs[:count], refs[count : -4 - base]
    out_ref, w_ref, a_ref, sems = refs[-4:]
    feat = parts[0].shape[1]
    cols = out_ref.shape[1]
    copies = []
    for n in range(cols // tile):
        top = 0
        span = pl.ds(n * tile, tile)
        for k, weight in enumerate(weights):
            part = pl.ds(top, weight.shape[0])
            copies.append(
                pltpu.make_async_copy(
                    weight.at[:, span], w_ref.at[part, span], sems.at[n * len(weights) + k]
                )
            )
            copies[-1].start()
            top += weight.shape[0]
    for g, part in enumerate(parts):
        a_ref[:, pl.ds(g * feat, feat)] = part[...]
    for n in range(cols // tile):
        for k in range(len(weights)):
            copies[n * len(weights) + k].wait()
        span = pl.ds(n * tile, tile)
        value = dot_nn(a_ref[...], w_ref[:, span])
        if base:
            value += refs[-5][:, span]
        out_ref[:, span] = value.astype(out_ref.dtype)


def project(parts, weights, base=None, tile=1024):
    rows, feat = parts[0].shape
    cols = weights[0].shape[1]
    bases = [] if base is None else [base]
    return pl.pallas_call(
        lambda *refs: project_kernel(tile, len(parts), len(bases), *refs),
        out_shape=jax.ShapeDtypeStruct((rows, cols), F32 if base is None else BF16),
        in_specs=[VM] * len(parts) + [HB] * len(weights) + [VM] * len(bases),
        out_specs=VM,
        scratch_shapes=[
            pltpu.VMEM((len(parts) * feat, cols), BF16),
            pltpu.VMEM((rows, len(parts) * feat), BF16),
            pltpu.SemaphoreType.DMA((cols // tile * len(weights),)),
        ],
        compiler_params=pltpu.CompilerParams(vmem_limit_bytes=VMEM_LIMIT),
        cost_estimate=cost(6),
        name="project",
    )(*parts, *weights, *bases)


def z_shift(x, by):
    return lax.ppermute(x, "z", [(i, (i + by) % NZ) for i in range(NZ)])


def lane_exchange(x):
    return lax.all_to_all(x, LANE, split_axis=0, concat_axis=0, tiled=True)


def wanted_blocks(rand_blocks, block_ids, all_blocks, blocks_dev):
    taken = [
        block_ids - 1,
        block_ids,
        block_ids + 1,
        jnp.zeros_like(block_ids),
        jnp.zeros_like(block_ids) + (all_blocks - 1),
    ]
    fresh = []
    for column in range(rand_blocks.shape[1]):
        chosen = rand_blocks[:, column]
        clash = reduce(jnp.logical_or, [chosen == other for other in taken])
        fresh.append(jnp.logical_not(clash))
        taken.append(chosen)
    fresh = jnp.stack(fresh, axis=1).reshape(-1)
    flat = rand_blocks.reshape(-1)
    entries = flat.shape[0]
    query = jnp.arange(entries, dtype=jnp.int32) // rand_blocks.shape[1]
    owners = jnp.arange(all_blocks // blocks_dev, dtype=jnp.int32)
    named = (flat // blocks_dev)[:, None] == owners[None, :]
    offset = jnp.sum(jnp.where(named, (flat % blocks_dev)[:, None], 0), axis=0)
    used = jnp.logical_and(named, fresh[:, None])
    where = jnp.sum(jnp.where(used, query[:, None] + 1, 0), axis=0) - 1
    return offset.astype(jnp.int32), where.astype(jnp.int32)


def tie(*arrays):
    return lax.optimization_barrier(arrays)


def body(queries, keys_values, rand_blocks, w_out):
    tok, feat = queries.shape
    blocks_dev = tok // BLOCK
    all_blocks = blocks_dev * LANES * NZ
    lanes = range(LANES)
    half = LANES // 2
    z = lax.axis_index("z")
    zs = z.reshape(1)
    first_id = lax.axis_index(SEQ) * blocks_dev

    kv = keys_values.reshape(blocks_dev, BLOCK, 2 * feat)

    up1, down1 = z_shift(kv, 1), z_shift(kv, -1)
    block_ids = first_id + jnp.arange(blocks_dev, dtype=jnp.int32)
    offset, where = wanted_blocks(rand_blocks, block_ids, all_blocks, blocks_dev)
    asked = jnp.broadcast_to(offset.reshape(LANES, 1, NZ), (LANES, NZ, NZ)).reshape(-1, NZ)
    asked = lax.all_to_all(asked, SEQ, split_axis=0, concat_axis=0, tiled=True)
    rows = w_out.shape[0] // 2
    own = [w_out[:rows], w_out[rows:]]
    ring = NXH * NXL
    low = lax.ppermute(own[0], XRING, [(i, (i + 1) % ring) for i in range(ring)])
    high = lax.ppermute(own[1], XRING, [(i, (i - 1) % ring) for i in range(ring)])
    edge = jnp.where(z == 0, kv[0], kv[blocks_dev - 1])
    turns = [(NZ * i + NZ - 1, NZ * i + NZ) for i in range(LANES - 1)]
    crossed = lax.ppermute(edge, SEQ, turns + [(b, a) for a, b in turns])
    up1, down1, asked, low, high, crossed, w_core = tie(
        up1, down1, asked, low, high, crossed, w_out
    )

    up2, down2 = z_shift(up1, 1), z_shift(down1, -1)
    plan = [(0, (lane, 0), 0, lane, 0, 0) for lane in lanes]
    plan += [(0, (lane, 1), 1, lane, 0, -1) for lane in lanes]
    plan += [(0, (lane, 2), 2, lane, 0, 1) for lane in lanes]
    plan += [(0, (lane, 3), 0, None, 0, 0) for lane in lanes]
    (c1,) = pick(zs, asked, [kv, up1, down1], plan, [(LANES, 4)])
    r1 = lane_exchange(c1)
    swap = [(0, 1), (1, 0)]
    others = [lax.ppermute(x, "core", swap) for x in (w_core, low, high)]
    before = jnp.where(z == 0, crossed, up1[blocks_dev - 1])
    after = jnp.where(z == NZ - 1, crossed, down1[0])
    kv_pad = jnp.concatenate([before, kv.reshape(tok, 2 * feat), after], axis=0)
    up2, down2, kv_pad, *others = tie(up2, down2, kv_pad, *others)
    weights = own + [others[0], low, high] + others[1:]

    plan = [(0, (lane, 0), 0, lane, 1, -2) for lane in lanes]
    plan += [(0, (lane, 1), 1, lane, -1, 2) for lane in lanes]
    plan += [(1, lane, 0, lane, 2, -2) for lane in lanes[:half]]
    plan += [(2, lane - half, 1, lane, -2, 2) for lane in lanes[half:]]
    plan += [(3, (lane, 0), 0, lane, 0, -2) for lane in lanes]
    plan += [(3, (lane, 1), 1, lane, 0, 2) for lane in lanes]
    c3, fu, fd, c2 = pick(
        zs, asked, [up2, down2], plan, [(LANES, 2), (half,), (half,), (LANES, 2)], 60
    )
    c3, r1 = tie(c3, r1)
    fu, fd = z_shift(fu, 1), z_shift(fd, -1)
    c3 = lane_exchange(c3)
    held = jnp.where(z == 0, r1[0, 3], r1[LANES - 1, 3])
    got = lax.ppermute(held, "z", [(0, 4), (7, 3)])
    held = jnp.where(jnp.logical_or(z == 4, z == 3), got, held)
    c2, c3, fu, fd = tie(c2, c3, fu, fd)
    r2 = lane_exchange(c2)
    fu, fd = z_shift(fu, 1), z_shift(fd, -1)
    r3u, r3d = z_shift(c3[:, 0], 1), z_shift(c3[:, 1], -1)
    got = lax.ppermute(held, "z", [(0, 2), (4, 6), (7, 5), (3, 1)])
    fresh = reduce(jnp.logical_or, [z == 2, z == 6, z == 5, z == 1])
    held = jnp.where(fresh, got, held)
    got = lax.ppermute(held, "z", [(i, i ^ 1) for i in range(NZ)])
    even = z % 2 == 0
    ends = jnp.concatenate([jnp.where(even, held, got), jnp.where(even, got, held)], axis=0)
    far = jnp.concatenate([fu, fd], axis=0)
    far, r2 = tie(far, r2)
    r4 = lane_exchange(far)

    def slots(x):
        return x.reshape(LANES, 1, BLOCK, 2 * feat)

    o, st = local_part(
        zs, where, first_id.reshape(1), all_blocks, queries, kv_pad, ends, (0, -1, 1), r1
    )
    o, st = more_part(
        zs, where, queries, o, st, [(-3,), (3,), (-2, 2)], [slots(r3u), slots(r3d), r2]
    )
    me = lax.axis_index(HEAD).reshape(1)
    mine, *away = final_part(me, zs, where, queries, o, st, [(4,)], [slots(r4)])

    heads = range(NXL * NC)
    far_x, far_xc = [lax.ppermute(away[k - 1], HEAD, [(h, h ^ k) for h in heads]) for k in (2, 3)]
    near = lax.ppermute(away[0], HEAD, [(h, h ^ 1) for h in heads])
    partial = project([mine, near], weights[:3])
    return project([far_x, far_xc], weights[3:], partial)


def solution(mesh):
    fine = Mesh(mesh.devices.reshape(NY, NXH, NZ, NXL, NC), ("y", "xh", "z", "xl", "core"))
    in_specs = (P(SEQ, HEAD), P(SEQ, None, HEAD), P(SEQ, None), P(HEAD, None))
    out_specs = P(SEQ + HEAD, None)
    return jax.shard_map(body, mesh=fine, in_specs=in_specs, out_specs=out_specs, check_vma=False)
```

```python
from functools import reduce

import jax
import jax.numpy as jnp
from jax import lax
from jax.experimental import pallas as pl
from jax.experimental.pallas import tpu as pltpu
from jax.sharding import Mesh, PartitionSpec as P

HEAD_DIM = 128
BLOCK = 64
NEG = -1e30
SEQ = ("y", "xh", "z")
LANE = ("y", "xh")
HEAD = ("xl", "core")
XRING = ("xh", "xl")
NY, NXH, NZ, NXL, NC = 4, 2, 8, 2, 2
LANES = NY * NXH
SCALE = HEAD_DIM ** (-0.5)
F32 = jnp.float32
BF16 = jnp.bfloat16
VMEM_LIMIT = 24 * 1024 * 1024
VM = pl.BlockSpec(memory_space=pltpu.VMEM)
SM = pl.BlockSpec(memory_space=pltpu.SMEM)
HB = pl.BlockSpec(memory_space=pltpu.HBM)


def dot_nt(a, b):
    return lax.dot_general(a, b, (((1,), (1,)), ((), ())), preferred_element_type=F32)


def dot_nn(a, b):
    return jnp.dot(a, b, preferred_element_type=F32)


def row_max(a):
    return jnp.max(a, axis=1, keepdims=True)


def row_sum(a):
    return jnp.sum(a, axis=1, keepdims=True)


def local_kernel(all_blocks, deltas, z_ref, where_ref, id_ref, *refs):
    q_ref, kv_ref, ends_ref, slots_ref, o_ref, st_ref = refs
    feat = q_ref.shape[1]
    heads = range(feat // HEAD_DIM)
    blocks = q_ref.shape[0] // BLOCK
    col = lax.broadcasted_iota(jnp.int32, (BLOCK, 3 * BLOCK), 1)
    shift = jnp.where(col < BLOCK, -1, jnp.where(col < 2 * BLOCK, 0, 1))
    end_col = lax.broadcasted_iota(jnp.int32, (BLOCK, 2 * BLOCK), 1)
    kcol = [pl.ds(h * HEAD_DIM, HEAD_DIM) for h in heads]
    vcol = [pl.ds(feat + h * HEAD_DIM, HEAD_DIM) for h in heads]

    def step(j, carry):
        block = id_ref[0] + j
        near = block + shift
        near_ok = jnp.logical_and(near >= 0, near < all_blocks)
        ends_ok = jnp.where(end_col < BLOCK, block, all_blocks - 1 - block) >= 2
        rows = pl.ds(pl.multiple_of(j * BLOCK, BLOCK), BLOCK)
        wrows = pl.ds(pl.multiple_of(j * BLOCK, BLOCK), 3 * BLOCK)
        q = [q_ref[rows, kcol[h]] for h in heads]
        sw = [dot_nt(q[h], kv_ref[wrows, kcol[h]]) for h in heads]
        se = [dot_nt(q[h], ends_ref[:, kcol[h]]) for h in heads]
        sw = [jnp.where(near_ok, x * SCALE, NEG) for x in sw]
        se = [jnp.where(ends_ok, x * SCALE, NEG) for x in se]
        peak = [jnp.maximum(row_max(sw[h]), row_max(se[h])) for h in heads]
        pw = [jnp.exp(sw[h] - peak[h]) for h in heads]
        pe = [jnp.exp(se[h] - peak[h]) for h in heads]
        total = [row_sum(pw[h]) + row_sum(pe[h]) for h in heads]
        out = [
            dot_nn(pw[h].astype(BF16), kv_ref[wrows, vcol[h]])
            + dot_nn(pe[h].astype(BF16), ends_ref[:, vcol[h]])
            for h in heads
        ]
        for h in heads:
            o_ref[rows, kcol[h]] = out[h]
            st_ref[rows, pl.ds(h, 1)] = peak[h]
            st_ref[rows, pl.ds(len(heads) + h, 1)] = total[h]
        return carry

    lax.fori_loop(0, blocks, step, 0)
    add_slots(deltas, z_ref, where_ref, slots_ref, q_ref, o_ref, st_ref)


def add_slots(deltas, z_ref, where_ref, slots_ref, q_ref, o_ref, st_ref):
    feat = q_ref.shape[1]
    heads = range(feat // HEAD_DIM)
    kcol = [pl.ds(h * HEAD_DIM, HEAD_DIM) for h in heads]
    vcol = [pl.ds(feat + h * HEAD_DIM, HEAD_DIM) for h in heads]

    def step(lane, carry):
        for s, delta in enumerate(deltas):
            j = where_ref[lane * NZ + lax.rem(z_ref[0] + (delta + NZ), NZ)]

            @pl.when(j >= 0)
            def _():
                rows = pl.ds(pl.multiple_of(j * BLOCK, BLOCK), BLOCK)
                sc = [
                    dot_nt(q_ref[rows, kcol[h]], slots_ref[lane, s, :, kcol[h]]) * SCALE
                    for h in heads
                ]
                old = [st_ref[rows, pl.ds(h, 1)] for h in heads]
                tot = [st_ref[rows, pl.ds(len(heads) + h, 1)] for h in heads]
                acc = [o_ref[rows, kcol[h]] for h in heads]
                peak = [jnp.maximum(old[h], row_max(sc[h])) for h in heads]
                fade = [jnp.exp(old[h] - peak[h]) for h in heads]
                p = [jnp.exp(sc[h] - peak[h]) for h in heads]
                tot = [tot[h] * fade[h] + row_sum(p[h]) for h in heads]
                out = [dot_nn(p[h].astype(BF16), slots_ref[lane, s, :, vcol[h]]) for h in heads]
                for h in heads:
                    o_ref[rows, kcol[h]] = acc[h] * fade[h] + out[h]
                    st_ref[rows, pl.ds(h, 1)] = peak[h]
                    st_ref[rows, pl.ds(len(heads) + h, 1)] = tot[h]

        return carry

    lax.fori_loop(0, LANES, step, 0)


def more_kernel(deltas, z_ref, where_ref, q_ref, oin_ref, stin_ref, *refs):
    slots, (o_ref, st_ref) = refs[: len(deltas)], refs[len(deltas) :]
    o_ref[...] = oin_ref[...]
    st_ref[...] = stin_ref[...]
    for which, ref in zip(deltas, slots):
        add_slots(which, z_ref, where_ref, ref, q_ref, o_ref, st_ref)


def final_kernel(deltas, me_ref, z_ref, where_ref, q_ref, oin_ref, stin_ref, *refs):
    groups = NXL * NC
    slots, outs = refs[: len(deltas)], refs[len(deltas) : len(deltas) + groups]
    o_ref, st_ref = refs[-2:]
    more_kernel(deltas, z_ref, where_ref, q_ref, oin_ref, stin_ref, *slots, o_ref, st_ref)
    heads = range(q_ref.shape[1] // HEAD_DIM)
    share = q_ref.shape[0] // groups

    def step(i, carry):
        to = pl.ds(pl.multiple_of(i * BLOCK, BLOCK), BLOCK)
        for k, out_ref in enumerate(outs):
            start = (me_ref[0] ^ k) * share + i * BLOCK
            rows = pl.ds(pl.multiple_of(start, BLOCK), BLOCK)
            for h in heads:
                kcol = pl.ds(h * HEAD_DIM, HEAD_DIM)
                total = st_ref[rows, pl.ds(len(heads) + h, 1)]
                out_ref[to, kcol] = (o_ref[rows, kcol] / total).astype(BF16)
        return carry

    lax.fori_loop(0, share // BLOCK, step, 0)


def cost(us):
    return pl.CostEstimate(flops=int(us * 1e9), bytes_accessed=4 * 2**20, transcendentals=0)


def local_part(z, where, first_id, all_blocks, q, kv_pad, ends, deltas, slots):
    tok, feat = q.shape
    return pl.pallas_call(
        lambda *refs: local_kernel(all_blocks, deltas, *refs),
        out_shape=(
            jax.ShapeDtypeStruct((tok, feat), F32),
            jax.ShapeDtypeStruct((tok, 128), F32),
        ),
        in_specs=[SM, SM, SM, VM, VM, VM, VM],
        out_specs=(VM, VM),
        compiler_params=pltpu.CompilerParams(vmem_limit_bytes=VMEM_LIMIT),
        cost_estimate=cost(25),
        name="local_part",
    )(z, where, first_id, q, kv_pad, ends, slots)


def more_part(z, where, q, o, st, deltas, slots):
    tok, feat = q.shape
    return pl.pallas_call(
        lambda *refs: more_kernel(deltas, *refs),
        out_shape=(
            jax.ShapeDtypeStruct((tok, feat), F32),
            jax.ShapeDtypeStruct((tok, 128), F32),
        ),
        in_specs=[SM, SM] + [VM] * (3 + len(slots)),
        out_specs=(VM, VM),
        compiler_params=pltpu.CompilerParams(vmem_limit_bytes=VMEM_LIMIT),
        cost_estimate=cost(12),
        name="more_part",
    )(z, where, q, o, st, *slots)


def final_part(me, z, where, q, o, st, deltas, slots):
    tok, feat = q.shape
    groups = NXL * NC
    return pl.pallas_call(
        lambda *refs: final_kernel(deltas, *refs),
        out_shape=tuple(jax.ShapeDtypeStruct((tok // groups, feat), BF16) for _ in range(groups)),
        in_specs=[SM, SM, SM] + [VM] * (3 + len(slots)),
        out_specs=tuple(VM for _ in range(groups)),
        scratch_shapes=[pltpu.VMEM((tok, feat), F32), pltpu.VMEM((tok, 128), F32)],
        compiler_params=pltpu.CompilerParams(vmem_limit_bytes=VMEM_LIMIT),
        cost_estimate=cost(6),
        name="final_part",
    )(me, z, where, q, o, st, *slots)


def pick(z, asked, sources, plan, shapes, us=3):
    def kernel(z_ref, asked_ref, *refs):
        src, out = refs[: len(sources)], refs[len(sources) : -3]
        held, in_sems, out_sems = refs[-3:]
        loads, stores = [], []
        for n, (o, position, s, lane, plane, owner) in enumerate(plan):
            row = lane * NZ + lax.rem(z_ref[0] + (plane + NZ), NZ)
            block = asked_ref[row, lax.rem(z_ref[0] + (owner + NZ), NZ)]
            loads.append(pltpu.make_async_copy(src[s].at[block], held.at[n], in_sems.at[n]))
            stores.append(pltpu.make_async_copy(held.at[n], out[o].at[position], out_sems.at[n]))
            loads[-1].start()
        for load, store in zip(loads, stores):
            load.wait()
            store.start()
        for store in stores:
            store.wait()

    block_shape = sources[0].shape[1:]
    return pl.pallas_call(
        kernel,
        out_shape=tuple(pltpu.HBM(shape + block_shape, BF16) for shape in shapes),
        in_specs=[SM, SM] + [HB] * len(sources),
        out_specs=tuple(HB for _ in shapes),
        scratch_shapes=[
            pltpu.VMEM((len(plan),) + block_shape, BF16),
            pltpu.SemaphoreType.DMA((len(plan),)),
            pltpu.SemaphoreType.DMA((len(plan),)),
        ],
        compiler_params=pltpu.CompilerParams(vmem_limit_bytes=8 * 1024 * 1024),
        cost_estimate=cost(us),
        name="pick",
    )(z, asked, *sources)


def project_kernel(tile, count, base, *refs):
    parts, weights = refs[:count], refs[count : -4 - base]
    out_ref, w_ref, a_ref, sems = refs[-4:]
    feat = parts[0].shape[1]
    cols = out_ref.shape[1]
    copies = []
    for n in range(cols // tile):
        top = 0
        span = pl.ds(n * tile, tile)
        for k, weight in enumerate(weights):
            part = pl.ds(top, weight.shape[0])
            copies.append(
                pltpu.make_async_copy(
                    weight.at[:, span], w_ref.at[part, span], sems.at[n * len(weights) + k]
                )
            )
            copies[-1].start()
            top += weight.shape[0]
    for g, part in enumerate(parts):
        a_ref[:, pl.ds(g * feat, feat)] = part[...]
    for n in range(cols // tile):
        for k in range(len(weights)):
            copies[n * len(weights) + k].wait()
        span = pl.ds(n * tile, tile)
        value = dot_nn(a_ref[...], w_ref[:, span])
        if base:
            value += refs[-5][:, span]
        out_ref[:, span] = value.astype(out_ref.dtype)


def project(parts, weights, base=None, tile=1024):
    rows, feat = parts[0].shape
    cols = weights[0].shape[1]
    bases = [] if base is None else [base]
    return pl.pallas_call(
        lambda *refs: project_kernel(tile, len(parts), len(bases), *refs),
        out_shape=jax.ShapeDtypeStruct((rows, cols), F32 if base is None else BF16),
        in_specs=[VM] * len(parts) + [HB] * len(weights) + [VM] * len(bases),
        out_specs=VM,
        scratch_shapes=[
            pltpu.VMEM((len(parts) * feat, cols), BF16),
            pltpu.VMEM((rows, len(parts) * feat), BF16),
            pltpu.SemaphoreType.DMA((cols // tile * len(weights),)),
        ],
        compiler_params=pltpu.CompilerParams(vmem_limit_bytes=VMEM_LIMIT),
        cost_estimate=cost(6),
        name="project",
    )(*parts, *weights, *bases)


def z_shift(x, by):
    return lax.ppermute(x, "z", [(i, (i + by) % NZ) for i in range(NZ)])


def lane_exchange(x):
    return lax.all_to_all(x, LANE, split_axis=0, concat_axis=0, tiled=True)


def spread_lanes(edge, z):
    lane = lax.axis_index(LANE)
    steps = ([(0, 4)], [(0, 2), (4, 6)], [(0, 1), (2, 3), (4, 5), (6, 7)])
    held = edge
    for pairs in steps:
        other = [(LANES - 1 - a, LANES - 1 - b) for a, b in pairs]
        moves = [(a * NZ, b * NZ) for a, b in pairs]
        moves += [(a * NZ + NZ - 1, b * NZ + NZ - 1) for a, b in other]
        got = lax.ppermute(held, SEQ, moves)
        low = reduce(jnp.logical_or, [lane == b for _, b in pairs])
        high = reduce(jnp.logical_or, [lane == b for _, b in other])
        fresh = jnp.logical_or(
            jnp.logical_and(z == 0, low), jnp.logical_and(z == NZ - 1, high)
        )
        held = jnp.where(fresh, got, held)
    return held


def wanted_blocks(rand_blocks, block_ids, all_blocks, blocks_dev):
    taken = [
        block_ids - 1,
        block_ids,
        block_ids + 1,
        jnp.zeros_like(block_ids),
        jnp.zeros_like(block_ids) + (all_blocks - 1),
    ]
    fresh = []
    for column in range(rand_blocks.shape[1]):
        chosen = rand_blocks[:, column]
        clash = reduce(jnp.logical_or, [chosen == other for other in taken])
        fresh.append(jnp.logical_not(clash))
        taken.append(chosen)
    fresh = jnp.stack(fresh, axis=1).reshape(-1)
    flat = rand_blocks.reshape(-1)
    entries = flat.shape[0]
    query = jnp.arange(entries, dtype=jnp.int32) // rand_blocks.shape[1]
    owners = jnp.arange(all_blocks // blocks_dev, dtype=jnp.int32)
    named = (flat // blocks_dev)[:, None] == owners[None, :]
    offset = jnp.sum(jnp.where(named, (flat % blocks_dev)[:, None], 0), axis=0)
    used = jnp.logical_and(named, fresh[:, None])
    where = jnp.sum(jnp.where(used, query[:, None] + 1, 0), axis=0) - 1
    return offset.astype(jnp.int32), where.astype(jnp.int32)


def tie(*arrays):
    return lax.optimization_barrier(arrays)


def body(queries, keys_values, rand_blocks, w_out):
    tok, feat = queries.shape
    blocks_dev = tok // BLOCK
    all_blocks = blocks_dev * LANES * NZ
    lanes = range(LANES)
    half = LANES // 2
    z = lax.axis_index("z")
    zs = z.reshape(1)
    first_id = lax.axis_index(SEQ) * blocks_dev

    kv = keys_values.reshape(blocks_dev, BLOCK, 2 * feat)

    up1, down1 = z_shift(kv, 1), z_shift(kv, -1)
    block_ids = first_id + jnp.arange(blocks_dev, dtype=jnp.int32)
    offset, where = wanted_blocks(rand_blocks, block_ids, all_blocks, blocks_dev)
    asked = jnp.broadcast_to(offset.reshape(LANES, 1, NZ), (LANES, NZ, NZ)).reshape(-1, NZ)
    asked = lax.all_to_all(asked, SEQ, split_axis=0, concat_axis=0, tiled=True)
    edge = jnp.where(z == 0, kv[0], kv[blocks_dev - 1])
    held = spread_lanes(edge, z)
    w_first, held = tie(w_out, held)
    rows = w_out.shape[0] // 2
    own = [w_first[:rows], w_first[rows:]]
    ring = NXH * NXL
    low = lax.ppermute(own[0], XRING, [(i, (i + 1) % ring) for i in range(ring)])
    high = lax.ppermute(own[1], XRING, [(i, (i - 1) % ring) for i in range(ring)])
    turns = [(NZ * i + NZ - 1, NZ * i + NZ) for i in range(LANES - 1)]
    crossed = lax.ppermute(edge, SEQ, turns + [(b, a) for a, b in turns])
    up1, down1, asked, crossed = tie(up1, down1, asked, crossed)

    up2, down2 = z_shift(up1, 1), z_shift(down1, -1)
    plan = [(0, (lane, 0), 0, lane, 0, 0) for lane in lanes]
    plan += [(0, (lane, 1), 1, lane, 0, -1) for lane in lanes]
    plan += [(0, (lane, 2), 2, lane, 0, 1) for lane in lanes]
    (c1,) = pick(zs, asked, [kv, up1, down1], plan, [(LANES, 3)])
    c1, crossed, kv_late = tie(c1, crossed, kv)
    r1 = lane_exchange(c1)
    before = jnp.where(z == 0, crossed, up1[blocks_dev - 1])
    after = jnp.where(z == NZ - 1, crossed, down1[0])
    kv_pad = jnp.concatenate([before, kv_late.reshape(tok, 2 * feat), after], axis=0)
    up2, down2, kv_pad, w_core, low, high = tie(up2, down2, kv_pad, w_out, low, high)

    plan = [(0, (lane, 0), 0, lane, 1, -2) for lane in lanes]
    plan += [(0, (lane, 1), 1, lane, -1, 2) for lane in lanes]
    plan += [(1, lane, 0, lane, 2, -2) for lane in lanes[:half]]
    plan += [(2, lane - half, 1, lane, -2, 2) for lane in lanes[half:]]
    plan += [(3, (lane, 0), 0, lane, 0, -2) for lane in lanes]
    plan += [(3, (lane, 1), 1, lane, 0, 2) for lane in lanes]
    c3, fu, fd, c2 = pick(
        zs, asked, [up2, down2], plan, [(LANES, 2), (half,), (half,), (LANES, 2)], 60
    )
    c3, r1 = tie(c3, r1)
    fu, fd = z_shift(fu, 1), z_shift(fd, -1)
    c3 = lane_exchange(c3)
    got = lax.ppermute(held, "z", [(0, 4), (7, 3)])
    held = jnp.where(jnp.logical_or(z == 4, z == 3), got, held)
    swap = [(0, 1), (1, 0)]
    others = [lax.ppermute(x, "core", swap) for x in (w_core, low, high)]
    c2, c3, fu, fd = tie(c2, c3, fu, fd)
    r2 = lane_exchange(c2)
    fu, fd = z_shift(fu, 1), z_shift(fd, -1)
    r3u, r3d = z_shift(c3[:, 0], 1), z_shift(c3[:, 1], -1)
    got = lax.ppermute(held, "z", [(0, 2), (4, 6), (7, 5), (3, 1)])
    fresh = reduce(jnp.logical_or, [z == 2, z == 6, z == 5, z == 1])
    held = jnp.where(fresh, got, held)
    got = lax.ppermute(held, "z", [(i, i ^ 1) for i in range(NZ)])
    even = z % 2 == 0
    ends = jnp.concatenate([jnp.where(even, held, got), jnp.where(even, got, held)], axis=0)
    far = jnp.concatenate([fu, fd], axis=0)
    far, r2, *others = tie(far, r2, *others)
    weights = own + [others[0], low, high] + others[1:]
    r4 = lane_exchange(far)

    def slots(x):
        return x.reshape(LANES, 1, BLOCK, 2 * feat)

    o, st = local_part(
        zs, where, first_id.reshape(1), all_blocks, queries, kv_pad, ends, (0, -1, 1), r1
    )
    o, st = more_part(
        zs, where, queries, o, st, [(-3,), (3,), (-2, 2)], [slots(r3u), slots(r3d), r2]
    )
    me = lax.axis_index(HEAD).reshape(1)
    mine, *away = final_part(me, zs, where, queries, o, st, [(4,)], [slots(r4)])

    heads = range(NXL * NC)
    far_x, far_xc = [lax.ppermute(away[k - 1], HEAD, [(h, h ^ k) for h in heads]) for k in (2, 3)]
    near = lax.ppermute(away[0], HEAD, [(h, h ^ 1) for h in heads])
    partial = project([mine, near], weights[:3])
    return project([far_x, far_xc], weights[3:], partial)


def solution(mesh):
    fine = Mesh(mesh.devices.reshape(NY, NXH, NZ, NXL, NC), ("y", "xh", "z", "xl", "core"))
    in_specs = (P(SEQ, HEAD), P(SEQ, None, HEAD), P(SEQ, None), P(HEAD, None))
    out_specs = P(SEQ + HEAD, None)
    return jax.shard_map(body, mesh=fine, in_specs=in_specs, out_specs=out_specs, check_vma=False)
```

```python
from functools import reduce

import jax
import jax.numpy as jnp
from jax import lax
from jax.experimental import pallas as pl
from jax.experimental.pallas import tpu as pltpu
from jax.sharding import Mesh, PartitionSpec as P

HEAD_DIM = 128
BLOCK = 64
NEG = -1e30
SEQ = ("y", "xh", "z")
LANE = ("y", "xh")
HEAD = ("xl", "core")
XRING = ("xh", "xl")
NY, NXH, NZ, NXL, NC = 4, 2, 8, 2, 2
LANES = NY * NXH
SCALE = HEAD_DIM ** (-0.5)
F32 = jnp.float32
BF16 = jnp.bfloat16
VMEM_LIMIT = 24 * 1024 * 1024
VM = pl.BlockSpec(memory_space=pltpu.VMEM)
SM = pl.BlockSpec(memory_space=pltpu.SMEM)
HB = pl.BlockSpec(memory_space=pltpu.HBM)


def dot_nt(a, b):
    return lax.dot_general(a, b, (((1,), (1,)), ((), ())), preferred_element_type=F32)


def dot_nn(a, b):
    return jnp.dot(a, b, preferred_element_type=F32)


def row_max(a):
    return jnp.max(a, axis=1, keepdims=True)


def row_sum(a):
    return jnp.sum(a, axis=1, keepdims=True)


def local_kernel(all_blocks, deltas, z_ref, where_ref, id_ref, *refs):
    q_ref, kv_ref, ends_ref, slots_ref, o_ref, st_ref = refs
    feat = q_ref.shape[1]
    heads = range(feat // HEAD_DIM)
    blocks = q_ref.shape[0] // BLOCK
    col = lax.broadcasted_iota(jnp.int32, (BLOCK, 3 * BLOCK), 1)
    shift = jnp.where(col < BLOCK, -1, jnp.where(col < 2 * BLOCK, 0, 1))
    end_col = lax.broadcasted_iota(jnp.int32, (BLOCK, 2 * BLOCK), 1)
    kcol = [pl.ds(h * HEAD_DIM, HEAD_DIM) for h in heads]
    vcol = [pl.ds(feat + h * HEAD_DIM, HEAD_DIM) for h in heads]

    def step(j, carry):
        block = id_ref[0] + j
        near = block + shift
        near_ok = jnp.logical_and(near >= 0, near < all_blocks)
        ends_ok = jnp.where(end_col < BLOCK, block, all_blocks - 1 - block) >= 2
        rows = pl.ds(pl.multiple_of(j * BLOCK, BLOCK), BLOCK)
        wrows = pl.ds(pl.multiple_of(j * BLOCK, BLOCK), 3 * BLOCK)
        q = [q_ref[rows, kcol[h]] for h in heads]
        sw = [dot_nt(q[h], kv_ref[wrows, kcol[h]]) for h in heads]
        se = [dot_nt(q[h], ends_ref[:, kcol[h]]) for h in heads]
        sw = [jnp.where(near_ok, x * SCALE, NEG) for x in sw]
        se = [jnp.where(ends_ok, x * SCALE, NEG) for x in se]
        peak = [jnp.maximum(row_max(sw[h]), row_max(se[h])) for h in heads]
        pw = [jnp.exp(sw[h] - peak[h]) for h in heads]
        pe = [jnp.exp(se[h] - peak[h]) for h in heads]
        total = [row_sum(pw[h]) + row_sum(pe[h]) for h in heads]
        out = [
            dot_nn(pw[h].astype(BF16), kv_ref[wrows, vcol[h]])
            + dot_nn(pe[h].astype(BF16), ends_ref[:, vcol[h]])
            for h in heads
        ]
        for h in heads:
            o_ref[rows, kcol[h]] = out[h]
            st_ref[rows, pl.ds(h, 1)] = peak[h]
            st_ref[rows, pl.ds(len(heads) + h, 1)] = total[h]
        return carry

    lax.fori_loop(0, blocks, step, 0)
    add_slots(deltas, z_ref, where_ref, slots_ref, q_ref, o_ref, st_ref)


def add_slots(deltas, z_ref, where_ref, slots_ref, q_ref, o_ref, st_ref):
    feat = q_ref.shape[1]
    heads = range(feat // HEAD_DIM)
    kcol = [pl.ds(h * HEAD_DIM, HEAD_DIM) for h in heads]
    vcol = [pl.ds(feat + h * HEAD_DIM, HEAD_DIM) for h in heads]

    def step(lane, carry):
        for s, delta in enumerate(deltas):
            j = where_ref[lane * NZ + lax.rem(z_ref[0] + (delta + NZ), NZ)]

            @pl.when(j >= 0)
            def _():
                rows = pl.ds(pl.multiple_of(j * BLOCK, BLOCK), BLOCK)
                sc = [
                    dot_nt(q_ref[rows, kcol[h]], slots_ref[lane, s, :, kcol[h]]) * SCALE
                    for h in heads
                ]
                old = [st_ref[rows, pl.ds(h, 1)] for h in heads]
                tot = [st_ref[rows, pl.ds(len(heads) + h, 1)] for h in heads]
                acc = [o_ref[rows, kcol[h]] for h in heads]
                peak = [jnp.maximum(old[h], row_max(sc[h])) for h in heads]
                fade = [jnp.exp(old[h] - peak[h]) for h in heads]
                p = [jnp.exp(sc[h] - peak[h]) for h in heads]
                tot = [tot[h] * fade[h] + row_sum(p[h]) for h in heads]
                out = [dot_nn(p[h].astype(BF16), slots_ref[lane, s, :, vcol[h]]) for h in heads]
                for h in heads:
                    o_ref[rows, kcol[h]] = acc[h] * fade[h] + out[h]
                    st_ref[rows, pl.ds(h, 1)] = peak[h]
                    st_ref[rows, pl.ds(len(heads) + h, 1)] = tot[h]

        return carry

    lax.fori_loop(0, LANES, step, 0)


def more_kernel(deltas, z_ref, where_ref, q_ref, oin_ref, stin_ref, *refs):
    slots, (o_ref, st_ref) = refs[: len(deltas)], refs[len(deltas) :]
    o_ref[...] = oin_ref[...]
    st_ref[...] = stin_ref[...]
    for which, ref in zip(deltas, slots):
        add_slots(which, z_ref, where_ref, ref, q_ref, o_ref, st_ref)


def final_kernel(deltas, me_ref, z_ref, where_ref, q_ref, oin_ref, stin_ref, *refs):
    groups = NXL * NC
    slots, outs = refs[: len(deltas)], refs[len(deltas) : len(deltas) + groups]
    o_ref, st_ref = refs[-2:]
    more_kernel(deltas, z_ref, where_ref, q_ref, oin_ref, stin_ref, *slots, o_ref, st_ref)
    heads = range(q_ref.shape[1] // HEAD_DIM)
    share = q_ref.shape[0] // groups

    def step(i, carry):
        to = pl.ds(pl.multiple_of(i * BLOCK, BLOCK), BLOCK)
        for k, out_ref in enumerate(outs):
            start = (me_ref[0] ^ k) * share + i * BLOCK
            rows = pl.ds(pl.multiple_of(start, BLOCK), BLOCK)
            for h in heads:
                kcol = pl.ds(h * HEAD_DIM, HEAD_DIM)
                total = st_ref[rows, pl.ds(len(heads) + h, 1)]
                out_ref[to, kcol] = (o_ref[rows, kcol] / total).astype(BF16)
        return carry

    lax.fori_loop(0, share // BLOCK, step, 0)


def cost(us):
    return pl.CostEstimate(flops=int(us * 1e9), bytes_accessed=4 * 2**20, transcendentals=0)


def local_part(z, where, first_id, all_blocks, q, kv_pad, ends, deltas, slots):
    tok, feat = q.shape
    return pl.pallas_call(
        lambda *refs: local_kernel(all_blocks, deltas, *refs),
        out_shape=(
            jax.ShapeDtypeStruct((tok, feat), F32),
            jax.ShapeDtypeStruct((tok, 128), F32),
        ),
        in_specs=[SM, SM, SM, VM, VM, VM, VM],
        out_specs=(VM, VM),
        compiler_params=pltpu.CompilerParams(vmem_limit_bytes=VMEM_LIMIT),
        cost_estimate=cost(25),
        name="local_part",
    )(z, where, first_id, q, kv_pad, ends, slots)


def more_part(z, where, q, o, st, deltas, slots):
    tok, feat = q.shape
    return pl.pallas_call(
        lambda *refs: more_kernel(deltas, *refs),
        out_shape=(
            jax.ShapeDtypeStruct((tok, feat), F32),
            jax.ShapeDtypeStruct((tok, 128), F32),
        ),
        in_specs=[SM, SM] + [VM] * (3 + len(slots)),
        out_specs=(VM, VM),
        compiler_params=pltpu.CompilerParams(vmem_limit_bytes=VMEM_LIMIT),
        cost_estimate=cost(12),
        name="more_part",
    )(z, where, q, o, st, *slots)


def final_part(me, z, where, q, o, st, deltas, slots):
    tok, feat = q.shape
    groups = NXL * NC
    return pl.pallas_call(
        lambda *refs: final_kernel(deltas, *refs),
        out_shape=tuple(jax.ShapeDtypeStruct((tok // groups, feat), BF16) for _ in range(groups)),
        in_specs=[SM, SM, SM] + [VM] * (3 + len(slots)),
        out_specs=tuple(VM for _ in range(groups)),
        scratch_shapes=[pltpu.VMEM((tok, feat), F32), pltpu.VMEM((tok, 128), F32)],
        compiler_params=pltpu.CompilerParams(vmem_limit_bytes=VMEM_LIMIT),
        cost_estimate=cost(6),
        name="final_part",
    )(me, z, where, q, o, st, *slots)


def pick(z, asked, sources, plan, shapes, us=3):
    def kernel(z_ref, asked_ref, *refs):
        src, out = refs[: len(sources)], refs[len(sources) : -3]
        held, in_sems, out_sems = refs[-3:]
        loads, stores = [], []
        for n, (o, position, s, lane, plane, owner) in enumerate(plan):
            row = lane * NZ + lax.rem(z_ref[0] + (plane + NZ), NZ)
            block = asked_ref[row, lax.rem(z_ref[0] + (owner + NZ), NZ)]
            loads.append(pltpu.make_async_copy(src[s].at[block], held.at[n], in_sems.at[n]))
            stores.append(pltpu.make_async_copy(held.at[n], out[o].at[position], out_sems.at[n]))
            loads[-1].start()
        for load, store in zip(loads, stores):
            load.wait()
            store.start()
        for store in stores:
            store.wait()

    block_shape = sources[0].shape[1:]
    return pl.pallas_call(
        kernel,
        out_shape=tuple(pltpu.HBM(shape + block_shape, BF16) for shape in shapes),
        in_specs=[SM, SM] + [HB] * len(sources),
        out_specs=tuple(HB for _ in shapes),
        scratch_shapes=[
            pltpu.VMEM((len(plan),) + block_shape, BF16),
            pltpu.SemaphoreType.DMA((len(plan),)),
            pltpu.SemaphoreType.DMA((len(plan),)),
        ],
        compiler_params=pltpu.CompilerParams(vmem_limit_bytes=8 * 1024 * 1024),
        cost_estimate=cost(us),
        name="pick",
    )(z, asked, *sources)


def project_kernel(tile, count, base, *refs):
    parts, weights = refs[:count], refs[count : -4 - base]
    out_ref, w_ref, a_ref, sems = refs[-4:]
    feat = parts[0].shape[1]
    cols = out_ref.shape[1]
    copies = []
    for n in range(cols // tile):
        top = 0
        span = pl.ds(n * tile, tile)
        for k, weight in enumerate(weights):
            part = pl.ds(top, weight.shape[0])
            copies.append(
                pltpu.make_async_copy(
                    weight.at[:, span], w_ref.at[part, span], sems.at[n * len(weights) + k]
                )
            )
            copies[-1].start()
            top += weight.shape[0]
    for g, part in enumerate(parts):
        a_ref[:, pl.ds(g * feat, feat)] = part[...]
    for n in range(cols // tile):
        for k in range(len(weights)):
            copies[n * len(weights) + k].wait()
        span = pl.ds(n * tile, tile)
        value = dot_nn(a_ref[...], w_ref[:, span])
        if base:
            value += refs[-5][:, span]
        out_ref[:, span] = value.astype(out_ref.dtype)


def project(parts, weights, base=None, tile=1024):
    rows, feat = parts[0].shape
    cols = weights[0].shape[1]
    bases = [] if base is None else [base]
    return pl.pallas_call(
        lambda *refs: project_kernel(tile, len(parts), len(bases), *refs),
        out_shape=jax.ShapeDtypeStruct((rows, cols), F32 if base is None else BF16),
        in_specs=[VM] * len(parts) + [HB] * len(weights) + [VM] * len(bases),
        out_specs=VM,
        scratch_shapes=[
            pltpu.VMEM((len(parts) * feat, cols), BF16),
            pltpu.VMEM((rows, len(parts) * feat), BF16),
            pltpu.SemaphoreType.DMA((cols // tile * len(weights),)),
        ],
        compiler_params=pltpu.CompilerParams(vmem_limit_bytes=VMEM_LIMIT),
        cost_estimate=cost(6),
        name="project",
    )(*parts, *weights, *bases)


def z_shift(x, by):
    return lax.ppermute(x, "z", [(i, (i + by) % NZ) for i in range(NZ)])


def lane_exchange(x):
    return lax.all_to_all(x, LANE, split_axis=0, concat_axis=0, tiled=True)


def spread_lanes(edge, z):
    lane = lax.axis_index(LANE)
    steps = ([(0, 4)], [(0, 2), (4, 6)], [(0, 1), (2, 3), (4, 5), (6, 7)])
    held = edge
    for pairs in steps:
        other = [(LANES - 1 - a, LANES - 1 - b) for a, b in pairs]
        moves = [(a * NZ, b * NZ) for a, b in pairs]
        moves += [(a * NZ + NZ - 1, b * NZ + NZ - 1) for a, b in other]
        got = lax.ppermute(held, SEQ, moves)
        low = reduce(jnp.logical_or, [lane == b for _, b in pairs])
        high = reduce(jnp.logical_or, [lane == b for _, b in other])
        fresh = jnp.logical_or(
            jnp.logical_and(z == 0, low), jnp.logical_and(z == NZ - 1, high)
        )
        held = jnp.where(fresh, got, held)
    return held


def wanted_blocks(rand_blocks, block_ids, all_blocks, blocks_dev):
    taken = [
        block_ids - 1,
        block_ids,
        block_ids + 1,
        jnp.zeros_like(block_ids),
        jnp.zeros_like(block_ids) + (all_blocks - 1),
    ]
    fresh = []
    for column in range(rand_blocks.shape[1]):
        chosen = rand_blocks[:, column]
        clash = reduce(jnp.logical_or, [chosen == other for other in taken])
        fresh.append(jnp.logical_not(clash))
        taken.append(chosen)
    fresh = jnp.stack(fresh, axis=1).reshape(-1)
    flat = rand_blocks.reshape(-1)
    entries = flat.shape[0]
    query = jnp.arange(entries, dtype=jnp.int32) // rand_blocks.shape[1]
    owners = jnp.arange(all_blocks // blocks_dev, dtype=jnp.int32)
    named = (flat // blocks_dev)[:, None] == owners[None, :]
    offset = jnp.sum(jnp.where(named, (flat % blocks_dev)[:, None], 0), axis=0)
    used = jnp.logical_and(named, fresh[:, None])
    where = jnp.sum(jnp.where(used, query[:, None] + 1, 0), axis=0) - 1
    return offset.astype(jnp.int32), where.astype(jnp.int32)


def tie(*arrays):
    return lax.optimization_barrier(arrays)


def body(queries, keys_values, rand_blocks, w_out):
    tok, feat = queries.shape
    blocks_dev = tok // BLOCK
    all_blocks = blocks_dev * LANES * NZ
    lanes = range(LANES)
    half = LANES // 2
    z = lax.axis_index("z")
    zs = z.reshape(1)
    first_id = lax.axis_index(SEQ) * blocks_dev

    kv = keys_values.reshape(blocks_dev, BLOCK, 2 * feat)

    up1, down1 = z_shift(kv, 1), z_shift(kv, -1)
    block_ids = first_id + jnp.arange(blocks_dev, dtype=jnp.int32)
    offset, where = wanted_blocks(rand_blocks, block_ids, all_blocks, blocks_dev)
    asked = jnp.broadcast_to(offset.reshape(LANES, 1, NZ), (LANES, NZ, NZ)).reshape(-1, NZ)
    asked = lax.all_to_all(asked, SEQ, split_axis=0, concat_axis=0, tiled=True)
    edge = jnp.where(z == 0, kv[0], kv[blocks_dev - 1])
    held = spread_lanes(edge, z)
    w_first, held = tie(w_out, held)
    rows = w_out.shape[0] // 2
    own = [w_first[:rows], w_first[rows:]]
    ring = NXH * NXL
    low = lax.ppermute(own[0], XRING, [(i, (i + 1) % ring) for i in range(ring)])
    high = lax.ppermute(own[1], XRING, [(i, (i - 1) % ring) for i in range(ring)])
    turns = [(NZ * i + NZ - 1, NZ * i + NZ) for i in range(LANES - 1)]
    crossed = lax.ppermute(edge, SEQ, turns + [(b, a) for a, b in turns])
    up1, down1, asked, crossed = tie(up1, down1, asked, crossed)

    up2, down2 = z_shift(up1, 1), z_shift(down1, -1)
    plan = [(0, (lane, 0), 0, lane, 0, 0) for lane in lanes]
    plan += [(0, (lane, 1), 1, lane, 0, -1) for lane in lanes]
    plan += [(0, (lane, 2), 2, lane, 0, 1) for lane in lanes]
    (c1,) = pick(zs, asked, [kv, up1, down1], plan, [(LANES, 3)])
    c1, crossed, kv_late = tie(c1, crossed, kv)
    r1 = lane_exchange(c1)
    before = jnp.where(z == 0, crossed, up1[blocks_dev - 1])
    after = jnp.where(z == NZ - 1, crossed, down1[0])
    kv_pad = jnp.concatenate([before, kv_late.reshape(tok, 2 * feat), after], axis=0)
    up2, down2, kv_pad, w_core, low, high = tie(up2, down2, kv_pad, w_out, low, high)

    plan = [(0, (lane, 0), 0, lane, 1, -2) for lane in lanes]
    plan += [(0, (lane, 1), 1, lane, -1, 2) for lane in lanes]
    plan += [(1, lane, 0, lane, 2, -2) for lane in lanes[:half]]
    plan += [(2, lane - half, 1, lane, -2, 2) for lane in lanes[half:]]
    plan += [(3, (lane, 0), 0, lane, 0, -2) for lane in lanes]
    plan += [(3, (lane, 1), 1, lane, 0, 2) for lane in lanes]
    c3, fu, fd, c2 = pick(
        zs, asked, [up2, down2], plan, [(LANES, 2), (half,), (half,), (LANES, 2)], 60
    )
    c3, r1 = tie(c3, r1)
    fu, fd = z_shift(fu, 1), z_shift(fd, -1)
    c3 = lane_exchange(c3)
    got = lax.ppermute(held, "z", [(0, 4), (7, 3)])
    held = jnp.where(jnp.logical_or(z == 4, z == 3), got, held)
    got = lax.ppermute(held, "z", [(0, 2), (4, 6), (7, 5), (3, 1)])
    fresh = reduce(jnp.logical_or, [z == 2, z == 6, z == 5, z == 1])
    held = jnp.where(fresh, got, held)
    got = lax.ppermute(held, "z", [(i, i ^ 1) for i in range(NZ)])
    even = z % 2 == 0
    ends = jnp.concatenate([jnp.where(even, held, got), jnp.where(even, got, held)], axis=0)
    c2, c3, fu, fd, ends = tie(c2, c3, fu, fd, ends)
    low, high, w_core, ends = tie(low, high, w_core, ends)
    swap = [(0, 1), (1, 0)]
    others = [lax.ppermute(x, "core", swap) for x in (w_core, low, high)]
    r2 = lane_exchange(c2)
    fu, fd = z_shift(fu, 1), z_shift(fd, -1)
    r3u, r3d = z_shift(c3[:, 0], 1), z_shift(c3[:, 1], -1)
    far = jnp.concatenate([fu, fd], axis=0)
    far, r2, *others = tie(far, r2, *others)
    weights = own + [others[0], low, high] + others[1:]
    r4 = lane_exchange(far)

    def slots(x):
        return x.reshape(LANES, 1, BLOCK, 2 * feat)

    o, st = local_part(
        zs, where, first_id.reshape(1), all_blocks, queries, kv_pad, ends, (0, -1, 1), r1
    )
    o, st = more_part(
        zs, where, queries, o, st, [(-3,), (3,), (-2, 2)], [slots(r3u), slots(r3d), r2]
    )
    me = lax.axis_index(HEAD).reshape(1)
    mine, *away = final_part(me, zs, where, queries, o, st, [(4,)], [slots(r4)])

    heads = range(NXL * NC)
    far_x, far_xc = [lax.ppermute(away[k - 1], HEAD, [(h, h ^ k) for h in heads]) for k in (2, 3)]
    near = lax.ppermute(away[0], HEAD, [(h, h ^ 1) for h in heads])
    partial = project([mine, near], weights[:3])
    return project([far_x, far_xc], weights[3:], partial)


def solution(mesh):
    fine = Mesh(mesh.devices.reshape(NY, NXH, NZ, NXL, NC), ("y", "xh", "z", "xl", "core"))
    in_specs = (P(SEQ, HEAD), P(SEQ, None, HEAD), P(SEQ, None), P(HEAD, None))
    out_specs = P(SEQ + HEAD, None)
    return jax.shard_map(body, mesh=fine, in_specs=in_specs, out_specs=out_specs, check_vma=False)
```

```python
from functools import reduce

import jax
import jax.numpy as jnp
from jax import lax
from jax.experimental import pallas as pl
from jax.experimental.pallas import tpu as pltpu
from jax.sharding import Mesh, PartitionSpec as P

HEAD_DIM = 128
BLOCK = 64
NEG = -1e30
SEQ = ("y", "xh", "z")
LANE = ("y", "xh")
HEAD = ("xl", "core")
XRING = ("xh", "xl")
NY, NXH, NZ, NXL, NC = 4, 2, 8, 2, 2
LANES = NY * NXH
SCALE = HEAD_DIM ** (-0.5)
F32 = jnp.float32
BF16 = jnp.bfloat16
VMEM_LIMIT = 24 * 1024 * 1024
VM = pl.BlockSpec(memory_space=pltpu.VMEM)
SM = pl.BlockSpec(memory_space=pltpu.SMEM)
HB = pl.BlockSpec(memory_space=pltpu.HBM)


def dot_nt(a, b):
    return lax.dot_general(a, b, (((1,), (1,)), ((), ())), preferred_element_type=F32)


def dot_nn(a, b):
    return jnp.dot(a, b, preferred_element_type=F32)


def row_max(a):
    return jnp.max(a, axis=1, keepdims=True)


def row_sum(a):
    return jnp.sum(a, axis=1, keepdims=True)


def local_kernel(all_blocks, deltas, z_ref, where_ref, id_ref, *refs):
    q_ref, kv_ref, ends_ref, slots_ref, o_ref, st_ref = refs
    feat = q_ref.shape[1]
    heads = range(feat // HEAD_DIM)
    blocks = q_ref.shape[0] // BLOCK
    col = lax.broadcasted_iota(jnp.int32, (BLOCK, 3 * BLOCK), 1)
    shift = jnp.where(col < BLOCK, -1, jnp.where(col < 2 * BLOCK, 0, 1))
    end_col = lax.broadcasted_iota(jnp.int32, (BLOCK, 2 * BLOCK), 1)
    kcol = [pl.ds(h * HEAD_DIM, HEAD_DIM) for h in heads]
    vcol = [pl.ds(feat + h * HEAD_DIM, HEAD_DIM) for h in heads]

    def step(j, carry):
        block = id_ref[0] + j
        near = block + shift
        near_ok = jnp.logical_and(near >= 0, near < all_blocks)
        ends_ok = jnp.where(end_col < BLOCK, block, all_blocks - 1 - block) >= 2
        rows = pl.ds(pl.multiple_of(j * BLOCK, BLOCK), BLOCK)
        wrows = pl.ds(pl.multiple_of(j * BLOCK, BLOCK), 3 * BLOCK)
        q = [q_ref[rows, kcol[h]] for h in heads]
        sw = [dot_nt(q[h], kv_ref[wrows, kcol[h]]) for h in heads]
        se = [dot_nt(q[h], ends_ref[:, kcol[h]]) for h in heads]
        sw = [jnp.where(near_ok, x * SCALE, NEG) for x in sw]
        se = [jnp.where(ends_ok, x * SCALE, NEG) for x in se]
        peak = [jnp.maximum(row_max(sw[h]), row_max(se[h])) for h in heads]
        pw = [jnp.exp(sw[h] - peak[h]) for h in heads]
        pe = [jnp.exp(se[h] - peak[h]) for h in heads]
        total = [row_sum(pw[h]) + row_sum(pe[h]) for h in heads]
        out = [
            dot_nn(pw[h].astype(BF16), kv_ref[wrows, vcol[h]])
            + dot_nn(pe[h].astype(BF16), ends_ref[:, vcol[h]])
            for h in heads
        ]
        for h in heads:
            o_ref[rows, kcol[h]] = out[h]
            st_ref[rows, pl.ds(h, 1)] = peak[h]
            st_ref[rows, pl.ds(len(heads) + h, 1)] = total[h]
        return carry

    lax.fori_loop(0, blocks, step, 0)
    add_slots(deltas, z_ref, where_ref, slots_ref, q_ref, o_ref, st_ref)


def add_slots(deltas, z_ref, where_ref, slots_ref, q_ref, o_ref, st_ref):
    feat = q_ref.shape[1]
    heads = range(feat // HEAD_DIM)
    kcol = [pl.ds(h * HEAD_DIM, HEAD_DIM) for h in heads]
    vcol = [pl.ds(feat + h * HEAD_DIM, HEAD_DIM) for h in heads]

    def step(lane, carry):
        for s, delta in enumerate(deltas):
            j = where_ref[lane * NZ + lax.rem(z_ref[0] + (delta + NZ), NZ)]

            @pl.when(j >= 0)
            def _():
                rows = pl.ds(pl.multiple_of(j * BLOCK, BLOCK), BLOCK)
                sc = [
                    dot_nt(q_ref[rows, kcol[h]], slots_ref[lane, s, :, kcol[h]]) * SCALE
                    for h in heads
                ]
                old = [st_ref[rows, pl.ds(h, 1)] for h in heads]
                tot = [st_ref[rows, pl.ds(len(heads) + h, 1)] for h in heads]
                acc = [o_ref[rows, kcol[h]] for h in heads]
                peak = [jnp.maximum(old[h], row_max(sc[h])) for h in heads]
                fade = [jnp.exp(old[h] - peak[h]) for h in heads]
                p = [jnp.exp(sc[h] - peak[h]) for h in heads]
                tot = [tot[h] * fade[h] + row_sum(p[h]) for h in heads]
                out = [dot_nn(p[h].astype(BF16), slots_ref[lane, s, :, vcol[h]]) for h in heads]
                for h in heads:
                    o_ref[rows, kcol[h]] = acc[h] * fade[h] + out[h]
                    st_ref[rows, pl.ds(h, 1)] = peak[h]
                    st_ref[rows, pl.ds(len(heads) + h, 1)] = tot[h]

        return carry

    lax.fori_loop(0, LANES, step, 0)


def more_kernel(deltas, z_ref, where_ref, q_ref, oin_ref, stin_ref, *refs):
    slots, (o_ref, st_ref) = refs[: len(deltas)], refs[len(deltas) :]
    o_ref[...] = oin_ref[...]
    st_ref[...] = stin_ref[...]
    for which, ref in zip(deltas, slots):
        add_slots(which, z_ref, where_ref, ref, q_ref, o_ref, st_ref)


def final_kernel(deltas, me_ref, z_ref, where_ref, q_ref, oin_ref, stin_ref, *refs):
    groups = NXL * NC
    slots, outs = refs[: len(deltas)], refs[len(deltas) : len(deltas) + groups]
    o_ref, st_ref = refs[-2:]
    more_kernel(deltas, z_ref, where_ref, q_ref, oin_ref, stin_ref, *slots, o_ref, st_ref)
    heads = range(q_ref.shape[1] // HEAD_DIM)
    share = q_ref.shape[0] // groups

    def step(i, carry):
        to = pl.ds(pl.multiple_of(i * BLOCK, BLOCK), BLOCK)
        for k, out_ref in enumerate(outs):
            start = (me_ref[0] ^ k) * share + i * BLOCK
            rows = pl.ds(pl.multiple_of(start, BLOCK), BLOCK)
            for h in heads:
                kcol = pl.ds(h * HEAD_DIM, HEAD_DIM)
                total = st_ref[rows, pl.ds(len(heads) + h, 1)]
                out_ref[to, kcol] = (o_ref[rows, kcol] / total).astype(BF16)
        return carry

    lax.fori_loop(0, share // BLOCK, step, 0)


def cost(us):
    return pl.CostEstimate(flops=int(us * 1e9), bytes_accessed=4 * 2**20, transcendentals=0)


def local_part(z, where, first_id, all_blocks, q, kv_pad, ends, deltas, slots):
    tok, feat = q.shape
    return pl.pallas_call(
        lambda *refs: local_kernel(all_blocks, deltas, *refs),
        out_shape=(
            jax.ShapeDtypeStruct((tok, feat), F32),
            jax.ShapeDtypeStruct((tok, 128), F32),
        ),
        in_specs=[SM, SM, SM, VM, VM, VM, VM],
        out_specs=(VM, VM),
        compiler_params=pltpu.CompilerParams(vmem_limit_bytes=VMEM_LIMIT),
        cost_estimate=cost(25),
        name="local_part",
    )(z, where, first_id, q, kv_pad, ends, slots)


def more_part(z, where, q, o, st, deltas, slots):
    tok, feat = q.shape
    return pl.pallas_call(
        lambda *refs: more_kernel(deltas, *refs),
        out_shape=(
            jax.ShapeDtypeStruct((tok, feat), F32),
            jax.ShapeDtypeStruct((tok, 128), F32),
        ),
        in_specs=[SM, SM] + [VM] * (3 + len(slots)),
        out_specs=(VM, VM),
        compiler_params=pltpu.CompilerParams(vmem_limit_bytes=VMEM_LIMIT),
        cost_estimate=cost(12),
        name="more_part",
    )(z, where, q, o, st, *slots)


def final_part(me, z, where, q, o, st, deltas, slots):
    tok, feat = q.shape
    groups = NXL * NC
    return pl.pallas_call(
        lambda *refs: final_kernel(deltas, *refs),
        out_shape=tuple(jax.ShapeDtypeStruct((tok // groups, feat), BF16) for _ in range(groups)),
        in_specs=[SM, SM, SM] + [VM] * (3 + len(slots)),
        out_specs=tuple(VM for _ in range(groups)),
        scratch_shapes=[pltpu.VMEM((tok, feat), F32), pltpu.VMEM((tok, 128), F32)],
        compiler_params=pltpu.CompilerParams(vmem_limit_bytes=VMEM_LIMIT),
        cost_estimate=cost(6),
        name="final_part",
    )(me, z, where, q, o, st, *slots)


def pick(z, asked, sources, plan, shapes, us=3):
    def kernel(z_ref, asked_ref, *refs):
        src, out = refs[: len(sources)], refs[len(sources) : -3]
        held, in_sems, out_sems = refs[-3:]
        loads, stores = [], []
        for n, (o, position, s, lane, plane, owner) in enumerate(plan):
            row = lane * NZ + lax.rem(z_ref[0] + (plane + NZ), NZ)
            block = asked_ref[row, lax.rem(z_ref[0] + (owner + NZ), NZ)]
            loads.append(pltpu.make_async_copy(src[s].at[block], held.at[n], in_sems.at[n]))
            stores.append(pltpu.make_async_copy(held.at[n], out[o].at[position], out_sems.at[n]))
            loads[-1].start()
        for load, store in zip(loads, stores):
            load.wait()
            store.start()
        for store in stores:
            store.wait()

    block_shape = sources[0].shape[1:]
    return pl.pallas_call(
        kernel,
        out_shape=tuple(pltpu.HBM(shape + block_shape, BF16) for shape in shapes),
        in_specs=[SM, SM] + [HB] * len(sources),
        out_specs=tuple(HB for _ in shapes),
        scratch_shapes=[
            pltpu.VMEM((len(plan),) + block_shape, BF16),
            pltpu.SemaphoreType.DMA((len(plan),)),
            pltpu.SemaphoreType.DMA((len(plan),)),
        ],
        compiler_params=pltpu.CompilerParams(vmem_limit_bytes=8 * 1024 * 1024),
        cost_estimate=cost(us),
        name="pick",
    )(z, asked, *sources)


def project_kernel(tile, count, base, *refs):
    parts, weights = refs[:count], refs[count : -4 - base]
    out_ref, w_ref, a_ref, sems = refs[-4:]
    feat = parts[0].shape[1]
    cols = out_ref.shape[1]
    copies = []
    for n in range(cols // tile):
        top = 0
        span = pl.ds(n * tile, tile)
        for k, weight in enumerate(weights):
            part = pl.ds(top, weight.shape[0])
            copies.append(
                pltpu.make_async_copy(
                    weight.at[:, span], w_ref.at[part, span], sems.at[n * len(weights) + k]
                )
            )
            copies[-1].start()
            top += weight.shape[0]
    for g, part in enumerate(parts):
        a_ref[:, pl.ds(g * feat, feat)] = part[...]
    for n in range(cols // tile):
        for k in range(len(weights)):
            copies[n * len(weights) + k].wait()
        span = pl.ds(n * tile, tile)
        value = dot_nn(a_ref[...], w_ref[:, span])
        if base:
            value += refs[-5][:, span]
        out_ref[:, span] = value.astype(out_ref.dtype)


def project(parts, weights, base=None, tile=1024):
    rows, feat = parts[0].shape
    cols = weights[0].shape[1]
    bases = [] if base is None else [base]
    return pl.pallas_call(
        lambda *refs: project_kernel(tile, len(parts), len(bases), *refs),
        out_shape=jax.ShapeDtypeStruct((rows, cols), F32 if base is None else BF16),
        in_specs=[VM] * len(parts) + [HB] * len(weights) + [VM] * len(bases),
        out_specs=VM,
        scratch_shapes=[
            pltpu.VMEM((len(parts) * feat, cols), BF16),
            pltpu.VMEM((rows, len(parts) * feat), BF16),
            pltpu.SemaphoreType.DMA((cols // tile * len(weights),)),
        ],
        compiler_params=pltpu.CompilerParams(vmem_limit_bytes=VMEM_LIMIT),
        cost_estimate=cost(6),
        name="project",
    )(*parts, *weights, *bases)


def z_shift(x, by):
    return lax.ppermute(x, "z", [(i, (i + by) % NZ) for i in range(NZ)])


def lane_exchange(x):
    return lax.all_to_all(x, LANE, split_axis=0, concat_axis=0, tiled=True)


def spread_lanes(edge, z):
    lane = lax.axis_index(LANE)
    steps = ([(0, 4)], [(0, 2), (4, 6)], [(0, 1), (2, 3), (4, 5), (6, 7)])
    held = edge
    for pairs in steps:
        other = [(LANES - 1 - a, LANES - 1 - b) for a, b in pairs]
        moves = [(a * NZ, b * NZ) for a, b in pairs]
        moves += [(a * NZ + NZ - 1, b * NZ + NZ - 1) for a, b in other]
        got = lax.ppermute(held, SEQ, moves)
        low = reduce(jnp.logical_or, [lane == b for _, b in pairs])
        high = reduce(jnp.logical_or, [lane == b for _, b in other])
        fresh = jnp.logical_or(
            jnp.logical_and(z == 0, low), jnp.logical_and(z == NZ - 1, high)
        )
        held = jnp.where(fresh, got, held)
    return held


def wanted_blocks(rand_blocks, block_ids, all_blocks, blocks_dev):
    taken = [
        block_ids - 1,
        block_ids,
        block_ids + 1,
        jnp.zeros_like(block_ids),
        jnp.zeros_like(block_ids) + (all_blocks - 1),
    ]
    fresh = []
    for column in range(rand_blocks.shape[1]):
        chosen = rand_blocks[:, column]
        clash = reduce(jnp.logical_or, [chosen == other for other in taken])
        fresh.append(jnp.logical_not(clash))
        taken.append(chosen)
    fresh = jnp.stack(fresh, axis=1).reshape(-1)
    flat = rand_blocks.reshape(-1)
    entries = flat.shape[0]
    query = jnp.arange(entries, dtype=jnp.int32) // rand_blocks.shape[1]
    owners = jnp.arange(all_blocks // blocks_dev, dtype=jnp.int32)
    named = (flat // blocks_dev)[:, None] == owners[None, :]
    offset = jnp.sum(jnp.where(named, (flat % blocks_dev)[:, None], 0), axis=0)
    used = jnp.logical_and(named, fresh[:, None])
    where = jnp.sum(jnp.where(used, query[:, None] + 1, 0), axis=0) - 1
    return offset.astype(jnp.int32), where.astype(jnp.int32)


def tie(*arrays):
    return lax.optimization_barrier(arrays)


def body(queries, keys_values, rand_blocks, w_out):
    tok, feat = queries.shape
    blocks_dev = tok // BLOCK
    all_blocks = blocks_dev * LANES * NZ
    lanes = range(LANES)
    half = LANES // 2
    z = lax.axis_index("z")
    zs = z.reshape(1)
    first_id = lax.axis_index(SEQ) * blocks_dev

    kv = keys_values.reshape(blocks_dev, BLOCK, 2 * feat)

    up1, down1 = z_shift(kv, 1), z_shift(kv, -1)
    block_ids = first_id + jnp.arange(blocks_dev, dtype=jnp.int32)
    offset, where = wanted_blocks(rand_blocks, block_ids, all_blocks, blocks_dev)
    asked = jnp.broadcast_to(offset.reshape(LANES, 1, NZ), (LANES, NZ, NZ)).reshape(-1, NZ)
    asked = lax.all_to_all(asked, SEQ, split_axis=0, concat_axis=0, tiled=True)
    edge = jnp.where(z == 0, kv[0], kv[blocks_dev - 1])
    held = spread_lanes(edge, z)
    w_first, held = tie(w_out, held)
    rows = w_out.shape[0] // 2
    own = [w_first[:rows], w_first[rows:]]
    ring = NXH * NXL
    low = lax.ppermute(own[0], XRING, [(i, (i + 1) % ring) for i in range(ring)])
    high = lax.ppermute(own[1], XRING, [(i, (i - 1) % ring) for i in range(ring)])
    turns = [(NZ * i + NZ - 1, NZ * i + NZ) for i in range(LANES - 1)]
    crossed = lax.ppermute(edge, SEQ, turns + [(b, a) for a, b in turns])
    up1, down1, asked, crossed = tie(up1, down1, asked, crossed)

    up2, down2 = z_shift(up1, 1), z_shift(down1, -1)
    plan = [(0, (lane, 0), 0, lane, 0, 0) for lane in lanes]
    plan += [(0, (lane, 1), 1, lane, 0, -1) for lane in lanes]
    plan += [(0, (lane, 2), 2, lane, 0, 1) for lane in lanes]
    (c1,) = pick(zs, asked, [kv, up1, down1], plan, [(LANES, 3)])
    c1, crossed, kv_late = tie(c1, crossed, kv)
    r1 = lane_exchange(c1)
    before = jnp.where(z == 0, crossed, up1[blocks_dev - 1])
    after = jnp.where(z == NZ - 1, crossed, down1[0])
    kv_pad = jnp.concatenate([before, kv_late.reshape(tok, 2 * feat), after], axis=0)
    swap = [(0, 1), (1, 0)]
    w_core = lax.ppermute(w_out, "core", swap)
    up2, down2, kv_pad, w_core, low, high = tie(up2, down2, kv_pad, w_core, low, high)

    plan = [(0, (lane, 0), 0, lane, 1, -2) for lane in lanes]
    plan += [(0, (lane, 1), 1, lane, -1, 2) for lane in lanes]
    plan += [(1, lane, 0, lane, 2, -2) for lane in lanes[:half]]
    plan += [(2, lane - half, 1, lane, -2, 2) for lane in lanes[half:]]
    plan += [(3, (lane, 0), 0, lane, 0, -2) for lane in lanes]
    plan += [(3, (lane, 1), 1, lane, 0, 2) for lane in lanes]
    c3, fu, fd, c2 = pick(
        zs, asked, [up2, down2], plan, [(LANES, 2), (half,), (half,), (LANES, 2)], 60
    )
    c3, r1 = tie(c3, r1)
    fu, fd = z_shift(fu, 1), z_shift(fd, -1)
    c3 = lane_exchange(c3)
    got = lax.ppermute(held, "z", [(0, 4), (7, 3)])
    held = jnp.where(jnp.logical_or(z == 4, z == 3), got, held)
    got = lax.ppermute(held, "z", [(0, 2), (4, 6), (7, 5), (3, 1)])
    fresh = reduce(jnp.logical_or, [z == 2, z == 6, z == 5, z == 1])
    held = jnp.where(fresh, got, held)
    got = lax.ppermute(held, "z", [(i, i ^ 1) for i in range(NZ)])
    even = z % 2 == 0
    ends = jnp.concatenate([jnp.where(even, held, got), jnp.where(even, got, held)], axis=0)
    c2, c3, fu, fd, ends = tie(c2, c3, fu, fd, ends)
    low, high, ends = tie(low, high, ends)
    others = [w_core] + [lax.ppermute(x, "core", swap) for x in (low, high)]
    r2 = lane_exchange(c2)
    fu, fd = z_shift(fu, 1), z_shift(fd, -1)
    r3u, r3d = z_shift(c3[:, 0], 1), z_shift(c3[:, 1], -1)
    far = jnp.concatenate([fu, fd], axis=0)
    far, r2, *others = tie(far, r2, *others)
    weights = own + [others[0], low, high] + others[1:]
    r4 = lane_exchange(far)

    def slots(x):
        return x.reshape(LANES, 1, BLOCK, 2 * feat)

    o, st = local_part(
        zs, where, first_id.reshape(1), all_blocks, queries, kv_pad, ends, (0, -1, 1), r1
    )
    o, st = more_part(
        zs, where, queries, o, st, [(-3,), (3,), (-2, 2)], [slots(r3u), slots(r3d), r2]
    )
    me = lax.axis_index(HEAD).reshape(1)
    mine, *away = final_part(me, zs, where, queries, o, st, [(4,)], [slots(r4)])

    heads = range(NXL * NC)
    far_x, far_xc = [lax.ppermute(away[k - 1], HEAD, [(h, h ^ k) for h in heads]) for k in (2, 3)]
    near = lax.ppermute(away[0], HEAD, [(h, h ^ 1) for h in heads])
    partial = project([mine, near], weights[:3])
    return project([far_x, far_xc], weights[3:], partial)


def solution(mesh):
    fine = Mesh(mesh.devices.reshape(NY, NXH, NZ, NXL, NC), ("y", "xh", "z", "xl", "core"))
    in_specs = (P(SEQ, HEAD), P(SEQ, None, HEAD), P(SEQ, None), P(HEAD, None))
    out_specs = P(SEQ + HEAD, None)
    return jax.shard_map(body, mesh=fine, in_specs=in_specs, out_specs=out_specs, check_vma=False)
```

```python
from functools import reduce

import jax
import jax.numpy as jnp
from jax import lax
from jax.experimental import pallas as pl
from jax.experimental.pallas import tpu as pltpu
from jax.sharding import Mesh, PartitionSpec as P

HEAD_DIM = 128
BLOCK = 64
NEG = -1e30
SEQ = ("y", "xh", "z")
LANE = ("y", "xh")
HEAD = ("xl", "core")
XRING = ("xh", "xl")
NY, NXH, NZ, NXL, NC = 4, 2, 8, 2, 2
LANES = NY * NXH
SCALE = HEAD_DIM ** (-0.5)
F32 = jnp.float32
BF16 = jnp.bfloat16
VMEM_LIMIT = 24 * 1024 * 1024
VM = pl.BlockSpec(memory_space=pltpu.VMEM)
SM = pl.BlockSpec(memory_space=pltpu.SMEM)
HB = pl.BlockSpec(memory_space=pltpu.HBM)


def dot_nt(a, b):
    return lax.dot_general(a, b, (((1,), (1,)), ((), ())), preferred_element_type=F32)


def dot_nn(a, b):
    return jnp.dot(a, b, preferred_element_type=F32)


def row_max(a):
    return jnp.max(a, axis=1, keepdims=True)


def row_sum(a):
    return jnp.sum(a, axis=1, keepdims=True)


def local_kernel(all_blocks, deltas, z_ref, where_ref, id_ref, *refs):
    q_ref, kv_ref, ends_ref, slots_ref, o_ref, st_ref = refs
    feat = q_ref.shape[1]
    heads = range(feat // HEAD_DIM)
    blocks = q_ref.shape[0] // BLOCK
    col = lax.broadcasted_iota(jnp.int32, (BLOCK, 3 * BLOCK), 1)
    shift = jnp.where(col < BLOCK, -1, jnp.where(col < 2 * BLOCK, 0, 1))
    end_col = lax.broadcasted_iota(jnp.int32, (BLOCK, 2 * BLOCK), 1)
    kcol = [pl.ds(h * HEAD_DIM, HEAD_DIM) for h in heads]
    vcol = [pl.ds(feat + h * HEAD_DIM, HEAD_DIM) for h in heads]

    def step(j, carry):
        block = id_ref[0] + j
        near = block + shift
        near_ok = jnp.logical_and(near >= 0, near < all_blocks)
        ends_ok = jnp.where(end_col < BLOCK, block, all_blocks - 1 - block) >= 2
        rows = pl.ds(pl.multiple_of(j * BLOCK, BLOCK), BLOCK)
        wrows = pl.ds(pl.multiple_of(j * BLOCK, BLOCK), 3 * BLOCK)
        q = [q_ref[rows, kcol[h]] for h in heads]
        sw = [dot_nt(q[h], kv_ref[wrows, kcol[h]]) for h in heads]
        se = [dot_nt(q[h], ends_ref[:, kcol[h]]) for h in heads]
        sw = [jnp.where(near_ok, x * SCALE, NEG) for x in sw]
        se = [jnp.where(ends_ok, x * SCALE, NEG) for x in se]
        peak = [jnp.maximum(row_max(sw[h]), row_max(se[h])) for h in heads]
        pw = [jnp.exp(sw[h] - peak[h]) for h in heads]
        pe = [jnp.exp(se[h] - peak[h]) for h in heads]
        total = [row_sum(pw[h]) + row_sum(pe[h]) for h in heads]
        out = [
            dot_nn(pw[h].astype(BF16), kv_ref[wrows, vcol[h]])
            + dot_nn(pe[h].astype(BF16), ends_ref[:, vcol[h]])
            for h in heads
        ]
        for h in heads:
            o_ref[rows, kcol[h]] = out[h]
            st_ref[rows, pl.ds(h, 1)] = peak[h]
            st_ref[rows, pl.ds(len(heads) + h, 1)] = total[h]
        return carry

    lax.fori_loop(0, blocks, step, 0)
    add_slots(deltas, z_ref, where_ref, slots_ref, q_ref, o_ref, st_ref)


def add_slots(deltas, z_ref, where_ref, slots_ref, q_ref, o_ref, st_ref):
    feat = q_ref.shape[1]
    heads = range(feat // HEAD_DIM)
    kcol = [pl.ds(h * HEAD_DIM, HEAD_DIM) for h in heads]
    vcol = [pl.ds(feat + h * HEAD_DIM, HEAD_DIM) for h in heads]

    def step(lane, carry):
        for s, delta in enumerate(deltas):
            j = where_ref[lane * NZ + lax.rem(z_ref[0] + (delta + NZ), NZ)]

            @pl.when(j >= 0)
            def _():
                rows = pl.ds(pl.multiple_of(j * BLOCK, BLOCK), BLOCK)
                sc = [
                    dot_nt(q_ref[rows, kcol[h]], slots_ref[lane, s, :, kcol[h]]) * SCALE
                    for h in heads
                ]
                old = [st_ref[rows, pl.ds(h, 1)] for h in heads]
                tot = [st_ref[rows, pl.ds(len(heads) + h, 1)] for h in heads]
                acc = [o_ref[rows, kcol[h]] for h in heads]
                peak = [jnp.maximum(old[h], row_max(sc[h])) for h in heads]
                fade = [jnp.exp(old[h] - peak[h]) for h in heads]
                p = [jnp.exp(sc[h] - peak[h]) for h in heads]
                tot = [tot[h] * fade[h] + row_sum(p[h]) for h in heads]
                out = [dot_nn(p[h].astype(BF16), slots_ref[lane, s, :, vcol[h]]) for h in heads]
                for h in heads:
                    o_ref[rows, kcol[h]] = acc[h] * fade[h] + out[h]
                    st_ref[rows, pl.ds(h, 1)] = peak[h]
                    st_ref[rows, pl.ds(len(heads) + h, 1)] = tot[h]

        return carry

    lax.fori_loop(0, LANES, step, 0)


def more_kernel(deltas, z_ref, where_ref, q_ref, oin_ref, stin_ref, *refs):
    slots, (o_ref, st_ref) = refs[: len(deltas)], refs[len(deltas) :]
    o_ref[...] = oin_ref[...]
    st_ref[...] = stin_ref[...]
    for which, ref in zip(deltas, slots):
        add_slots(which, z_ref, where_ref, ref, q_ref, o_ref, st_ref)


def final_kernel(deltas, me_ref, z_ref, where_ref, q_ref, oin_ref, stin_ref, *refs):
    groups = NXL * NC
    slots, outs = refs[: len(deltas)], refs[len(deltas) : len(deltas) + groups]
    o_ref, st_ref = refs[-2:]
    more_kernel(deltas, z_ref, where_ref, q_ref, oin_ref, stin_ref, *slots, o_ref, st_ref)
    heads = range(q_ref.shape[1] // HEAD_DIM)
    share = q_ref.shape[0] // groups

    def step(i, carry):
        to = pl.ds(pl.multiple_of(i * BLOCK, BLOCK), BLOCK)
        for k, out_ref in enumerate(outs):
            start = (me_ref[0] ^ k) * share + i * BLOCK
            rows = pl.ds(pl.multiple_of(start, BLOCK), BLOCK)
            for h in heads:
                kcol = pl.ds(h * HEAD_DIM, HEAD_DIM)
                total = st_ref[rows, pl.ds(len(heads) + h, 1)]
                out_ref[to, kcol] = (o_ref[rows, kcol] / total).astype(BF16)
        return carry

    lax.fori_loop(0, share // BLOCK, step, 0)


def cost(us):
    return pl.CostEstimate(flops=int(us * 1e9), bytes_accessed=4 * 2**20, transcendentals=0)


def local_part(z, where, first_id, all_blocks, q, kv_pad, ends, deltas, slots):
    tok, feat = q.shape
    return pl.pallas_call(
        lambda *refs: local_kernel(all_blocks, deltas, *refs),
        out_shape=(
            jax.ShapeDtypeStruct((tok, feat), F32),
            jax.ShapeDtypeStruct((tok, 128), F32),
        ),
        in_specs=[SM, SM, SM, VM, VM, VM, VM],
        out_specs=(VM, VM),
        compiler_params=pltpu.CompilerParams(vmem_limit_bytes=VMEM_LIMIT),
        cost_estimate=cost(25),
        name="local_part",
    )(z, where, first_id, q, kv_pad, ends, slots)


def more_part(z, where, q, o, st, deltas, slots):
    tok, feat = q.shape
    return pl.pallas_call(
        lambda *refs: more_kernel(deltas, *refs),
        out_shape=(
            jax.ShapeDtypeStruct((tok, feat), F32),
            jax.ShapeDtypeStruct((tok, 128), F32),
        ),
        in_specs=[SM, SM] + [VM] * (3 + len(slots)),
        out_specs=(VM, VM),
        compiler_params=pltpu.CompilerParams(vmem_limit_bytes=VMEM_LIMIT),
        cost_estimate=cost(12),
        name="more_part",
    )(z, where, q, o, st, *slots)


def final_part(me, z, where, q, o, st, deltas, slots):
    tok, feat = q.shape
    groups = NXL * NC
    return pl.pallas_call(
        lambda *refs: final_kernel(deltas, *refs),
        out_shape=tuple(jax.ShapeDtypeStruct((tok // groups, feat), BF16) for _ in range(groups)),
        in_specs=[SM, SM, SM] + [VM] * (3 + len(slots)),
        out_specs=tuple(VM for _ in range(groups)),
        scratch_shapes=[pltpu.VMEM((tok, feat), F32), pltpu.VMEM((tok, 128), F32)],
        compiler_params=pltpu.CompilerParams(vmem_limit_bytes=VMEM_LIMIT),
        cost_estimate=cost(6),
        name="final_part",
    )(me, z, where, q, o, st, *slots)


def pick(z, asked, sources, plan, shapes, us=3):
    def kernel(z_ref, asked_ref, *refs):
        src, out = refs[: len(sources)], refs[len(sources) : -3]
        held, in_sems, out_sems = refs[-3:]
        loads, stores = [], []
        for n, (o, position, s, lane, plane, owner) in enumerate(plan):
            row = lane * NZ + lax.rem(z_ref[0] + (plane + NZ), NZ)
            block = asked_ref[row, lax.rem(z_ref[0] + (owner + NZ), NZ)]
            loads.append(pltpu.make_async_copy(src[s].at[block], held.at[n], in_sems.at[n]))
            stores.append(pltpu.make_async_copy(held.at[n], out[o].at[position], out_sems.at[n]))
            loads[-1].start()
        for load, store in zip(loads, stores):
            load.wait()
            store.start()
        for store in stores:
            store.wait()

    block_shape = sources[0].shape[1:]
    return pl.pallas_call(
        kernel,
        out_shape=tuple(pltpu.HBM(shape + block_shape, BF16) for shape in shapes),
        in_specs=[SM, SM] + [HB] * len(sources),
        out_specs=tuple(HB for _ in shapes),
        scratch_shapes=[
            pltpu.VMEM((len(plan),) + block_shape, BF16),
            pltpu.SemaphoreType.DMA((len(plan),)),
            pltpu.SemaphoreType.DMA((len(plan),)),
        ],
        compiler_params=pltpu.CompilerParams(vmem_limit_bytes=8 * 1024 * 1024),
        cost_estimate=cost(us),
        name="pick",
    )(z, asked, *sources)


def project_kernel(tile, count, base, *refs):
    parts, weights = refs[:count], refs[count : -4 - base]
    out_ref, w_ref, a_ref, sems = refs[-4:]
    feat = parts[0].shape[1]
    cols = out_ref.shape[1]
    copies = []
    for n in range(cols // tile):
        top = 0
        span = pl.ds(n * tile, tile)
        for k, weight in enumerate(weights):
            part = pl.ds(top, weight.shape[0])
            copies.append(
                pltpu.make_async_copy(
                    weight.at[:, span], w_ref.at[part, span], sems.at[n * len(weights) + k]
                )
            )
            copies[-1].start()
            top += weight.shape[0]
    for g, part in enumerate(parts):
        a_ref[:, pl.ds(g * feat, feat)] = part[...]
    for n in range(cols // tile):
        for k in range(len(weights)):
            copies[n * len(weights) + k].wait()
        span = pl.ds(n * tile, tile)
        value = dot_nn(a_ref[...], w_ref[:, span])
        if base:
            value += refs[-5][:, span]
        out_ref[:, span] = value.astype(out_ref.dtype)


def project(parts, weights, base=None, tile=1024):
    rows, feat = parts[0].shape
    cols = weights[0].shape[1]
    bases = [] if base is None else [base]
    return pl.pallas_call(
        lambda *refs: project_kernel(tile, len(parts), len(bases), *refs),
        out_shape=jax.ShapeDtypeStruct((rows, cols), F32 if base is None else BF16),
        in_specs=[VM] * len(parts) + [HB] * len(weights) + [VM] * len(bases),
        out_specs=VM,
        scratch_shapes=[
            pltpu.VMEM((len(parts) * feat, cols), BF16),
            pltpu.VMEM((rows, len(parts) * feat), BF16),
            pltpu.SemaphoreType.DMA((cols // tile * len(weights),)),
        ],
        compiler_params=pltpu.CompilerParams(vmem_limit_bytes=VMEM_LIMIT),
        cost_estimate=cost(6),
        name="project",
    )(*parts, *weights, *bases)


def z_shift(x, by):
    return lax.ppermute(x, "z", [(i, (i + by) % NZ) for i in range(NZ)])


def lane_exchange(x):
    return lax.all_to_all(x, LANE, split_axis=0, concat_axis=0, tiled=True)


def spread_lanes(edge, z):
    lane = lax.axis_index(LANE)
    steps = ([(0, 4)], [(0, 2), (4, 6)], [(0, 1), (2, 3), (4, 5), (6, 7)])
    held = edge
    for pairs in steps:
        other = [(LANES - 1 - a, LANES - 1 - b) for a, b in pairs]
        moves = [(a * NZ, b * NZ) for a, b in pairs]
        moves += [(a * NZ + NZ - 1, b * NZ + NZ - 1) for a, b in other]
        got = lax.ppermute(held, SEQ, moves)
        low = reduce(jnp.logical_or, [lane == b for _, b in pairs])
        high = reduce(jnp.logical_or, [lane == b for _, b in other])
        fresh = jnp.logical_or(
            jnp.logical_and(z == 0, low), jnp.logical_and(z == NZ - 1, high)
        )
        held = jnp.where(fresh, got, held)
    return held


def wanted_blocks(rand_blocks, block_ids, all_blocks, blocks_dev):
    taken = [
        block_ids - 1,
        block_ids,
        block_ids + 1,
        jnp.zeros_like(block_ids),
        jnp.zeros_like(block_ids) + (all_blocks - 1),
    ]
    fresh = []
    for column in range(rand_blocks.shape[1]):
        chosen = rand_blocks[:, column]
        clash = reduce(jnp.logical_or, [chosen == other for other in taken])
        fresh.append(jnp.logical_not(clash))
        taken.append(chosen)
    fresh = jnp.stack(fresh, axis=1).reshape(-1)
    flat = rand_blocks.reshape(-1)
    entries = flat.shape[0]
    query = jnp.arange(entries, dtype=jnp.int32) // rand_blocks.shape[1]
    owners = jnp.arange(all_blocks // blocks_dev, dtype=jnp.int32)
    named = (flat // blocks_dev)[:, None] == owners[None, :]
    offset = jnp.sum(jnp.where(named, (flat % blocks_dev)[:, None], 0), axis=0)
    used = jnp.logical_and(named, fresh[:, None])
    where = jnp.sum(jnp.where(used, query[:, None] + 1, 0), axis=0) - 1
    return offset.astype(jnp.int32), where.astype(jnp.int32)


def tie(*arrays):
    return lax.optimization_barrier(arrays)


def body(queries, keys_values, rand_blocks, w_out):
    tok, feat = queries.shape
    blocks_dev = tok // BLOCK
    all_blocks = blocks_dev * LANES * NZ
    lanes = range(LANES)
    half = LANES // 2
    z = lax.axis_index("z")
    zs = z.reshape(1)
    first_id = lax.axis_index(SEQ) * blocks_dev

    kv = keys_values.reshape(blocks_dev, BLOCK, 2 * feat)

    up1, down1 = z_shift(kv, 1), z_shift(kv, -1)
    block_ids = first_id + jnp.arange(blocks_dev, dtype=jnp.int32)
    offset, where = wanted_blocks(rand_blocks, block_ids, all_blocks, blocks_dev)
    asked = jnp.broadcast_to(offset.reshape(LANES, 1, NZ), (LANES, NZ, NZ)).reshape(-1, NZ)
    asked = lax.all_to_all(asked, SEQ, split_axis=0, concat_axis=0, tiled=True)
    edge = jnp.where(z == 0, kv[0], kv[blocks_dev - 1])
    held = spread_lanes(edge, z)
    w_first, held = tie(w_out, held)
    rows = w_out.shape[0] // 2
    own = [w_first[:rows], w_first[rows:]]
    ring = NXH * NXL
    low = lax.ppermute(own[0], XRING, [(i, (i + 1) % ring) for i in range(ring)])
    high = lax.ppermute(own[1], XRING, [(i, (i - 1) % ring) for i in range(ring)])
    turns = [(NZ * i + NZ - 1, NZ * i + NZ) for i in range(LANES - 1)]
    crossed = lax.ppermute(edge, SEQ, turns + [(b, a) for a, b in turns])
    up1, down1, asked, crossed = tie(up1, down1, asked, crossed)

    up2, down2 = z_shift(up1, 1), z_shift(down1, -1)
    plan = [(0, (lane, 0), 0, lane, 0, 0) for lane in lanes]
    plan += [(0, (lane, 1), 1, lane, 0, -1) for lane in lanes]
    plan += [(0, (lane, 2), 2, lane, 0, 1) for lane in lanes]
    (c1,) = pick(zs, asked, [kv, up1, down1], plan, [(LANES, 3)])
    c1, crossed, kv_late = tie(c1, crossed, kv)
    r1 = lane_exchange(c1)
    before = jnp.where(z == 0, crossed, up1[blocks_dev - 1])
    after = jnp.where(z == NZ - 1, crossed, down1[0])
    kv_pad = jnp.concatenate([before, kv_late.reshape(tok, 2 * feat), after], axis=0)
    up2, down2, kv_pad, w_core, low, high = tie(up2, down2, kv_pad, w_out, low, high)

    plan = [(0, (lane, 0), 0, lane, 1, -2) for lane in lanes]
    plan += [(0, (lane, 1), 1, lane, -1, 2) for lane in lanes]
    plan += [(1, lane, 0, lane, 2, -2) for lane in lanes[:half]]
    plan += [(2, lane - half, 1, lane, -2, 2) for lane in lanes[half:]]
    plan += [(3, (lane, 0), 0, lane, 0, -2) for lane in lanes]
    plan += [(3, (lane, 1), 1, lane, 0, 2) for lane in lanes]
    c3, fu, fd, c2 = pick(
        zs, asked, [up2, down2], plan, [(LANES, 2), (half,), (half,), (LANES, 2)], 60
    )
    c3, r1 = tie(c3, r1)
    fu, fd = z_shift(fu, 1), z_shift(fd, -1)
    c3 = lane_exchange(c3)
    got = lax.ppermute(held, "z", [(0, 4), (7, 3)])
    held = jnp.where(jnp.logical_or(z == 4, z == 3), got, held)
    got = lax.ppermute(held, "z", [(0, 2), (4, 6), (7, 5), (3, 1)])
    fresh = reduce(jnp.logical_or, [z == 2, z == 6, z == 5, z == 1])
    held = jnp.where(fresh, got, held)
    got = lax.ppermute(held, "z", [(i, i ^ 1) for i in range(NZ)])
    even = z % 2 == 0
    ends = jnp.concatenate([jnp.where(even, held, got), jnp.where(even, got, held)], axis=0)
    c2, c3, fu, fd, ends = tie(c2, c3, fu, fd, ends)
    r2 = lane_exchange(c2)
    fu, fd = z_shift(fu, 1), z_shift(fd, -1)
    r3u, r3d = z_shift(c3[:, 0], 1), z_shift(c3[:, 1], -1)
    far = jnp.concatenate([fu, fd], axis=0)
    far, r2 = tie(far, r2)
    r4 = lane_exchange(far)

    def slots(x):
        return x.reshape(LANES, 1, BLOCK, 2 * feat)

    o, st = local_part(
        zs, where, first_id.reshape(1), all_blocks, queries, kv_pad, ends, (0, -1, 1), r1
    )
    low, high, w_core, st = tie(low, high, w_core, st)
    swap = [(0, 1), (1, 0)]
    others = [lax.ppermute(x, "core", swap) for x in (w_core, low, high)]
    weights = own + [others[0], low, high] + others[1:]
    o, st = more_part(
        zs, where, queries, o, st, [(-3,), (3,), (-2, 2)], [slots(r3u), slots(r3d), r2]
    )
    me = lax.axis_index(HEAD).reshape(1)
    mine, *away = final_part(me, zs, where, queries, o, st, [(4,)], [slots(r4)])

    heads = range(NXL * NC)
    far_x, far_xc = [lax.ppermute(away[k - 1], HEAD, [(h, h ^ k) for h in heads]) for k in (2, 3)]
    near = lax.ppermute(away[0], HEAD, [(h, h ^ 1) for h in heads])
    partial = project([mine, near], weights[:3])
    return project([far_x, far_xc], weights[3:], partial)


def solution(mesh):
    fine = Mesh(mesh.devices.reshape(NY, NXH, NZ, NXL, NC), ("y", "xh", "z", "xl", "core"))
    in_specs = (P(SEQ, HEAD), P(SEQ, None, HEAD), P(SEQ, None), P(HEAD, None))
    out_specs = P(SEQ + HEAD, None)
    return jax.shard_map(body, mesh=fine, in_specs=in_specs, out_specs=out_specs, check_vma=False)
```
